32 devices in a mesh: batch: 16 (over z, y, x), tensor: 2 (over core).
Axes of the slice: x: 2, y: 2, z: 4, core: 2. Of those that a mesh axis runs over, the one named last changes fastest.
Arguments:
- images: bfloat16 [128, 256, 256], P('batch', 'tensor'), may hold values from -6 to 6
- timesteps: int32 [128], P('batch'), may hold values from 0 to 1023
- embed_table: bfloat16 [1024, 512], replicated, may hold values from -6 to 6
- first_gain: float32 [256], P('tensor'), may hold values from 0.5 to 1.5
- first_shift: float32 [256], P('tensor'), may hold values from -3 to 3
- first_conv: bfloat16 [9, 256, 256], P(None, None, 'tensor'), may hold values from -0.125 to 0.125
- first_bias: float32 [256], P('tensor'), may hold values from -3 to 3
- time_weight: bfloat16 [512, 256], P(None, 'tensor'), may hold values from -0.25 to 0.25
- time_bias: float32 [256], P('tensor'), may hold values from -3 to 3
- second_gain: float32 [256], P('tensor'), may hold values from 0.5 to 1.5
- second_shift: float32 [256], P('tensor'), may hold values from -3 to 3
- second_conv: bfloat16 [9, 256, 256], P(None, 'tensor'), may hold values from -0.125 to 0.125
- second_bias: float32 [256], P('tensor'), may hold values from -3 to 3
- third_gain: float32 [256], P('tensor'), may hold values from 0.5 to 1.5
- third_shift: float32 [256], P('tensor'), may hold values from -3 to 3
- project_in: bfloat16 [3, 256, 256], P(None, None, 'tensor'), may hold values from -0.5 to 0.5
- query_bias: float32 [256], P('tensor'), may hold values from -3 to 3
- value_bias: float32 [256], P('tensor'), may hold values from -3 to 3
- project_out: bfloat16 [256, 256], P('tensor'), may hold values from -1.5 to 1.5
- output_bias: float32 [256], P('tensor'), may hold values from -3 to 3
- cotangent: bfloat16 [128, 256, 256], P('batch', 'tensor'), may hold values from -6 to 6
Outputs:
- block_out: float32 [128, 256, 256], P('batch', 'tensor')
- images_grad: float32 [128, 256, 256], P('batch', 'tensor')
- table_grad: float32 [1024, 512], replicated
- first_gain_grad: float32 [256], P('tensor')
- first_shift_grad: float32 [256], P('tensor')
- first_conv_grad: float32 [9, 256, 256], P(None, None, 'tensor')
- first_bias_grad: float32 [256], P('tensor')
- time_weight_grad: float32 [512, 256], P(None, 'tensor')
- time_bias_grad: float32 [256], P('tensor')
- second_gain_grad: float32 [256], P('tensor')
- second_shift_grad: float32 [256], P('tensor')
- second_conv_grad: float32 [9, 256, 256], P(None, 'tensor')
- second_bias_grad: float32 [256], P('tensor')
- third_gain_grad: float32 [256], P('tensor')
- third_shift_grad: float32 [256], P('tensor')
- project_in_grad: float32 [3, 256, 256], P(None, None, 'tensor')
- query_bias_grad: float32 [256], P('tensor')
- value_bias_grad: float32 [256], P('tensor')
- project_out_grad: float32 [256, 256], P('tensor')
- output_bias_grad: float32 [256], P('tensor')
The draws below stay inside these ranges and needn't reach their ends.
All inputs are finite; a program needn't handle non-finite values.
Results may differ from the reference program's by a relative error of at most 0.017.
Values may be sent and summed in bfloat16 or wider, within the bound.
No kernel may reach another device: no remote copies, remote signals or barrier semaphores. Data moves between devices by JAX's collectives and lax.ppermute only.
A program may use at most 128 MiB of HBM per device.

```python
import math
import jax
import jax.numpy as jnp
from jax import lax

C = 256
GROUPS = 32
E = 512
STEPS = 1024
P_SIZE = 256
IMAGES = 128


def with_ends(array, key, least, high):
    dims = array.shape
    index_at = [jax.random.randint(jax.random.fold_in(key, axis), (), 0, dims[axis]) for axis in range(len(dims))]
    array = array.at[tuple(index_at)].set(least)
    longest = dims.index(max(dims))
    index_at[longest] = (index_at[longest] + 1) % dims[longest]
    return array.at[tuple(index_at)].set(high)


def shard_levels(own_key, extent, cuts, least, largest):
    def one(axis_at, parts):
        heights = jax.random.uniform(jax.random.fold_in(jax.random.fold_in(own_key, 6), axis_at), (parts,), jnp.float32, least / len(cuts), largest / len(cuts))
        return jnp.repeat(jnp.exp(heights), extent[axis_at] // parts).reshape((-1,) + (1,) * (len(extent) - axis_at - 1))

    level = one(*cuts[0])
    for cut in cuts[1:]:
        level = level * one(*cut)
    return level


def noise(rng, dims, width, reach, shards=(), dtype=jnp.bfloat16):
    array = jax.random.normal(rng, dims, jnp.float32) * width
    if len(shards) > 0:
        array = shard_levels(rng, dims, shards, -0.22, 0.18) * array
    return jnp.clip(array, min=-reach, max=reach).astype(dtype)


def setup_inputs(seed: int = 0) -> dict:
    key_of = jax.random.split(jax.random.key(seed), 22)
    return {
        "images": noise(key_of[0], (IMAGES, C, P_SIZE), 1.0, 6.0, ((0, 16), (1, 2))),
        "timesteps": with_ends(jax.random.randint(key_of[1], (IMAGES,), 0, STEPS), jax.random.fold_in(key_of[1], 1), 0, STEPS - 1).astype(jnp.int32),
        "embed_table": noise(key_of[2], (STEPS, E), 1.0, 6.0),
        "first_gain": jnp.clip(1.0 + 0.1 * jax.random.normal(key_of[3], (C,), jnp.float32), 0.5, 1.5),
        "first_shift": noise(key_of[4], (C,), 0.5, 3.0, ((0, 2),), jnp.float32),
        "first_conv": noise(key_of[5], (9, C, C), (9 * C) ** -0.5, 0.125, ((2, 2),)),
        "first_bias": noise(key_of[6], (C,), 0.5, 3.0, ((0, 2),), jnp.float32),
        "time_weight": noise(key_of[7], (E, C), E ** -0.5, 0.25, ((1, 2),)),
        "time_bias": noise(key_of[8], (C,), 0.5, 3.0, ((0, 2),), jnp.float32),
        "second_gain": jnp.clip(1.0 + 0.1 * jax.random.normal(key_of[9], (C,), jnp.float32), 0.5, 1.5),
        "second_shift": noise(key_of[10], (C,), 0.5, 3.0, ((0, 2),), jnp.float32),
        "second_conv": noise(key_of[11], (9, C, C), (9 * C) ** -0.5, 0.125, ((1, 2),)),
        "second_bias": noise(key_of[12], (C,), 0.5, 3.0, ((0, 2),), jnp.float32),
        "third_gain": jnp.clip(1.0 + 0.1 * jax.random.normal(key_of[13], (C,), jnp.float32), 0.5, 1.5),
        "third_shift": noise(key_of[14], (C,), 0.5, 3.0, ((0, 2),), jnp.float32),
        "project_in": noise(key_of[15], (3, C, C), (C // 2) ** -0.5, 0.5, ((2, 2),)),
        "query_bias": noise(key_of[16], (C,), 0.5, 3.0, ((0, 2),), jnp.float32),
        "value_bias": noise(key_of[17], (C,), 0.5, 3.0, ((0, 2),), jnp.float32),
        "project_out": noise(key_of[18], (C, C), (C // 16) ** -0.5, 1.5, ((0, 2),)),
        "output_bias": noise(key_of[19], (C,), 0.5, 3.0, ((0, 2),), jnp.float32),
        "cotangent": noise(key_of[20], (IMAGES, C, P_SIZE), 1.0, 6.0, ((0, 16), (1, 2))),
    }


@jax.custom_vjp
def low(v):
    return lax.optimization_barrier(v.astype(jnp.bfloat16)).astype(jnp.float32)

@jax.custom_vjp
def low_back(v):
    return v

def low_keep(v):
    return (low(v), None)

def low_pass(kept, grad):
    return (grad,)

def back_keep(v):
    return (v, None)

def back_low(kept, grad):
    return (low(grad),)
low.defvjp(low_keep, low_pass)
low_back.defvjp(back_keep, back_low)
norm_eps = 1e-06

def shifted_taps(values, sign):
    side = math.isqrt(values.shape[-1])
    lead = values.shape[:-1]
    grid = values.reshape(lead + (side, side))
    padded = jnp.pad(grid, [(0, 0)] * len(lead) + [(1, 1), (1, 1)])
    pieces = []
    for row_off in (-1, 0, 1):
        for col_off in (-1, 0, 1):
            top = 1 + sign * row_off
            left = 1 + sign * col_off
            pieces.append(padded[..., top:top + side, left:left + side].reshape(values.shape))
    return jnp.stack(pieces, 0)

def convolve(values, weight):
    return jnp.einsum('kio,kbip->bop', weight, shifted_taps(values, 1), precision=lax.Precision.HIGHEST)

def group_norm(values, gain, shift):
    count, chans, points = values.shape
    grouped = values.reshape(count, GROUPS, chans // GROUPS, points)
    center = lax.optimization_barrier(jnp.mean(grouped, axis=(2, 3), keepdims=True))
    spread = lax.optimization_barrier(jnp.mean(jnp.square(grouped - center), axis=(2, 3), keepdims=True))
    normal = ((grouped - center) * lax.rsqrt(spread + norm_eps)).reshape(values.shape)
    return normal * gain[None, :, None] + shift[None, :, None]

def layer(steps_index, images, embed_table, first_gain, first_shift, first_conv, first_bias, time_weight, time_bias, second_gain, second_shift, second_conv, second_bias, third_gain, third_shift, project_in, query_bias, value_bias, project_out, output_bias):
    highest = lax.Precision.HIGHEST
    embed_act = low(jax.nn.silu(embed_table[steps_index]))
    time_add = jnp.dot(embed_act, time_weight, precision=highest) + time_bias
    act_one = low(jax.nn.silu(group_norm(images, first_gain, first_shift)))
    conv_one = low_back(convolve(act_one, first_conv))
    sum_one = conv_one + first_bias[None, :, None] + time_add[:, :, None]
    act_two = low(jax.nn.silu(group_norm(sum_one, second_gain, second_shift)))
    conv_two = low_back(convolve(act_two, second_conv))
    resid = images + conv_two + second_bias[None, :, None]
    normed = low(group_norm(resid, third_gain, third_shift))
    linear = jnp.einsum('jio,bip->jbop', project_in, normed, precision=highest)
    query = low(low_back(linear[0] + query_bias[None, :, None]))
    keys = low(low_back(linear[1]))
    values = low(low_back(linear[2] + value_bias[None, :, None]))
    scale = C ** (-0.5)
    scores = low_back(jnp.einsum('bcp,bcq->bpq', query, keys, precision=highest) * scale)
    weights = low(jax.nn.softmax(scores, axis=-1))
    mixed = low(low_back(jnp.einsum('bcq,bpq->bcp', values, weights, precision=highest)))
    projected = low_back(jnp.einsum('io,bip->bop', project_out, mixed, precision=highest))
    return resid + projected + output_bias[None, :, None]

def reference(images, timesteps, embed_table, first_gain, first_shift, first_conv, first_bias, time_weight, time_bias, second_gain, second_shift, second_conv, second_bias, third_gain, third_shift, project_in, query_bias, value_bias, project_out, output_bias, cotangent):
    floats = (images, embed_table, first_gain, first_shift, first_conv, first_bias, time_weight, time_bias, second_gain, second_shift, second_conv, second_bias, third_gain, third_shift, project_in, query_bias, value_bias, project_out, output_bias)
    floats = tuple((item.astype(jnp.float32) for item in floats))
    block_out, pullback = jax.vjp(partial_layer(timesteps), *floats)
    grads = pullback(cotangent.astype(jnp.float32))
    return (block_out, grads[0], grads[1], grads[2], grads[3], grads[4], grads[5], grads[6], grads[7], grads[8], grads[9], grads[10], grads[11], grads[12], grads[13], grads[14], grads[15], grads[16], grads[17], grads[18])

def partial_layer(timesteps):

    def bound_layer(*floats):
        return layer(timesteps, *floats)
    return bound_layer
```

```python
import functools
import math

import jax
import jax.numpy as jnp
from jax import lax
from jax.experimental import pallas as pl
from jax.experimental.pallas import tpu as pltpu
from jax.sharding import PartitionSpec as P

GROUPS = 32
EPS = 1e-06
VMEM_LIMIT = 56 * 1024 * 1024
ANY = pl.BlockSpec(memory_space=pl.ANY)
VMEM = pl.BlockSpec(memory_space=pltpu.VMEM)
SMEM = pl.BlockSpec(memory_space=pltpu.SMEM)
f32 = jnp.float32
bf16 = jnp.bfloat16

(
    FIRST_GAIN,
    FIRST_SHIFT,
    FIRST_BIAS,
    TIME_BIAS,
    SECOND_GAIN,
    SECOND_SHIFT,
    SECOND_BIAS,
    THIRD_GAIN,
    THIRD_SHIFT,
    QUERY_BIAS,
    VALUE_BIAS,
    OUTPUT_BIAS,
) = range(12)


def nn(a, b):
    return lax.dot_general(a, b, (((1,), (0,)), ((), ())), preferred_element_type=f32)


def nt(a, b):
    return lax.dot_general(a, b, (((1,), (1,)), ((), ())), preferred_element_type=f32)


def sigmoid(v):
    return 0.5 * jnp.tanh(0.5 * v) + 0.5


def silu_slope(v, sig):
    return sig * (1.0 + v * (1.0 - sig))


def col_sum(v):
    return jnp.sum(v, axis=0, keepdims=True)


def lane_groups(v, width):
    lanes = v.shape[1]
    lane = lax.broadcasted_iota(jnp.int32, v.shape, 1)
    step = 1
    while step < width:
        up = pltpu.roll(v, step, 1)
        down = pltpu.roll(v, lanes - step, 1)
        v = v + jnp.where((lane & step) != 0, up, down)
        step *= 2
    return v


def fill_shift(shift_ref, side):
    points = shift_ref.shape[1]
    to = lax.broadcasted_iota(jnp.int32, (points, points), 0)
    of = lax.broadcasted_iota(jnp.int32, (points, points), 1)
    for d in range(3):
        s = d - 1
        col = (to & (side - 1)) + s
        hit = (of == to + s) & (col >= 0) & (col < side)
        shift_ref[d * points : (d + 1) * points, :] = jnp.where(hit, 1.0, 0.0).astype(bf16)


def zero_pads(pad_ref, side, points):
    images, chans = pad_ref.shape[1], pad_ref.shape[3]
    for d in range(3):
        for b in range(images):
            pad_ref[d, b, 0:side, :] = jnp.zeros((side, chans), bf16)
            pad_ref[d, b, side + points : 2 * side + points, :] = jnp.zeros((side, chans), bf16)


def put_pads(pad_ref, b, moved, side, points):
    for d in range(3):
        pad_ref[d, b, side : side + points, :] = moved[d * points : (d + 1) * points]


def taps(pad_ref, b, sign, side, points):
    out = []
    for dr in (-1, 0, 1):
        for dc in (-1, 0, 1):
            top = side + sign * dr * side
            out.append(pad_ref[1 + sign * dc, b, top : top + points, :])
    return out


class Copies:
    def __init__(self, sems):
        self.sems = sems
        self.used = 0

    def start(self, src, dst):
        copy = pltpu.make_async_copy(src, dst, self.sems.at[self.used])
        self.used += 1
        copy.start()
        return copy


def wait_all(copies):
    for c in copies:
        c.wait()


def side_of(points):
    return math.isqrt(points)


def load_split(cps, refs, dst, axis, places):
    out = []
    for ref, place in zip(refs, places, strict=True):
        size = ref.shape[axis]
        idx = [slice(None)] * len(ref.shape)
        idx[axis] = pl.ds(pl.multiple_of(place * size, size), size)
        out.append(cps.start(ref, dst.at[tuple(idx)]))
    return out


def load_images(cps, refs, dst, places, count):
    out = []
    for j, (ref, place) in enumerate(zip(refs, places, strict=True)):
        size = ref.shape[1]
        first = pl.multiple_of(places[0] * count, count) if j == 0 else 0
        out.append(
            cps.start(
                ref.at[pl.ds(first, count)],
                dst.at[:, pl.ds(pl.multiple_of(place * size, size), size), :],
            )
        )
    return out


def places_of(pieces):
    if pieces == 1:
        return [0]
    me = lax.axis_index("tensor")
    return [me, 1 - me]


def split_store(own_ref, send_ref, at, value, axis, places):
    if send_ref is None:
        own_ref[at] = value.astype(own_ref.dtype)
        return
    half = value.shape[axis] // 2
    low = lax.slice_in_dim(value, 0, half, axis=axis)
    high = lax.slice_in_dim(value, half, 2 * half, axis=axis)
    first = places[0] == 0
    own_ref[at] = jnp.where(first, low, high).astype(own_ref.dtype)
    send_ref[at] = jnp.where(first, high, low).astype(send_ref.dtype)


def front_kernel(pieces, count, *refs):
    it = iter(refs)

    def take(n):
        return [next(it) for _ in range(n)]

    x_in, g_in, w1_in, w2_in, pi_in, po_in, tw_in, vec_in = (take(pieces) for _ in range(8))
    steps_ref, table_ref = take(2)
    dw2_own, dpo_own, dpi_own = take(3)
    dw2_send, dpo_send, dpi_send = take(3) if pieces == 2 else (None, None, None)
    vec_out, stat_out = take(2)
    gpad_out, sum_out, a1t_out, resid_out, gres_out, mix_out = take(6)
    xin, gin, w1, w2, pi, po, tw, vec, rows = take(9)
    shift, apad, gpad, sum_one, a1t, resid, gres, mix = take(8)
    a2t, nmt, gl = take(3)
    sems = next(it)

    cps = Copies(sems)
    places = places_of(pieces)
    chans, points = xin.shape[1], xin.shape[2]
    side = side_of(points)
    width = chans // GROUPS
    size = float(width * points)
    scale = chans ** (-0.5)

    x_cp = load_images(cps, x_in, xin, places, count)
    vec_cp = load_split(cps, vec_in, vec, 1, places)
    row_cp = []
    for b in range(count):
        step = steps_ref[places[0] * count + b]
        row_cp.append(
            cps.start(table_ref.at[pl.ds(pl.multiple_of(step // 16 * 16, 16), 16), :], rows.at[b])
        )
    tw_cp = load_split(cps, tw_in, tw, 1, places)
    w1_cp = load_split(cps, w1_in, w1, 2, places)
    w2_cp = load_split(cps, w2_in, w2, 1, places)
    pi_cp = load_split(cps, pi_in, pi, 2, places)
    po_cp = load_split(cps, po_in, po, 0, places)
    g_cp = load_images(cps, g_in, gin, places, count)

    fill_shift(shift, side)
    zero_pads(apad, side, points)
    zero_pads(gpad, side, points)
    eye = shift[points : 2 * points, :]

    wait_all(vec_cp)
    vcols = jnp.transpose(vec[...])

    def col(j):
        return vcols[:, j : j + 1]

    def row(j):
        return vec[j : j + 1, :]

    wait_all(x_cp)
    for b in range(count):
        x3 = xin[b].astype(f32).reshape(GROUPS, width, points)
        mean = jnp.sum(jnp.sum(x3, axis=2, keepdims=True), axis=1, keepdims=True) / size
        off = x3 - mean
        var = jnp.sum(jnp.sum(off * off, axis=2, keepdims=True), axis=1, keepdims=True) / size
        hat = (off * lax.rsqrt(var + EPS)).reshape(chans, points)
        pre = hat * col(FIRST_GAIN) + col(FIRST_SHIFT)
        act = (pre * sigmoid(pre)).astype(bf16)
        a1t[b] = act
        put_pads(apad, b, nt(shift[...], act).astype(bf16), side, points)
    outs = [cps.start(a1t, a1t_out)]

    wait_all(row_cp)
    wait_all(tw_cp)
    picked = []
    for b in range(count):
        step = steps_ref[places[0] * count + b]
        r = lax.broadcasted_iota(jnp.int32, (16, rows.shape[2]), 0)
        picked.append(
            col_sum(jnp.where(r == lax.rem(step, 16), rows[b].astype(f32), 0.0))
        )
    emb = jnp.concatenate(picked + picked[:1] * (8 - count), axis=0)
    time_add = nn((emb * sigmoid(emb)).astype(bf16), tw[...]) + row(TIME_BIAS)

    wait_all(w1_cp)
    w1_rows = w1[...].reshape(9 * chans, chans)
    sums = []
    for b in range(count):
        lhs = jnp.concatenate(taps(apad, b, 1, side, points), axis=1)
        val = nn(lhs, w1_rows) + (row(FIRST_BIAS) + time_add[b : b + 1])
        sum_one[b] = val
        sums.append(col_sum(val))
    outs.append(cps.start(sum_one, sum_out))
    mean2 = lane_groups(jnp.concatenate(sums, axis=0), width) / size
    sums = []
    for b in range(count):
        off = sum_one[b] - mean2[b : b + 1]
        sums.append(col_sum(off * off))
    rstd2 = lax.rsqrt(lane_groups(jnp.concatenate(sums, axis=0), width) / size + EPS)
    stat_out[0, 0:count, :] = mean2
    stat_out[1, 0:count, :] = rstd2
    for b in range(count):
        hat = (sum_one[b] - mean2[b : b + 1]) * rstd2[b : b + 1]
        pre = hat * row(SECOND_GAIN) + row(SECOND_SHIFT)
        act = (pre * sigmoid(pre)).astype(bf16)
        a2t[b] = nt(eye, act).astype(bf16)
        put_pads(apad, b, nn(shift[...], act).astype(bf16), side, points)

    wait_all(w2_cp)
    w2_rows = w2[...].reshape(9 * chans, chans)
    sums = []
    for b in range(count):
        lhs = jnp.concatenate(taps(apad, b, 1, side, points), axis=1)
        val = nn(lhs, w2_rows) + row(SECOND_BIAS) + nt(eye, xin[b])
        resid[b] = val
        sums.append(col_sum(val))
    outs.append(cps.start(resid, resid_out))
    mean3 = lane_groups(jnp.concatenate(sums, axis=0), width) / size
    sums = []
    for b in range(count):
        off = resid[b] - mean3[b : b + 1]
        sums.append(col_sum(off * off))
    rstd3 = lax.rsqrt(lane_groups(jnp.concatenate(sums, axis=0), width) / size + EPS)

    wait_all(pi_cp)
    wait_all(po_cp)
    wait_all(g_cp)
    pi_q, pi_k, pi_v = pi[0], pi[1], pi[2]
    pi_row = jnp.concatenate([pi_q, pi_k, pi_v], axis=1)
    pi_kt = nt(eye, pi_k).astype(bf16) if chans == points else jnp.transpose(pi_k)
    pi_vt = nt(eye, pi_v).astype(bf16) if chans == points else jnp.transpose(pi_v)
    zero = jnp.zeros((1, chans), f32)
    qb_grad, vb_grad, ob_grad = zero, zero, zero
    gain3, shift3 = [], []
    dpo = None
    for b in range(count):
        hat = (resid[b] - mean3[b : b + 1]) * rstd3[b : b + 1]
        normed = (hat * row(THIRD_GAIN) + row(THIRD_SHIFT)).astype(bf16)
        nmt[b] = nt(eye, normed).astype(bf16)
        lin = nn(normed, pi_row)
        q = (lin[:, :chans] + row(QUERY_BIAS)).astype(bf16)
        k = lin[:, chans : 2 * chans].astype(bf16)
        v = (lin[:, 2 * chans :] + row(VALUE_BIAS)).astype(bf16)
        kt = nt(pi_kt, normed).astype(bf16)
        vt = (nt(pi_vt, normed) + col(VALUE_BIAS)).astype(bf16)
        scores = nt(k, q) * scale
        expo = jnp.exp(scores - jnp.max(scores, axis=0, keepdims=True))
        probs = expo * (1.0 / jnp.sum(expo, axis=0, keepdims=True))
        weights = probs.astype(bf16)
        mixed = nn(vt, weights).astype(bf16)
        mix[b] = mixed
        grad = gin[b]
        part = nt(mixed, grad)
        dpo = part if dpo is None else dpo + part
        grad_mixed = nn(po[...], grad).astype(bf16)
        grad_w = nn(v, grad_mixed)
        grad_v = nt(weights, grad_mixed).astype(bf16)
        inner = probs * grad_w
        grad_s = (inner - probs * jnp.sum(inner, axis=0, keepdims=True)).astype(bf16)
        grad_qt = (nn(kt, grad_s) * scale).astype(bf16)
        grad_q = nt(eye, grad_qt).astype(bf16)
        grad_k = (nn(grad_s, q) * scale).astype(bf16)
        qb_grad = qb_grad + col_sum(grad_q.astype(f32))
        vb_grad = vb_grad + col_sum(grad_v.astype(f32))
        lhs = jnp.concatenate([grad_q, grad_k, grad_v], axis=1)
        gl[b] = lhs
        grad_n = nt(lhs, pi_row)
        gres[b] = grad_n
        gain3.append(col_sum(grad_n * hat))
        shift3.append(col_sum(grad_n))
    outs.append(cps.start(mix, mix_out))
    split_store(dpo_own, dpo_send, ..., dpo, 0, places)
    gain3 = jnp.concatenate(gain3, axis=0)
    shift3 = jnp.concatenate(shift3, axis=0)
    first_mean = lane_groups(shift3 * row(THIRD_GAIN), width) / size
    second_mean = lane_groups(gain3 * row(THIRD_GAIN), width) / size
    sb_grad = zero
    for b in range(count):
        hat = (resid[b] - mean3[b : b + 1]) * rstd3[b : b + 1]
        h = gres[b] * row(THIRD_GAIN)
        grad_out = nt(eye, gin[b])
        ob_grad = ob_grad + col_sum(grad_out)
        val = grad_out + rstd3[b : b + 1] * (
            h - first_mean[b : b + 1] - hat * second_mean[b : b + 1]
        )
        gres[b] = val
        sb_grad = sb_grad + col_sum(val)
        put_pads(gpad, b, nn(shift[...], val.astype(bf16)).astype(bf16), side, points)
    outs.append(cps.start(gres, gres_out))
    outs.append(cps.start(gpad, gpad_out))

    nm_all = jnp.concatenate([nmt[b] for b in range(count)], axis=1)
    gl_all = jnp.concatenate([gl[b] for b in range(count)], axis=0)
    for j in range(3):
        val = nn(nm_all, gl_all[:, j * chans : (j + 1) * chans])
        split_store(dpi_own, dpi_send, j, val, 1, places)
    a_all = jnp.concatenate([a2t[b] for b in range(count)], axis=1)
    moved = [taps(gpad, b, -1, side, points) for b in range(count)]
    for tap in range(9):
        val = nn(a_all, jnp.concatenate([moved[b][tap] for b in range(count)], axis=0))
        split_store(dw2_own, dw2_send, tap, val, 0, places)

    vec_out[...] = jnp.concatenate(
        [sb_grad, col_sum(gain3), col_sum(shift3), qb_grad, vb_grad, ob_grad, zero, zero], axis=0
    )
    wait_all(outs)


def middle_kernel(pieces, count, *refs):
    it = iter(refs)

    def take(n):
        return [next(it) for _ in range(n)]

    w2_in, vec_in = (take(pieces) for _ in range(2))
    gpad_in, sum_in, a1t_in, stat = take(4)
    dw1_own = next(it)
    dw1_send = next(it) if pieces == 2 else None
    vec_out, time_out, hpad_out = take(3)
    w2, vec, gpad, sum_one, a1t, shift, hpad, grad = take(8)
    sems = next(it)
    cps = Copies(sems)
    places = places_of(pieces)
    chans, points = a1t.shape[1], a1t.shape[2]
    side = side_of(points)
    width = chans // GROUPS
    size = float(width * points)

    vec_cp = load_split(cps, vec_in, vec, 1, places)
    w2_cp = load_split(cps, w2_in, w2, 1, places)
    gpad_cp = cps.start(gpad_in, gpad)
    sum_cp = cps.start(sum_in, sum_one)
    a1t_cp = cps.start(a1t_in, a1t)
    fill_shift(shift, side)
    zero_pads(hpad, side, points)
    wait_all(vec_cp)

    def row(j):
        return vec[j : j + 1, :]

    wait_all(w2_cp)
    gpad_cp.wait()
    sum_cp.wait()
    mean2, rstd2 = stat[0], stat[1]
    w2_cols = jnp.concatenate([w2[k] for k in range(9)], axis=1)
    gain, shift_g = [], []
    for b in range(count):
        back = nt(jnp.concatenate(taps(gpad, b, -1, side, points), axis=1), w2_cols)
        hat = (sum_one[b] - mean2[b : b + 1]) * rstd2[b : b + 1]
        pre = hat * row(SECOND_GAIN) + row(SECOND_SHIFT)
        val = back * silu_slope(pre, sigmoid(pre))
        grad[b] = val
        gain.append(col_sum(val * hat))
        shift_g.append(col_sum(val))
    gain = jnp.concatenate(gain, axis=0)
    shift_g = jnp.concatenate(shift_g, axis=0)
    first_mean = lane_groups(shift_g * row(SECOND_GAIN), width) / size
    second_mean = lane_groups(gain * row(SECOND_GAIN), width) / size
    times = []
    for b in range(count):
        hat = (sum_one[b] - mean2[b : b + 1]) * rstd2[b : b + 1]
        val = rstd2[b : b + 1] * (
            grad[b] * row(SECOND_GAIN) - first_mean[b : b + 1] - hat * second_mean[b : b + 1]
        )
        times.append(col_sum(val))
        put_pads(hpad, b, nn(shift[...], val.astype(bf16)).astype(bf16), side, points)
    out_cp = cps.start(hpad, hpad_out)
    times = jnp.concatenate(times, axis=0)
    time_out[0:count, :] = times
    zero = jnp.zeros((1, chans), f32)
    vec_out[...] = jnp.concatenate(
        [col_sum(gain), col_sum(shift_g), col_sum(times)] + [zero] * 5, axis=0
    )
    a1t_cp.wait()
    a_all = jnp.concatenate([a1t[b] for b in range(count)], axis=1)
    moved = [taps(hpad, b, -1, side, points) for b in range(count)]
    for tap in range(9):
        val = nn(a_all, jnp.concatenate([moved[b][tap] for b in range(count)], axis=0))
        split_store(dw1_own, dw1_send, tap, val, 1, places)
    out_cp.wait()


def last_kernel(pieces, count, *refs):
    it = iter(refs)

    def take(n):
        return [next(it) for _ in range(n)]

    x_in, w1_in, po_in, vec_in = (take(pieces) for _ in range(4))
    hpad_in, resid_in, gres_in, mix_in = take(4)
    block_own, image_own = take(2)
    block_send, image_send = take(2) if pieces == 2 else (None, None)
    vec_out = next(it)
    xin, w1, po, vec, hpad, resid, gres, mix = take(8)
    sems = next(it)
    cps = Copies(sems)
    places = places_of(pieces)
    chans, points = xin.shape[1], xin.shape[2]
    side = side_of(points)
    width = chans // GROUPS
    size = float(width * points)

    vec_cp = load_split(cps, vec_in, vec, 1, places)
    po_cp = load_split(cps, po_in, po, 0, places)
    mix_cp = cps.start(mix_in, mix)
    resid_cp = cps.start(resid_in, resid)
    x_cp = load_images(cps, x_in, xin, places, count)
    w1_cp = load_split(cps, w1_in, w1, 2, places)
    hpad_cp = cps.start(hpad_in, hpad)
    gres_cp = cps.start(gres_in, gres)
    wait_all(vec_cp)
    vcols = jnp.transpose(vec[...])

    def col(j):
        return vcols[:, j : j + 1]

    wait_all(po_cp)
    mix_cp.wait()
    resid_cp.wait()
    po_t = jnp.transpose(po[...].astype(f32)).astype(bf16)
    for b in range(count):
        val = jnp.transpose(resid[b]) + nn(po_t, mix[b]) + col(OUTPUT_BIAS)
        split_store(block_own, block_send, b, val, 0, places)

    wait_all(x_cp)
    wait_all(w1_cp)
    hpad_cp.wait()
    gres_cp.wait()
    w1_cols = jnp.concatenate([w1[k] for k in range(9)], axis=1)
    zero = jnp.zeros((chans, 1), f32)
    gain_sum, shift_sum = zero, zero

    def groups(v):
        total = jnp.sum(v.reshape(GROUPS, width, 1), axis=1, keepdims=True) / size
        return jnp.broadcast_to(total, (GROUPS, width, 1)).reshape(chans, 1)

    for b in range(count):
        back = nt(w1_cols, jnp.concatenate(taps(hpad, b, -1, side, points), axis=1))
        x3 = xin[b].astype(f32).reshape(GROUPS, width, points)
        mean = jnp.sum(jnp.sum(x3, axis=2, keepdims=True), axis=1, keepdims=True) / size
        off = x3 - mean
        var = jnp.sum(jnp.sum(off * off, axis=2, keepdims=True), axis=1, keepdims=True) / size
        rstd = lax.rsqrt(var + EPS)
        hat = (off * rstd).reshape(chans, points)
        rstd = jnp.broadcast_to(rstd, (GROUPS, width, 1)).reshape(chans, 1)
        pre = hat * col(FIRST_GAIN) + col(FIRST_SHIFT)
        val = back * silu_slope(pre, sigmoid(pre))
        gain = jnp.sum(val * hat, axis=1, keepdims=True)
        shift_g = jnp.sum(val, axis=1, keepdims=True)
        gain_sum = gain_sum + gain
        shift_sum = shift_sum + shift_g
        first_mean = groups(shift_g * col(FIRST_GAIN))
        second_mean = groups(gain * col(FIRST_GAIN))
        val = rstd * (val * col(FIRST_GAIN) - first_mean - hat * second_mean)
        val = val + jnp.transpose(gres[b])
        split_store(image_own, image_send, b, val, 0, places)
    lane = lax.broadcasted_iota(jnp.int32, (chans, 128), 1)
    both = jnp.where(lane == 0, gain_sum, 0.0) + jnp.where(lane == 1, shift_sum, 0.0)
    vec_out[...] = jnp.transpose(both)[0:8]


def swap(value, axis, size, bit):
    return lax.ppermute(value, axis, [(i, i ^ bit) for i in range(size)])


def phases_of(size):
    bits = size.bit_length() - 1
    out = []
    low = 0
    while low < bits:
        out.append((low, min(2, bits - low)))
        low += 2
    return out


def scatter_sum(total, batch):
    me = lax.axis_index("batch")
    for low, bits in phases_of(batch):
        m = 1 << bits
        mine = (me >> low) & (m - 1)
        parts = total.reshape(m, total.shape[0] // m, total.shape[1])
        got = [
            swap(
                lax.dynamic_index_in_dim(parts, mine ^ j, 0, False).astype(bf16),
                "batch",
                batch,
                j << low,
            )
            for j in range(1, m)
        ]
        total = lax.dynamic_index_in_dim(parts, mine, 0, False).astype(f32)
        for g in got:
            total = total + g.astype(f32)
    return total


def gather_all(piece, extra, batch):
    me = lax.axis_index("batch")
    rows = piece.shape[0]
    for low, bits in reversed(phases_of(batch)):
        m = 1 << bits
        mine = (me >> low) & (m - 1)
        both = jnp.concatenate([piece, extra], axis=0)
        all_of = [both] + [swap(both, "batch", batch, j << low) for j in range(1, m)]
        extra = jnp.concatenate([a[rows:] for a in all_of], axis=0)
        parts = jnp.stack([a[:rows] for a in all_of], axis=0)
        for i in range(bits):
            shape = parts.shape
            split = parts.reshape((1 << (bits - 1 - i), 2, 1 << i) + shape[1:])
            turned = jnp.flip(split, axis=1)
            parts = jnp.where(((mine >> i) & 1) == 1, turned, split).reshape(shape)
        piece = parts.reshape(m * rows, piece.shape[1])
        rows = piece.shape[0]
    return piece, extra


def pack(arrays, unit):
    flat = jnp.concatenate([a.reshape(-1, 128) for a in arrays], axis=0)
    pad = -flat.shape[0] % unit
    return jnp.pad(flat, ((0, pad), (0, 0)))


def unpack(flat, shapes):
    out = []
    at = 0
    for shape in shapes:
        n = math.prod(shape) // 128
        out.append(flat[at : at + n].reshape(shape).astype(f32))
        at += n
    return out


def per_device(
    batch,
    tensor,
    images,
    timesteps,
    embed_table,
    first_gain,
    first_shift,
    first_conv,
    first_bias,
    time_weight,
    time_bias,
    second_gain,
    second_shift,
    second_conv,
    second_bias,
    third_gain,
    third_shift,
    project_in,
    query_bias,
    value_bias,
    project_out,
    output_bias,
    cotangent,
):
    per_batch, local, points = images.shape
    chans = local * tensor
    count = per_batch // tensor
    steps, embed = embed_table.shape
    pieces = 2 if tensor == 2 else 1
    me = lax.axis_index("tensor")
    vec = jnp.stack(
        [
            first_gain,
            first_shift,
            first_bias,
            time_bias,
            second_gain,
            second_shift,
            second_bias,
            third_gain,
            third_shift,
            query_bias,
            value_bias,
            output_bias,
        ]
        + [output_bias] * 4,
        axis=0,
    )

    def other_half(array):
        parts = array.reshape((2, count) + array.shape[1:])
        return lax.dynamic_index_in_dim(parts, 1 - me, 0, False)

    def images_of(array):
        if pieces == 2:
            return [array, swap(other_half(array), "tensor", 2, 1)]
        return [lax.all_to_all(array, "tensor", 0, 1, tiled=True)]

    def whole(array, axis):
        if pieces == 2:
            return [array, swap(array, "tensor", 2, 1)]
        return [lax.all_gather(array, "tensor", axis=axis, tiled=True)]

    x_in = images_of(images)
    vec_in = whole(vec, 1)
    tw_in = whole(time_weight, 1)
    w1_in = whole(first_conv, 2)
    w2_in = whole(second_conv, 1)
    pi_in = whole(project_in, 2)
    po_in = whole(project_out, 0)
    g_in = images_of(cotangent)
    my_steps = timesteps if pieces == 2 else lax.dynamic_slice_in_dim(timesteps, me * count, count)

    side = side_of(points)
    image_b = (count, chans, points)
    image_p = (count, points, chans)
    pads = (3, count, points + 2 * side, chans)

    def shape(s, d):
        return jax.ShapeDtypeStruct(s, d)

    def grads(full, axis):
        if pieces == 1:
            return [shape(full, f32)]
        half = full[:axis] + (full[axis] // 2,) + full[axis + 1 :]
        return [shape(half, bf16), shape(half, bf16)]

    dw2_t, dpo_t = grads((9, chans, chans), 1), grads((chans, chans), 0)
    dpi_t, dw1_t = grads((3, chans, chans), 2), grads((9, chans, chans), 2)
    params = pltpu.CompilerParams(vmem_limit_bytes=VMEM_LIMIT)
    n_grad = 3 * pieces
    front = pl.pallas_call(
        functools.partial(front_kernel, pieces, count),
        out_shape=[g[0] for g in (dw2_t, dpo_t, dpi_t)]
        + ([g[1] for g in (dw2_t, dpo_t, dpi_t)] if pieces == 2 else [])
        + [
            shape((8, chans), f32),
            shape((2, count, chans), f32),
            shape(pads, bf16),
            shape(image_p, f32),
            shape(image_b, bf16),
            shape(image_p, f32),
            shape(image_p, f32),
            shape(image_b, bf16),
        ],
        in_specs=[ANY] * (8 * pieces) + [SMEM, ANY],
        out_specs=[VMEM] * (n_grad + 2) + [ANY] * 6,
        scratch_shapes=[
            pltpu.VMEM(image_b, bf16),
            pltpu.VMEM(image_b, bf16),
            pltpu.VMEM((9, chans, chans), bf16),
            pltpu.VMEM((9, chans, chans), bf16),
            pltpu.VMEM((3, chans, chans), bf16),
            pltpu.VMEM((chans, chans), bf16),
            pltpu.VMEM((embed, chans), bf16),
            pltpu.VMEM((16, chans), f32),
            pltpu.VMEM((count, 16, embed), bf16),
            pltpu.VMEM((3 * points, points), bf16),
            pltpu.VMEM(pads, bf16),
            pltpu.VMEM(pads, bf16),
            pltpu.VMEM(image_p, f32),
            pltpu.VMEM(image_b, bf16),
            pltpu.VMEM(image_p, f32),
            pltpu.VMEM(image_p, f32),
            pltpu.VMEM(image_b, bf16),
            pltpu.VMEM(image_b, bf16),
            pltpu.VMEM(image_b, bf16),
            pltpu.VMEM((count, points, 3 * chans), bf16),
            pltpu.SemaphoreType.DMA((8 * pieces + count + 6,)),
        ],
        compiler_params=params,
        name="front",
    )(*x_in, *g_in, *w1_in, *w2_in, *pi_in, *po_in, *tw_in, *vec_in, my_steps, embed_table)
    g_front = front[:n_grad]
    vec_a, stat, gpad, sum_one, a1t, resid, gres, mix = front[n_grad:]

    middle = pl.pallas_call(
        functools.partial(middle_kernel, pieces, count),
        out_shape=dw1_t + [shape((8, chans), f32), shape((count, chans), f32), shape(pads, bf16)],
        in_specs=[ANY] * (2 * pieces + 3) + [VMEM],
        out_specs=[VMEM] * (pieces + 2) + [ANY],
        scratch_shapes=[
            pltpu.VMEM((9, chans, chans), bf16),
            pltpu.VMEM((16, chans), f32),
            pltpu.VMEM(pads, bf16),
            pltpu.VMEM(image_p, f32),
            pltpu.VMEM(image_b, bf16),
            pltpu.VMEM((3 * points, points), bf16),
            pltpu.VMEM(pads, bf16),
            pltpu.VMEM(image_p, f32),
            pltpu.SemaphoreType.DMA((2 * pieces + 4,)),
        ],
        compiler_params=params,
        name="middle",
    )(*w2_in, *vec_in, gpad, sum_one, a1t, stat)
    g_middle = middle[:pieces]
    vec_b, times, hpad = middle[pieces:]

    if pieces == 2:
        half = (count, chans // 2, points)
        out_t = [shape(half, f32)] * 2 + [shape(half, bf16)] * 2
    else:
        out_t = [shape(image_b, f32)] * 2
    last = pl.pallas_call(
        functools.partial(last_kernel, pieces, count),
        out_shape=out_t + [shape((8, chans), f32)],
        in_specs=[ANY] * (4 * pieces + 4),
        out_specs=[VMEM] * (2 * pieces + 1),
        scratch_shapes=[
            pltpu.VMEM(image_b, bf16),
            pltpu.VMEM((9, chans, chans), bf16),
            pltpu.VMEM((chans, chans), bf16),
            pltpu.VMEM((16, chans), f32),
            pltpu.VMEM(pads, bf16),
            pltpu.VMEM(image_p, f32),
            pltpu.VMEM(image_p, f32),
            pltpu.VMEM(image_b, bf16),
            pltpu.SemaphoreType.DMA((4 * pieces + 4,)),
        ],
        compiler_params=params,
        name="last",
    )(*x_in, *w1_in, *po_in, *vec_in, hpad, resid, gres, mix)
    block, image = last[0], last[1]
    vec_c = last[-1]

    def placed(own, send):
        if pieces == 2:
            got = swap(send, "tensor", 2, 1).astype(f32)
            low = jnp.where(me == 0, own, got)
            high = jnp.where(me == 0, got, own)
            return jnp.concatenate([low, high], axis=0)
        return lax.all_to_all(own, "tensor", 1, 0, tiled=True)

    block_out = placed(block, last[pieces])
    images_grad = placed(image, last[pieces + 1])

    unit = 16 * batch

    def over_tensor(own, send, axis):
        if pieces == 2:
            return own.astype(f32) + swap(send, "tensor", 2, 1).astype(f32)
        return lax.psum_scatter(own, "tensor", scatter_dimension=axis, tiled=True)

    dw2 = over_tensor(g_front[0], g_front[-3], 1)
    dpo = over_tensor(g_front[1], g_front[-2], 0)
    dpi = over_tensor(g_front[2], g_front[-1], 2)
    dw1 = over_tensor(g_middle[0], g_middle[-1], 2)
    shapes_a = [dw2.shape, dpo.shape, dpi.shape]
    piece_a = scatter_sum(pack([dw2, dpo, dpi], unit), batch)
    piece_b = scatter_sum(pack([dw1], unit), batch)

    vecs = jnp.concatenate([vec_a, vec_b, vec_c], axis=0)
    if pieces == 2:
        vecs = vecs + swap(vecs, "tensor", 2, 1)
        theirs = swap(times, "tensor", 2, 1)
        times = jnp.concatenate(
            [jnp.where(me == 0, times, theirs), jnp.where(me == 0, theirs, times)], axis=0
        )
    else:
        vecs = lax.psum(vecs, "tensor")
        times = lax.all_gather(times, "tensor", axis=0, tiled=True)
    stamp = jnp.zeros((8, chans), f32)
    stamp = stamp.at[:per_batch, 0].set((timesteps >> 5).astype(f32))
    stamp = stamp.at[:per_batch, 1].set((timesteps & 31).astype(f32))
    small = jnp.concatenate([vecs, times, stamp], axis=0)
    n_small = small.shape[0]
    small = small.reshape(-1, 128).astype(bf16)
    done_a, _ = gather_all(piece_a.astype(bf16), small[:0], batch)
    done_b, small = gather_all(piece_b.astype(bf16), small, batch)
    second_conv_grad, project_out_grad, project_in_grad = unpack(done_a, shapes_a)
    (first_conv_grad,) = unpack(done_b, [dw1.shape])

    small = small.reshape(batch, n_small, chans)
    sums = jnp.sum(small[:, :24].astype(f32), axis=0)
    mine = lax.dynamic_slice_in_dim(sums, me * local, local, axis=1)
    all_times = small[:, 24 : 24 + per_batch].reshape(batch * per_batch, chans)
    stamps = small[:, 24 + per_batch :].astype(jnp.int32)[:, :per_batch]
    all_steps = (stamps[:, :, 0] * 32 + stamps[:, :, 1]).reshape(batch * per_batch)
    one_hot = (all_steps[:, None] == jnp.arange(steps, dtype=jnp.int32)[None, :]).astype(bf16)
    emb = nn(one_hot, embed_table)
    sig = sigmoid(emb)
    act = (emb * sig).astype(bf16)
    my_times = lax.dynamic_slice_in_dim(all_times, me * local, local, axis=1)
    time_weight_grad = lax.dot_general(
        act, my_times, (((0,), (0,)), ((), ())), preferred_element_type=f32
    )
    if pieces == 2:
        tw = jnp.where(
            me == 0, jnp.concatenate(tw_in, axis=1), jnp.concatenate(tw_in[::-1], axis=1)
        )
    else:
        tw = tw_in[0]
    grad_emb = (nt(all_times, tw) * silu_slope(emb, sig)).astype(bf16)
    table_grad = lax.dot_general(
        one_hot, grad_emb, (((0,), (0,)), ((), ())), preferred_element_type=f32
    )
    return (
        block_out,
        images_grad,
        table_grad,
        mine[16],
        mine[17],
        first_conv_grad,
        mine[10],
        time_weight_grad,
        mine[10],
        mine[8],
        mine[9],
        second_conv_grad,
        mine[0],
        mine[1],
        mine[2],
        project_in_grad,
        mine[3],
        mine[4],
        project_out_grad,
        mine[5],
    )


def solution(mesh):
    in_specs = (
        P("batch", "tensor", None),
        P("batch"),
        P(),
        P("tensor"),
        P("tensor"),
        P(None, None, "tensor"),
        P("tensor"),
        P(None, "tensor"),
        P("tensor"),
        P("tensor"),
        P("tensor"),
        P(None, "tensor", None),
        P("tensor"),
        P("tensor"),
        P("tensor"),
        P(None, None, "tensor"),
        P("tensor"),
        P("tensor"),
        P("tensor", None),
        P("tensor"),
        P("batch", "tensor", None),
    )
    out_specs = (
        P("batch", "tensor", None),
        P("batch", "tensor", None),
        P(),
        P("tensor"),
        P("tensor"),
        P(None, None, "tensor"),
        P("tensor"),
        P(None, "tensor"),
        P("tensor"),
        P("tensor"),
        P("tensor"),
        P(None, "tensor", None),
        P("tensor"),
        P("tensor"),
        P("tensor"),
        P(None, None, "tensor"),
        P("tensor"),
        P("tensor"),
        P("tensor", None),
        P("tensor"),
    )
    sizes = dict(mesh.shape)
    return jax.shard_map(
        functools.partial(per_device, sizes["batch"], sizes["tensor"]),
        mesh=mesh,
        in_specs=in_specs,
        out_specs=out_specs,
        check_vma=False,
    )
```

```python
import functools
import math

import jax
import jax.numpy as jnp
from jax import lax
from jax.experimental import pallas as pl
from jax.experimental.pallas import tpu as pltpu
from jax.sharding import PartitionSpec as P

GROUPS = 32
LANES = 128
BLOCK = 32
EPS = 1e-06
VMEM_LIMIT = 56 * 1024 * 1024
ANY = pl.BlockSpec(memory_space=pl.ANY)
VMEM = pl.BlockSpec(memory_space=pltpu.VMEM)
SMEM = pl.BlockSpec(memory_space=pltpu.SMEM)
f32 = jnp.float32
bf16 = jnp.bfloat16

(
    FIRST_GAIN,
    FIRST_SHIFT,
    FIRST_BIAS,
    TIME_BIAS,
    SECOND_GAIN,
    SECOND_SHIFT,
    SECOND_BIAS,
    THIRD_GAIN,
    THIRD_SHIFT,
    QUERY_BIAS,
    VALUE_BIAS,
    OUTPUT_BIAS,
) = range(12)


def nn(a, b):
    return lax.dot_general(a, b, (((1,), (0,)), ((), ())), preferred_element_type=f32)


def nt(a, b):
    return lax.dot_general(a, b, (((1,), (1,)), ((), ())), preferred_element_type=f32)


def sigmoid(v):
    return 0.5 * jnp.tanh(0.5 * v) + 0.5


def silu_slope(v, sig):
    return sig * (1.0 + v * (1.0 - sig))


def col_sum(v):
    return jnp.sum(v, axis=0, keepdims=True)


def lane_groups(v, width):
    lanes = v.shape[1]
    lane = lax.broadcasted_iota(jnp.int32, v.shape, 1)
    step = 1
    while step < width:
        up = pltpu.roll(v, step, 1)
        down = pltpu.roll(v, lanes - step, 1)
        v = v + jnp.where((lane & step) != 0, up, down)
        step *= 2
    return v


def fill_shift(shift_ref, side):
    points = shift_ref.shape[1]
    to = lax.broadcasted_iota(jnp.int32, (points, points), 0)
    of = lax.broadcasted_iota(jnp.int32, (points, points), 1)
    for d in range(3):
        s = d - 1
        col = (to & (side - 1)) + s
        hit = (of == to + s) & (col >= 0) & (col < side)
        shift_ref[d * points : (d + 1) * points, :] = jnp.where(hit, 1.0, 0.0).astype(bf16)


def zero_pads(pad_ref, side, points):
    images, chans = pad_ref.shape[1], pad_ref.shape[3]
    for d in range(3):
        for b in range(images):
            pad_ref[d, b, 0:side, :] = jnp.zeros((side, chans), bf16)
            pad_ref[d, b, side + points : 2 * side + points, :] = jnp.zeros((side, chans), bf16)


def put_pads(pad_ref, b, moved, side, points):
    for d in range(3):
        pad_ref[d, b, side : side + points, :] = moved[d * points : (d + 1) * points]


def taps(pad_ref, b, sign, side, points):
    out = []
    for dr in (-1, 0, 1):
        for dc in (-1, 0, 1):
            top = side + sign * dr * side
            out.append(pad_ref[1 + sign * dc, b, top : top + points, :])
    return out


class Copies:
    def __init__(self, sems):
        self.sems = sems
        self.used = 0

    def start(self, src, dst):
        copy = pltpu.make_async_copy(src, dst, self.sems.at[self.used])
        self.used += 1
        copy.start()
        return copy


def wait_all(copies):
    for c in copies:
        c.wait()


def side_of(points):
    return math.isqrt(points)


def load_split(cps, refs, dst, axis, places):
    out = []
    for ref, place in zip(refs, places, strict=True):
        size = ref.shape[axis]
        idx = [slice(None)] * len(ref.shape)
        idx[axis] = pl.ds(pl.multiple_of(place * size, size), size)
        out.append(cps.start(ref, dst.at[tuple(idx)]))
    return out


def load_images(cps, refs, dst, places, count):
    out = []
    for j, (ref, place) in enumerate(zip(refs, places, strict=True)):
        size = ref.shape[1]
        first = pl.multiple_of(places[0] * count, count) if j == 0 else 0
        out.append(
            cps.start(
                ref.at[pl.ds(first, count)],
                dst.at[:, pl.ds(pl.multiple_of(place * size, size), size), :],
            )
        )
    return out


def places_of(pieces):
    if pieces == 1:
        return [0]
    me = lax.axis_index("tensor")
    return [me, 1 - me]


def split_store(own_ref, send_ref, at, value, axis, places):
    if send_ref is None:
        own_ref[at] = value.astype(own_ref.dtype)
        return
    half = value.shape[axis] // 2
    low = lax.slice_in_dim(value, 0, half, axis=axis)
    high = lax.slice_in_dim(value, half, 2 * half, axis=axis)
    first = places[0] == 0
    own_ref[at] = jnp.where(first, low, high).astype(own_ref.dtype)
    send_ref[at] = jnp.where(first, high, low).astype(send_ref.dtype)


def pack_store(own_ref, send_ref, at, value, axis, places):
    half = value.shape[axis] // 2
    low = lax.slice_in_dim(value, 0, half, axis=axis)
    high = lax.slice_in_dim(value, half, 2 * half, axis=axis)
    first = places[0] == 0
    own = jnp.where(first, low, high).astype(own_ref.dtype)
    send = jnp.where(first, high, low).astype(send_ref.dtype)
    rows = own.shape[0]
    for i in range(own.shape[1] // LANES):
        lanes = slice(i * LANES, (i + 1) * LANES)
        own_ref[at : at + rows, :] = own[:, lanes]
        send_ref[at : at + rows, :] = send[:, lanes]
        at += rows
    return at


def front_kernel(pieces, count, *refs):
    it = iter(refs)

    def take(n):
        return [next(it) for _ in range(n)]

    x_in, g_in, w1_in, w2_in, pi_in, po_in, tw_in, vec_in = (take(pieces) for _ in range(8))
    steps_ref, table_ref = take(2)
    if pieces == 2:
        own, send = take(2)
    else:
        dw2_own, dpo_own, dpi_own = take(3)
    vec_out, stat_out = take(2)
    gpad_out, sum_out, a1t_out, resid_out, gres_out, mix_out = take(6)
    xin, gin, w1, w2, pi, po, tw, vec, rows = take(9)
    shift, apad, gpad, sum_one, a1t, resid, gres, mix = take(8)
    a2t, nmt, gl = take(3)
    sems = next(it)

    cps = Copies(sems)
    places = places_of(pieces)
    chans, points = xin.shape[1], xin.shape[2]
    side = side_of(points)
    width = chans // GROUPS
    size = float(width * points)
    scale = chans ** (-0.5)

    x_cp = load_images(cps, x_in, xin, places, count)
    vec_cp = load_split(cps, vec_in, vec, 1, places)
    row_cp = []
    for b in range(count):
        step = steps_ref[places[0] * count + b]
        row_cp.append(
            cps.start(table_ref.at[pl.ds(pl.multiple_of(step // 16 * 16, 16), 16), :], rows.at[b])
        )
    tw_cp = load_split(cps, tw_in, tw, 1, places)
    w1_cp = load_split(cps, w1_in, w1, 2, places)
    w2_cp = load_split(cps, w2_in, w2, 1, places)
    pi_cp = load_split(cps, pi_in, pi, 2, places)
    po_cp = load_split(cps, po_in, po, 0, places)
    g_cp = load_images(cps, g_in, gin, places, count)

    fill_shift(shift, side)
    zero_pads(apad, side, points)
    zero_pads(gpad, side, points)
    eye = shift[points : 2 * points, :]

    wait_all(vec_cp)
    vcols = jnp.transpose(vec[...])

    def col(j):
        return vcols[:, j : j + 1]

    def row(j):
        return vec[j : j + 1, :]

    wait_all(x_cp)
    for b in range(count):
        x3 = xin[b].astype(f32).reshape(GROUPS, width, points)
        mean = jnp.sum(jnp.sum(x3, axis=2, keepdims=True), axis=1, keepdims=True) / size
        off = x3 - mean
        var = jnp.sum(jnp.sum(off * off, axis=2, keepdims=True), axis=1, keepdims=True) / size
        hat = (off * lax.rsqrt(var + EPS)).reshape(chans, points)
        pre = hat * col(FIRST_GAIN) + col(FIRST_SHIFT)
        act = (pre * sigmoid(pre)).astype(bf16)
        a1t[b] = act
        put_pads(apad, b, nt(shift[...], act).astype(bf16), side, points)
    outs = [cps.start(a1t, a1t_out)]

    wait_all(row_cp)
    wait_all(tw_cp)
    picked = []
    for b in range(count):
        step = steps_ref[places[0] * count + b]
        r = lax.broadcasted_iota(jnp.int32, (16, rows.shape[2]), 0)
        picked.append(
            col_sum(jnp.where(r == lax.rem(step, 16), rows[b].astype(f32), 0.0))
        )
    emb = jnp.concatenate(picked + picked[:1] * (8 - count), axis=0)
    time_add = nn((emb * sigmoid(emb)).astype(bf16), tw[...]) + row(TIME_BIAS)

    wait_all(w1_cp)
    w1_rows = w1[...].reshape(9 * chans, chans)
    sums = []
    for b in range(count):
        lhs = jnp.concatenate(taps(apad, b, 1, side, points), axis=1)
        val = nn(lhs, w1_rows) + (row(FIRST_BIAS) + time_add[b : b + 1])
        sum_one[b] = val
        sums.append(col_sum(val))
    outs.append(cps.start(sum_one, sum_out))
    mean2 = lane_groups(jnp.concatenate(sums, axis=0), width) / size
    sums = []
    for b in range(count):
        off = sum_one[b] - mean2[b : b + 1]
        sums.append(col_sum(off * off))
    rstd2 = lax.rsqrt(lane_groups(jnp.concatenate(sums, axis=0), width) / size + EPS)
    stat_out[0, 0:count, :] = mean2
    stat_out[1, 0:count, :] = rstd2
    for b in range(count):
        hat = (sum_one[b] - mean2[b : b + 1]) * rstd2[b : b + 1]
        pre = hat * row(SECOND_GAIN) + row(SECOND_SHIFT)
        act = (pre * sigmoid(pre)).astype(bf16)
        a2t[b] = nt(eye, act).astype(bf16)
        put_pads(apad, b, nn(shift[...], act).astype(bf16), side, points)

    wait_all(w2_cp)
    w2_rows = w2[...].reshape(9 * chans, chans)
    sums = []
    for b in range(count):
        lhs = jnp.concatenate(taps(apad, b, 1, side, points), axis=1)
        val = nn(lhs, w2_rows) + row(SECOND_BIAS) + nt(eye, xin[b])
        resid[b] = val
        sums.append(col_sum(val))
    outs.append(cps.start(resid, resid_out))
    mean3 = lane_groups(jnp.concatenate(sums, axis=0), width) / size
    sums = []
    for b in range(count):
        off = resid[b] - mean3[b : b + 1]
        sums.append(col_sum(off * off))
    rstd3 = lax.rsqrt(lane_groups(jnp.concatenate(sums, axis=0), width) / size + EPS)

    wait_all(pi_cp)
    wait_all(po_cp)
    wait_all(g_cp)
    pi_q, pi_k, pi_v = pi[0], pi[1], pi[2]
    pi_row = jnp.concatenate([pi_q, pi_k, pi_v], axis=1)
    pi_kt = nt(eye, pi_k).astype(bf16) if chans == points else jnp.transpose(pi_k)
    pi_vt = nt(eye, pi_v).astype(bf16) if chans == points else jnp.transpose(pi_v)
    zero = jnp.zeros((1, chans), f32)
    qb_grad, vb_grad, ob_grad = zero, zero, zero
    gain3, shift3 = [], []
    dpo = None
    for b in range(count):
        hat = (resid[b] - mean3[b : b + 1]) * rstd3[b : b + 1]
        normed = (hat * row(THIRD_GAIN) + row(THIRD_SHIFT)).astype(bf16)
        nmt[b] = nt(eye, normed).astype(bf16)
        lin = nn(normed, pi_row)
        q = (lin[:, :chans] + row(QUERY_BIAS)).astype(bf16)
        k = lin[:, chans : 2 * chans].astype(bf16)
        v = (lin[:, 2 * chans :] + row(VALUE_BIAS)).astype(bf16)
        kt = nt(pi_kt, normed).astype(bf16)
        vt = (nt(pi_vt, normed) + col(VALUE_BIAS)).astype(bf16)
        scores = nt(k, q) * scale
        expo = jnp.exp(scores - jnp.max(scores, axis=0, keepdims=True))
        probs = expo * (1.0 / jnp.sum(expo, axis=0, keepdims=True))
        weights = probs.astype(bf16)
        mixed = nn(vt, weights).astype(bf16)
        mix[b] = mixed
        grad = gin[b]
        part = nt(mixed, grad)
        dpo = part if dpo is None else dpo + part
        grad_mixed = nn(po[...], grad).astype(bf16)
        grad_w = nn(v, grad_mixed)
        grad_v = nt(weights, grad_mixed).astype(bf16)
        inner = probs * grad_w
        grad_s = (inner - probs * jnp.sum(inner, axis=0, keepdims=True)).astype(bf16)
        grad_qt = (nn(kt, grad_s) * scale).astype(bf16)
        grad_q = nt(eye, grad_qt).astype(bf16)
        grad_k = (nn(grad_s, q) * scale).astype(bf16)
        qb_grad = qb_grad + col_sum(grad_q.astype(f32))
        vb_grad = vb_grad + col_sum(grad_v.astype(f32))
        lhs = jnp.concatenate([grad_q, grad_k, grad_v], axis=1)
        gl[b] = lhs
        grad_n = nt(lhs, pi_row)
        gres[b] = grad_n
        gain3.append(col_sum(grad_n * hat))
        shift3.append(col_sum(grad_n))
    outs.append(cps.start(mix, mix_out))
    at = 0
    if pieces == 2:
        at = pack_store(own, send, at, dpo, 0, places)
    else:
        dpo_own[...] = dpo
    gain3 = jnp.concatenate(gain3, axis=0)
    shift3 = jnp.concatenate(shift3, axis=0)
    first_mean = lane_groups(shift3 * row(THIRD_GAIN), width) / size
    second_mean = lane_groups(gain3 * row(THIRD_GAIN), width) / size
    sb_grad = zero
    for b in range(count):
        hat = (resid[b] - mean3[b : b + 1]) * rstd3[b : b + 1]
        h = gres[b] * row(THIRD_GAIN)
        grad_out = nt(eye, gin[b])
        ob_grad = ob_grad + col_sum(grad_out)
        val = grad_out + rstd3[b : b + 1] * (
            h - first_mean[b : b + 1] - hat * second_mean[b : b + 1]
        )
        gres[b] = val
        sb_grad = sb_grad + col_sum(val)
        put_pads(gpad, b, nn(shift[...], val.astype(bf16)).astype(bf16), side, points)
    outs.append(cps.start(gres, gres_out))
    outs.append(cps.start(gpad, gpad_out))

    nm_all = jnp.concatenate([nmt[b] for b in range(count)], axis=1)
    gl_all = jnp.concatenate([gl[b] for b in range(count)], axis=0)
    for j in range(3):
        val = nn(nm_all, gl_all[:, j * chans : (j + 1) * chans])
        if pieces == 2:
            at = pack_store(own, send, at, val, 1, places)
        else:
            dpi_own[j] = val
    a_all = jnp.concatenate([a2t[b] for b in range(count)], axis=1)
    moved = [taps(gpad, b, -1, side, points) for b in range(count)]
    for tap in range(9):
        val = nn(a_all, jnp.concatenate([moved[b][tap] for b in range(count)], axis=0))
        if pieces == 2:
            at = pack_store(own, send, at, val, 0, places)
        else:
            dw2_own[tap] = val

    vec_out[...] = jnp.concatenate(
        [sb_grad, col_sum(gain3), col_sum(shift3), qb_grad, vb_grad, ob_grad, zero, zero], axis=0
    )
    wait_all(outs)


def middle_kernel(pieces, count, *refs):
    it = iter(refs)

    def take(n):
        return [next(it) for _ in range(n)]

    w2_in, vec_in = (take(pieces) for _ in range(2))
    gpad_in, sum_in, a1t_in, stat, vec_a, steps_ref = take(6)
    own = next(it)
    send = next(it) if pieces == 2 else None
    block_out, hpad_out = take(2)
    w2, vec, gpad, sum_one, a1t, shift, hpad, grad = take(8)
    sems = next(it)
    cps = Copies(sems)
    places = places_of(pieces)
    points, chans = sum_one.shape[1], sum_one.shape[2]
    side = side_of(points)
    width = chans // GROUPS
    size = float(width * points)

    vec_cp = load_split(cps, vec_in, vec, 1, places)
    w2_cp = load_split(cps, w2_in, w2, 1, places)
    gpad_cp = cps.start(gpad_in, gpad)
    sum_cp = cps.start(sum_in, sum_one)
    a1t_cp = cps.start(a1t_in, a1t)
    fill_shift(shift, side)
    zero_pads(hpad, side, points)
    wait_all(vec_cp)

    def row(j):
        return vec[j : j + 1, :]

    wait_all(w2_cp)
    gpad_cp.wait()
    sum_cp.wait()
    mean2, rstd2 = stat[0], stat[1]
    w2_cols = jnp.concatenate([w2[k] for k in range(9)], axis=1)
    gain, shift_g = [], []
    for b in range(count):
        back = nt(jnp.concatenate(taps(gpad, b, -1, side, points), axis=1), w2_cols)
        hat = (sum_one[b] - mean2[b : b + 1]) * rstd2[b : b + 1]
        pre = hat * row(SECOND_GAIN) + row(SECOND_SHIFT)
        val = back * silu_slope(pre, sigmoid(pre))
        grad[b] = val
        gain.append(col_sum(val * hat))
        shift_g.append(col_sum(val))
    gain = jnp.concatenate(gain, axis=0)
    shift_g = jnp.concatenate(shift_g, axis=0)
    first_mean = lane_groups(shift_g * row(SECOND_GAIN), width) / size
    second_mean = lane_groups(gain * row(SECOND_GAIN), width) / size
    times = []
    for b in range(count):
        hat = (sum_one[b] - mean2[b : b + 1]) * rstd2[b : b + 1]
        val = rstd2[b : b + 1] * (
            grad[b] * row(SECOND_GAIN) - first_mean[b : b + 1] - hat * second_mean[b : b + 1]
        )
        times.append(col_sum(val))
        put_pads(hpad, b, nn(shift[...], val.astype(bf16)).astype(bf16), side, points)
    out_cp = cps.start(hpad, hpad_out)

    rows = [vec_a[j : j + 1, :] for j in range(6)]
    rows += [col_sum(gain), col_sum(shift_g), col_sum(jnp.concatenate(times, axis=0))]
    lane = lax.broadcasted_iota(jnp.int32, (1, LANES), 1)
    stamp = jnp.zeros((1, LANES), f32)
    for b in range(count):
        step = jnp.full((1, LANES), steps_ref[places[0] * count + b], jnp.int32)
        stamp = jnp.where(lane == b, (step >> 5).astype(f32), stamp)
        stamp = jnp.where(lane == LANES // 2 + b, (step & 31).astype(f32), stamp)
    flat = []
    for r in rows + times:
        flat += [r[:, i * LANES : (i + 1) * LANES] for i in range(chans // LANES)]
    flat.append(stamp)
    flat += [jnp.zeros((1, LANES), f32)] * (BLOCK - len(flat))
    block_out[...] = jnp.concatenate(flat, axis=0).astype(bf16)

    a1t_cp.wait()
    a_all = jnp.concatenate([a1t[b] for b in range(count)], axis=1)
    moved = [taps(hpad, b, -1, side, points) for b in range(count)]
    at = 0
    for tap in range(9):
        val = nn(a_all, jnp.concatenate([moved[b][tap] for b in range(count)], axis=0))
        if pieces == 2:
            at = pack_store(own, send, at, val, 1, places)
        else:
            own[tap] = val
    out_cp.wait()


def block_kernel(pieces, count, *refs):
    it = iter(refs)

    def take(n):
        return [next(it) for _ in range(n)]

    po_in, vec_in = (take(pieces) for _ in range(2))
    resid_in, mix_in = take(2)
    own = next(it)
    send = next(it) if pieces == 2 else None
    po, vec, resid, mix = take(4)
    sems = next(it)
    cps = Copies(sems)
    places = places_of(pieces)
    vec_cp = load_split(cps, vec_in, vec, 1, places)
    po_cp = load_split(cps, po_in, po, 0, places)
    mix_cp = cps.start(mix_in, mix)
    resid_cp = cps.start(resid_in, resid)
    wait_all(vec_cp)
    bias = jnp.transpose(vec[...])[:, OUTPUT_BIAS : OUTPUT_BIAS + 1]
    wait_all(po_cp)
    mix_cp.wait()
    resid_cp.wait()
    po_t = jnp.transpose(po[...].astype(f32)).astype(bf16)
    for b in range(count):
        val = jnp.transpose(resid[b]) + nn(po_t, mix[b]) + bias
        split_store(own, send, b, val, 0, places)


def last_kernel(pieces, count, *refs):
    it = iter(refs)

    def take(n):
        return [next(it) for _ in range(n)]

    x_in, w1_in, vec_in = (take(pieces) for _ in range(3))
    hpad_in, gres_in = take(2)
    image_own = next(it)
    image_send = next(it) if pieces == 2 else None
    vec_out = next(it)
    xin, w1, vec, hpad, gres = take(5)
    sems = next(it)
    cps = Copies(sems)
    places = places_of(pieces)
    chans, points = xin.shape[1], xin.shape[2]
    side = side_of(points)
    width = chans // GROUPS
    size = float(width * points)

    vec_cp = load_split(cps, vec_in, vec, 1, places)
    x_cp = load_images(cps, x_in, xin, places, count)
    w1_cp = load_split(cps, w1_in, w1, 2, places)
    hpad_cp = cps.start(hpad_in, hpad)
    gres_cp = cps.start(gres_in, gres)
    wait_all(vec_cp)
    vcols = jnp.transpose(vec[...])

    def col(j):
        return vcols[:, j : j + 1]

    wait_all(x_cp)
    wait_all(w1_cp)
    hpad_cp.wait()
    gres_cp.wait()
    w1_cols = jnp.concatenate([w1[k] for k in range(9)], axis=1)
    zero = jnp.zeros((chans, 1), f32)
    gain_sum, shift_sum = zero, zero

    def groups(v):
        total = jnp.sum(v.reshape(GROUPS, width, 1), axis=1, keepdims=True) / size
        return jnp.broadcast_to(total, (GROUPS, width, 1)).reshape(chans, 1)

    for b in range(count):
        back = nt(w1_cols, jnp.concatenate(taps(hpad, b, -1, side, points), axis=1))
        x3 = xin[b].astype(f32).reshape(GROUPS, width, points)
        mean = jnp.sum(jnp.sum(x3, axis=2, keepdims=True), axis=1, keepdims=True) / size
        off = x3 - mean
        var = jnp.sum(jnp.sum(off * off, axis=2, keepdims=True), axis=1, keepdims=True) / size
        rstd = lax.rsqrt(var + EPS)
        hat = (off * rstd).reshape(chans, points)
        rstd = jnp.broadcast_to(rstd, (GROUPS, width, 1)).reshape(chans, 1)
        pre = hat * col(FIRST_GAIN) + col(FIRST_SHIFT)
        val = back * silu_slope(pre, sigmoid(pre))
        gain = jnp.sum(val * hat, axis=1, keepdims=True)
        shift_g = jnp.sum(val, axis=1, keepdims=True)
        gain_sum = gain_sum + gain
        shift_sum = shift_sum + shift_g
        first_mean = groups(shift_g * col(FIRST_GAIN))
        second_mean = groups(gain * col(FIRST_GAIN))
        val = rstd * (val * col(FIRST_GAIN) - first_mean - hat * second_mean)
        val = val + jnp.transpose(gres[b])
        split_store(image_own, image_send, b, val, 0, places)
    lane = lax.broadcasted_iota(jnp.int32, (chans, 128), 1)
    both = jnp.where(lane == 0, gain_sum, 0.0) + jnp.where(lane == 1, shift_sum, 0.0)
    vec_out[...] = jnp.transpose(both)[0:8]


def swap(value, axis, size, bit):
    return lax.ppermute(value, axis, [(i, i ^ bit) for i in range(size)])


def near_parts(part):
    me = lax.axis_index("batch") & 3
    return [part(me ^ j).astype(bf16) for j in range(1, 4)]


def after(values, *others):
    done = lax.optimization_barrier((tuple(values), others))
    return list(done[0])


def send_near(sent, batch):
    return [swap(v, "batch", batch, j + 1) for j, v in enumerate(sent)]


def sum_near(got, part):
    total = part(lax.axis_index("batch") & 3).astype(f32)
    for g in got:
        total = total + g.astype(f32)
    return total.astype(bf16)


def far_steps(batch):
    return batch.bit_length() - 3


def send_far(piece, extra, step, batch):
    steps = far_steps(batch)
    mine = piece if extra is None else jnp.concatenate([piece, extra], axis=0)
    tensor = lax.axis_size("tensor")
    pairs = []
    for i in range(batch):
        for core in range(tensor):
            bit = 4 << (step if core % 2 == 0 else steps - 1 - step)
            pairs.append((i * tensor + core, (i ^ bit) * tensor + core))
    return lax.ppermute(mine, ("batch", "tensor"), pairs)


def sum_far(piece, extra, got):
    rows = piece.shape[0]
    piece = (piece.astype(f32) + got[:rows].astype(f32)).astype(bf16)
    if extra is not None:
        extra = jnp.concatenate([extra, got[rows:]], axis=0)
    return piece, extra


def gather_near(piece, batch):
    return [piece] + [swap(piece, "batch", batch, j) for j in range(1, 4)]


def in_order(pieces):
    me = lax.axis_index("batch")
    parts = jnp.stack(pieces, axis=0)
    parts = parts.reshape((2, 2) + parts.shape[1:])
    parts = jnp.where((me & 1) == 1, jnp.flip(parts, axis=1), parts)
    parts = jnp.where((me & 2) == 2, jnp.flip(parts, axis=0), parts)
    return parts.reshape((-1, LANES))


def unpack(flat, shapes):
    out = []
    at = 0
    for shape in shapes:
        n = math.prod(shape) // 128
        out.append(flat[at : at + n].reshape(shape).astype(f32))
        at += n
    return out


def per_device(
    batch,
    tensor,
    images,
    timesteps,
    embed_table,
    first_gain,
    first_shift,
    first_conv,
    first_bias,
    time_weight,
    time_bias,
    second_gain,
    second_shift,
    second_conv,
    second_bias,
    third_gain,
    third_shift,
    project_in,
    query_bias,
    value_bias,
    project_out,
    output_bias,
    cotangent,
):
    per_batch, local, points = images.shape
    chans = local * tensor
    count = per_batch // tensor
    steps, embed = embed_table.shape
    pieces = 2 if tensor == 2 else 1
    me = lax.axis_index("tensor")
    vec = jnp.stack(
        [
            first_gain,
            first_shift,
            first_bias,
            time_bias,
            second_gain,
            second_shift,
            second_bias,
            third_gain,
            third_shift,
            query_bias,
            value_bias,
            output_bias,
        ]
        + [output_bias] * 4,
        axis=0,
    )

    def other_half(array):
        parts = array.reshape((2, count) + array.shape[1:])
        return lax.dynamic_index_in_dim(parts, 1 - me, 0, False)

    def images_of(array):
        if pieces == 2:
            return [array, swap(other_half(array), "tensor", 2, 1)]
        return [lax.all_to_all(array, "tensor", 0, 1, tiled=True)]

    def whole(array, axis):
        if pieces == 2:
            return [array, swap(array, "tensor", 2, 1)]
        return [lax.all_gather(array, "tensor", axis=axis, tiled=True)]

    x_in = images_of(images)
    vec_in = whole(vec, 1)
    tw_in = whole(time_weight, 1)
    w1_in = whole(first_conv, 2)
    w2_in = whole(second_conv, 1)
    pi_in = whole(project_in, 2)
    po_in = whole(project_out, 0)
    g_in = images_of(cotangent)
    my_steps = timesteps if pieces == 2 else lax.dynamic_slice_in_dim(timesteps, me * count, count)

    side = side_of(points)
    image_b = (count, chans, points)
    image_p = (count, points, chans)
    pads = (3, count, points + 2 * side, chans)

    def shape(s, d):
        return jax.ShapeDtypeStruct(s, d)

    params = pltpu.CompilerParams(vmem_limit_bytes=VMEM_LIMIT)

    def cost(units, moved):
        flops = 2 * units * count * points * chans * chans
        return pl.CostEstimate(flops=flops, bytes_accessed=moved, transcendentals=0)

    half_b = 9 * chans * chans // 2 // LANES
    half_a = half_b + 4 * chans * chans // 2 // LANES
    if pieces == 2:
        grads_a = [shape((half_a, LANES), bf16)] * 2
        grads_b = [shape((half_b, LANES), bf16)] * 2
    else:
        grads_a = [shape((9, chans, chans), f32), shape((chans, chans), f32)]
        grads_a.append(shape((3, chans, chans), f32))
        grads_b = [shape((9, chans, chans), f32)]
    n_grad = len(grads_a)
    front = pl.pallas_call(
        functools.partial(front_kernel, pieces, count),
        out_shape=grads_a
        + [
            shape((8, chans), f32),
            shape((2, count, chans), f32),
            shape(pads, bf16),
            shape(image_p, f32),
            shape(image_b, bf16),
            shape(image_p, f32),
            shape(image_p, f32),
            shape(image_b, bf16),
        ],
        in_specs=[ANY] * (8 * pieces) + [SMEM, ANY],
        out_specs=[VMEM] * (n_grad + 2) + [ANY] * 6,
        scratch_shapes=[
            pltpu.VMEM(image_b, bf16),
            pltpu.VMEM(image_b, bf16),
            pltpu.VMEM((9, chans, chans), bf16),
            pltpu.VMEM((9, chans, chans), bf16),
            pltpu.VMEM((3, chans, chans), bf16),
            pltpu.VMEM((chans, chans), bf16),
            pltpu.VMEM((embed, chans), bf16),
            pltpu.VMEM((16, chans), f32),
            pltpu.VMEM((count, 16, embed), bf16),
            pltpu.VMEM((3 * points, points), bf16),
            pltpu.VMEM(pads, bf16),
            pltpu.VMEM(pads, bf16),
            pltpu.VMEM(image_p, f32),
            pltpu.VMEM(image_b, bf16),
            pltpu.VMEM(image_p, f32),
            pltpu.VMEM(image_p, f32),
            pltpu.VMEM(image_b, bf16),
            pltpu.VMEM(image_b, bf16),
            pltpu.VMEM(image_b, bf16),
            pltpu.VMEM((count, points, 3 * chans), bf16),
            pltpu.SemaphoreType.DMA((8 * pieces + count + 6,)),
        ],
        compiler_params=params,
        cost_estimate=cost(54, 12 << 20),
        name="front",
    )(*x_in, *g_in, *w1_in, *w2_in, *pi_in, *po_in, *tw_in, *vec_in, my_steps, embed_table)
    sums_a = front[:n_grad]
    vec_a, stat, gpad, sum_one, a1t, resid, gres, mix = front[n_grad:]

    if pieces == 2:
        half = (count, chans // 2, points)
        out_t = [shape(half, f32), shape(half, bf16)]
    else:
        out_t = [shape(image_b, f32)]
    block_part = pl.pallas_call(
        functools.partial(block_kernel, pieces, count),
        out_shape=out_t,
        in_specs=[ANY] * (2 * pieces + 2),
        out_specs=[VMEM] * pieces,
        scratch_shapes=[
            pltpu.VMEM((chans, chans), bf16),
            pltpu.VMEM((16, chans), f32),
            pltpu.VMEM(image_p, f32),
            pltpu.VMEM(image_b, bf16),
            pltpu.SemaphoreType.DMA((2 * pieces + 2,)),
        ],
        compiler_params=params,
        cost_estimate=cost(3, 5 << 20),
        name="block",
    )(*po_in, *vec_in, resid, mix)

    def quarters(sums, axes, beside=None):
        if pieces == 2:
            got = swap(sums[1], "tensor", 2, 1)
            if beside is not None:
                (got,) = after([got], beside)
            rows = got.shape[0] // 4
            own4, got4 = (v.reshape(4, rows, LANES) for v in (sums[0], got))

            def part(q):
                pair = [lax.dynamic_index_in_dim(v, q, 0, False).astype(f32) for v in (own4, got4)]
                return pair[0] + pair[1]

            return part
        done = [
            lax.psum_scatter(v, "tensor", scatter_dimension=axis, tiled=True)
            for v, axis in zip(sums, axes, strict=True)
        ]
        flat = jnp.concatenate([v.reshape(-1, LANES) for v in done], axis=0)
        flat = jnp.pad(flat, ((0, -flat.shape[0] % 64), (0, 0)))
        rows = flat.shape[0] // 4
        flat = flat.reshape(4, rows, LANES)
        return lambda q: lax.dynamic_index_in_dim(flat, q, 0, False)

    part_a = quarters(sums_a, (1, 0, 2), block_part[0])
    sent_a = near_parts(part_a)

    got_a = send_near(sent_a, batch)
    gpad, sum_one = after([gpad, sum_one], *sent_a)

    *sums_b, block, hpad = pl.pallas_call(
        functools.partial(middle_kernel, pieces, count),
        out_shape=grads_b + [shape((BLOCK, LANES), bf16), shape(pads, bf16)],
        in_specs=[ANY] * (2 * pieces + 3) + [VMEM, VMEM, SMEM],
        out_specs=[VMEM] * (pieces + 1) + [ANY],
        scratch_shapes=[
            pltpu.VMEM((9, chans, chans), bf16),
            pltpu.VMEM((16, chans), f32),
            pltpu.VMEM(pads, bf16),
            pltpu.VMEM(image_p, f32),
            pltpu.VMEM(image_b, bf16),
            pltpu.VMEM((3 * points, points), bf16),
            pltpu.VMEM(pads, bf16),
            pltpu.VMEM(image_p, f32),
            pltpu.SemaphoreType.DMA((2 * pieces + 4,)),
        ],
        compiler_params=params,
        cost_estimate=cost(21, 7 << 20),
        name="middle",
    )(*w2_in, *vec_in, gpad, sum_one, a1t, stat, vec_a, my_steps)
    got_a = after(got_a, block)
    sums_b = after(sums_b, *got_a)
    piece_a = sum_near(got_a, part_a)
    part_b = quarters(sums_b, (2,))
    sent_b = near_parts(part_b)
    got_b = send_near(sent_b, batch)
    far_a = send_far(piece_a, block, 0, batch)
    hpad, gres = after([hpad, gres], piece_a, *sent_b)

    image_grad = pl.pallas_call(
        functools.partial(last_kernel, pieces, count),
        out_shape=out_t + [shape((8, chans), f32)],
        in_specs=[ANY] * (3 * pieces + 2),
        out_specs=[VMEM] * (pieces + 1),
        scratch_shapes=[
            pltpu.VMEM(image_b, bf16),
            pltpu.VMEM((9, chans, chans), bf16),
            pltpu.VMEM((16, chans), f32),
            pltpu.VMEM(pads, bf16),
            pltpu.VMEM(image_p, f32),
            pltpu.SemaphoreType.DMA((3 * pieces + 2,)),
        ],
        compiler_params=params,
        cost_estimate=cost(9, 8 << 20),
        name="last",
    )(*x_in, *w1_in, *vec_in, hpad, gres)
    got_b = after(got_b, image_grad[-1])
    *image_grad, far_a = after([*image_grad, far_a], *got_b)
    block_part = after(block_part, image_grad[-1])
    vec_c = image_grad[-1][:2].reshape(-1, LANES)

    def placed(own, send):
        if pieces == 2:
            got = swap(send, "tensor", 2, 1).astype(f32)
            low = jnp.where(me == 0, own, got)
            high = jnp.where(me == 0, got, own)
            return jnp.concatenate([low, high], axis=0)
        return lax.all_to_all(own, "tensor", 1, 0, tiled=True)

    block_out = placed(block_part[0], block_part[-1])
    images_grad = placed(image_grad[0], image_grad[1])

    piece_a, blocks = sum_far(piece_a, block, far_a)
    for step in range(1, far_steps(batch)):
        piece_a, blocks = sum_far(piece_a, blocks, send_far(piece_a, blocks, step, batch))

    piece_b = sum_near(got_b, part_b)
    vec_c = jnp.pad(vec_c, ((0, 16 - vec_c.shape[0]), (0, 0))).astype(bf16)
    piece_b = jnp.concatenate([piece_b, vec_c], axis=0)
    for step in range(far_steps(batch)):
        piece_b, _ = sum_far(piece_b, None, send_far(piece_b, None, step, batch))
    rows_a = piece_a.shape[0]
    got_a = gather_near(jnp.concatenate([piece_a, blocks], axis=0), batch)
    done_a = in_order([g[:rows_a] for g in got_a])
    blocks = jnp.concatenate([g[rows_a:] for g in got_a], axis=0)
    got_b = gather_near(piece_b, batch)
    rows_b = piece_b.shape[0] - 16
    done_b = in_order([g[:rows_b] for g in got_b])
    vec_c = sum(g[rows_b:].astype(f32) for g in got_b)[: 2 * chans // LANES].reshape(2, chans)
    if pieces == 2:
        vec_c = vec_c + swap(vec_c, "tensor", 2, 1)
    else:
        vec_c = lax.psum(vec_c, "tensor")

    half = local
    if pieces == 2:
        n = chans * chans // 2 // LANES
        project_out_grad = done_a[:n].reshape(2, local, LANES)
        project_out_grad = jnp.concatenate([project_out_grad[0], project_out_grad[1]], axis=1)
        project_in_grad = done_a[n : 4 * n].reshape(3, chans, local)
        taps_grad = done_a[4 * n :].reshape(9, 2, local, LANES)
        second_conv_grad = jnp.concatenate([taps_grad[:, 0], taps_grad[:, 1]], axis=2)
        first_conv_grad = done_b.reshape(9, chans, local)
    else:
        second_conv_grad, project_out_grad, project_in_grad = unpack(
            done_a, [(9, half, chans), (half, chans), (3, chans, half)]
        )
        (first_conv_grad,) = unpack(done_b, [(9, chans, half)])

    if pieces == 2:
        blocks = jnp.concatenate([blocks, swap(blocks, "tensor", 2, 1)], axis=0)
        two = blocks.reshape(2, batch, BLOCK, LANES)
        blocks = jnp.where(me == 0, two, jnp.flip(two, axis=0))
    else:
        blocks = lax.all_gather(blocks, "tensor", axis=0, tiled=True)
    blocks = blocks.reshape(batch * tensor, BLOCK, LANES)
    wide = chans // LANES
    n_vec = 9 * wide
    sums = jnp.sum(blocks[:, :n_vec].astype(f32), axis=0).reshape(9, chans)
    sums = jnp.concatenate([sums, vec_c], axis=0)
    mine = lax.dynamic_slice_in_dim(sums, me * local, local, axis=1)
    all_times = blocks[:, n_vec : n_vec + wide * count].reshape(-1, chans)
    stamps = blocks[:, n_vec + wide * count].astype(jnp.int32)
    all_steps = stamps[:, :count] * 32 + stamps[:, LANES // 2 : LANES // 2 + count]
    all_steps = all_steps.reshape(-1)
    one_hot = (all_steps[:, None] == jnp.arange(steps, dtype=jnp.int32)[None, :]).astype(bf16)
    emb = nn(one_hot, embed_table)
    sig = sigmoid(emb)
    act = (emb * sig).astype(bf16)
    my_times = lax.dynamic_slice_in_dim(all_times, me * local, local, axis=1)
    time_weight_grad = lax.dot_general(
        act, my_times, (((0,), (0,)), ((), ())), preferred_element_type=f32
    )
    if pieces == 2:
        tw = jnp.where(
            me == 0, jnp.concatenate(tw_in, axis=1), jnp.concatenate(tw_in[::-1], axis=1)
        )
    else:
        tw = tw_in[0]
    grad_emb = (nt(all_times, tw) * silu_slope(emb, sig)).astype(bf16)
    table_grad = lax.dot_general(
        one_hot, grad_emb, (((0,), (0,)), ((), ())), preferred_element_type=f32
    )
    return (
        block_out,
        images_grad,
        table_grad,
        mine[9],
        mine[10],
        first_conv_grad.astype(f32),
        mine[8],
        time_weight_grad,
        mine[8],
        mine[6],
        mine[7],
        second_conv_grad.astype(f32),
        mine[0],
        mine[1],
        mine[2],
        project_in_grad.astype(f32),
        mine[3],
        mine[4],
        project_out_grad.astype(f32),
        mine[5],
    )


def solution(mesh):
    in_specs = (
        P("batch", "tensor", None),
        P("batch"),
        P(),
        P("tensor"),
        P("tensor"),
        P(None, None, "tensor"),
        P("tensor"),
        P(None, "tensor"),
        P("tensor"),
        P("tensor"),
        P("tensor"),
        P(None, "tensor", None),
        P("tensor"),
        P("tensor"),
        P("tensor"),
        P(None, None, "tensor"),
        P("tensor"),
        P("tensor"),
        P("tensor", None),
        P("tensor"),
        P("batch", "tensor", None),
    )
    out_specs = (
        P("batch", "tensor", None),
        P("batch", "tensor", None),
        P(),
        P("tensor"),
        P("tensor"),
        P(None, None, "tensor"),
        P("tensor"),
        P(None, "tensor"),
        P("tensor"),
        P("tensor"),
        P("tensor"),
        P(None, "tensor", None),
        P("tensor"),
        P("tensor"),
        P("tensor"),
        P(None, None, "tensor"),
        P("tensor"),
        P("tensor"),
        P("tensor", None),
        P("tensor"),
    )
    sizes = dict(mesh.shape)
    return jax.shard_map(
        functools.partial(per_device, sizes["batch"], sizes["tensor"]),
        mesh=mesh,
        in_specs=in_specs,
        out_specs=out_specs,
        check_vma=False,
    )
```

```python
import functools
import math

import jax
import jax.numpy as jnp
from jax import lax
from jax.experimental import pallas as pl
from jax.experimental.pallas import tpu as pltpu
from jax.sharding import PartitionSpec as P

GROUPS = 32
LANES = 128
BLOCK = 32
EPS = 1e-06
MIB = 1024 * 1024
ANY = pl.BlockSpec(memory_space=pl.ANY)
VMEM = pl.BlockSpec(memory_space=pltpu.VMEM)
SMEM = pl.BlockSpec(memory_space=pltpu.SMEM)
f32 = jnp.float32
bf16 = jnp.bfloat16

(
    FIRST_GAIN,
    FIRST_SHIFT,
    FIRST_BIAS,
    TIME_BIAS,
    SECOND_GAIN,
    SECOND_SHIFT,
    SECOND_BIAS,
    THIRD_GAIN,
    THIRD_SHIFT,
    QUERY_BIAS,
    VALUE_BIAS,
    OUTPUT_BIAS,
) = range(12)


def nn(a, b):
    return lax.dot_general(a, b, (((1,), (0,)), ((), ())), preferred_element_type=f32)


def nt(a, b):
    return lax.dot_general(a, b, (((1,), (1,)), ((), ())), preferred_element_type=f32)


def sigmoid(v):
    return 0.5 * jnp.tanh(0.5 * v) + 0.5


def silu_slope(v, sig):
    return sig * (1.0 + v * (1.0 - sig))


def col_sum(v):
    return jnp.sum(v, axis=0, keepdims=True)


def lane_groups(v, width):
    lanes = v.shape[1]
    lane = lax.broadcasted_iota(jnp.int32, v.shape, 1)
    step = 1
    while step < width:
        up = pltpu.roll(v, step, 1)
        down = pltpu.roll(v, lanes - step, 1)
        v = v + jnp.where((lane & step) != 0, up, down)
        step *= 2
    return v


def fill_shift(shift_ref, side):
    points = shift_ref.shape[1]
    to = lax.broadcasted_iota(jnp.int32, (points, points), 0)
    of = lax.broadcasted_iota(jnp.int32, (points, points), 1)
    for d in range(3):
        s = d - 1
        col = (to & (side - 1)) + s
        hit = (of == to + s) & (col >= 0) & (col < side)
        shift_ref[d * points : (d + 1) * points, :] = jnp.where(hit, 1.0, 0.0).astype(bf16)


def zero_pads(pad_ref, side, points):
    images, chans = pad_ref.shape[1], pad_ref.shape[3]
    for d in range(3):
        for b in range(images):
            pad_ref[d, b, 0:side, :] = jnp.zeros((side, chans), bf16)
            pad_ref[d, b, side + points : 2 * side + points, :] = jnp.zeros((side, chans), bf16)


def put_moved(pad_ref, b, value, side, points):
    chans = value.shape[1]
    column = lax.broadcasted_iota(jnp.int32, (side, chans), 0)
    for d, edge in ((0, 0), (1, None), (2, side - 1)):
        moved = value
        if edge is not None:
            moved = pltpu.roll(value, (1 - d) % points, 0).reshape(side, side, chans)
            moved = jnp.where((column == edge)[None], 0.0, moved).reshape(points, chans)
        pad_ref[d, b, side : side + points, :] = moved.astype(bf16)


def put_pads(pad_ref, b, moved, side, points):
    for d in range(3):
        pad_ref[d, b, side : side + points, :] = moved[d * points : (d + 1) * points]


def taps(pad_ref, b, sign, side, points):
    out = []
    for dr in (-1, 0, 1):
        for dc in (-1, 0, 1):
            top = side + sign * dr * side
            out.append(pad_ref[1 + sign * dc, b, top : top + points, :])
    return out


class Copies:
    def __init__(self, sems):
        self.sems = sems
        self.used = 0

    def start(self, src, dst):
        copy = pltpu.make_async_copy(src, dst, self.sems.at[self.used])
        self.used += 1
        copy.start()
        return copy


def wait_all(copies):
    for c in copies:
        c.wait()


def side_of(points):
    return math.isqrt(points)


def load_split(cps, refs, dst, axis, places):
    out = []
    for ref, place in zip(refs, places, strict=True):
        size = ref.shape[axis]
        idx = [slice(None)] * len(ref.shape)
        idx[axis] = pl.ds(pl.multiple_of(place * size, size), size)
        out.append(cps.start(ref, dst.at[tuple(idx)]))
    return out


def load_images(cps, refs, dst, places, count):
    out = []
    for j, (ref, place) in enumerate(zip(refs, places, strict=True)):
        size = ref.shape[1]
        first = pl.multiple_of(places[0] * count, count) if j == 0 else 0
        out.append(
            cps.start(
                ref.at[pl.ds(first, count)],
                dst.at[:, pl.ds(pl.multiple_of(place * size, size), size), :],
            )
        )
    return out


def places_of(pieces):
    if pieces == 1:
        return [0]
    me = lax.axis_index("tensor")
    return [me, 1 - me]


def split_store(own_ref, send_ref, at, value, axis, places):
    if send_ref is None:
        own_ref[at] = value.astype(own_ref.dtype)
        return
    half = value.shape[axis] // 2
    low = lax.slice_in_dim(value, 0, half, axis=axis)
    high = lax.slice_in_dim(value, half, 2 * half, axis=axis)
    first = places[0] == 0
    own_ref[at] = jnp.where(first, low, high).astype(own_ref.dtype)
    send_ref[at] = jnp.where(first, high, low).astype(send_ref.dtype)


def pack_store(own_ref, send_ref, at, value, axis, places):
    half = value.shape[axis] // 2
    low = lax.slice_in_dim(value, 0, half, axis=axis)
    high = lax.slice_in_dim(value, half, 2 * half, axis=axis)
    first = places[0] == 0
    own = jnp.where(first, low, high).astype(own_ref.dtype)
    send = jnp.where(first, high, low).astype(send_ref.dtype)
    rows = own.shape[0]
    for i in range(own.shape[1] // LANES):
        lanes = slice(i * LANES, (i + 1) * LANES)
        own_ref[at : at + rows, :] = own[:, lanes]
        send_ref[at : at + rows, :] = send[:, lanes]
        at += rows
    return at


def pack_kernel(n_vec, *refs):
    vectors, arrays = refs[:n_vec], refs[n_vec : n_vec + 2]
    vec, x_half, g_half, sems = refs[n_vec + 2 :]
    cps = Copies(sems)
    count = x_half.shape[0]
    first = pl.multiple_of((1 - lax.axis_index("tensor")) * count, count)
    copies = [
        cps.start(src.at[pl.ds(first, count)], dst)
        for src, dst in zip(arrays, (x_half, g_half), strict=True)
    ]
    copies += [cps.start(v, vec.at[j]) for j, v in enumerate(vectors)]
    vec[n_vec:, :] = jnp.zeros((16 - n_vec, vec.shape[1]), f32)
    wait_all(copies)


def part(value, b, points):
    return value[b * points : (b + 1) * points]


def lane_part(value, b, points):
    return value[:, b * points : (b + 1) * points]


def norm_first(x, size, width):
    x3 = x.astype(f32).reshape(GROUPS, width, x.shape[1])
    mean = jnp.sum(jnp.sum(x3, axis=2, keepdims=True), axis=1, keepdims=True) / size
    off = x3 - mean
    var = jnp.sum(jnp.sum(off * off, axis=2, keepdims=True), axis=1, keepdims=True) / size
    rstd = lax.rsqrt(var + EPS)
    return (off * rstd).reshape(x.shape), rstd


def moments(value, width, size):
    mean = lane_groups(col_sum(value), width) / size
    off = value - mean
    return mean, lax.rsqrt(lane_groups(col_sum(off * off), width) / size + EPS)


def pipelined(stages, count):
    for t in range(count + len(stages) - 1):
        for i in reversed(range(len(stages))):
            if 0 <= t - i < count:
                stages[i](t - i)


def front_kernel(pieces, count, *refs):
    it = iter(refs)

    def take(n):
        return [next(it) for _ in range(n)]

    x_in, g_in, w1_in, w2_in, pi_in, po_in, tw_in, vec_in = (take(pieces) for _ in range(8))
    steps_ref, table_ref = take(2)
    if pieces == 2:
        own_out, send_out = take(2)
    else:
        dw2_own, dpo_own, dpi_own = take(3)
    vec_out, stat_out = take(2)
    w1_out, w2_out, po_out, all_vec_out, x_out = take(5)
    gpad_out, sum_out, a1t_out, resid_out, gres_out, mix_out = take(6)
    if pieces == 2:
        own, send = take(2)
    w1, w2, po, vec, xin = take(5)
    gpad, sum_one, a1t, resid, gres, mix = take(6)
    gin, pi, tw, rows, shift, apad, bpad = take(7)
    sems = next(it)

    cps = Copies(sems)
    places = places_of(pieces)
    chans, points = xin.shape[1], xin.shape[2]
    side = side_of(points)
    width = chans // GROUPS
    size = float(width * points)
    scale = chans ** (-0.5)
    images = range(count)

    x_cp = load_images(cps, x_in, xin, places, count)
    vec_cp = load_split(cps, vec_in, vec, 1, places)
    w1_cp = load_split(cps, w1_in, w1, 2, places)
    row_cp = []
    for b in images:
        step = steps_ref[places[0] * count + b]
        row_cp.append(
            cps.start(table_ref.at[pl.ds(pl.multiple_of(step // 16 * 16, 16), 16), :], rows.at[b])
        )
    tw_cp = load_split(cps, tw_in, tw, 1, places)
    w2_cp = load_split(cps, w2_in, w2, 1, places)
    pi_cp = load_split(cps, pi_in, pi, 2, places)
    po_cp = load_split(cps, po_in, po, 0, places)
    g_cp = load_images(cps, g_in, gin, places, count)

    fill_shift(shift, side)
    zero_pads(apad, side, points)
    zero_pads(bpad, side, points)
    zero_pads(gpad, side, points)
    eye = shift[points : 2 * points, :]

    wait_all(vec_cp)
    vcols = jnp.transpose(vec[...])

    def col(j):
        return vcols[:, j : j + 1]

    def row(j):
        return vec[j : j + 1, :]

    wait_all(x_cp)
    wait_all(row_cp)
    wait_all(tw_cp)
    wait_all(w1_cp)
    outs = [cps.start(vec, all_vec_out), cps.start(xin, x_out), cps.start(w1, w1_out)]
    picked = []
    for b in images:
        step = steps_ref[places[0] * count + b]
        r = lax.broadcasted_iota(jnp.int32, (16, rows.shape[2]), 0)
        picked.append(col_sum(jnp.where(r == lax.rem(step, 16), rows[b].astype(f32), 0.0)))
    emb = jnp.concatenate(picked + picked[:1] * (8 - count), axis=0)
    time_add = nn((emb * sigmoid(emb)).astype(bf16), tw[...]) + row(TIME_BIAS) + row(FIRST_BIAS)

    stats2, stats3 = [], []
    act_t = [None] * count

    def norm_one(b):
        hat, _ = norm_first(xin[b], size, width)
        pre = hat * col(FIRST_GAIN) + col(FIRST_SHIFT)
        act = (pre * sigmoid(pre)).astype(bf16)
        a1t[b] = act
        put_pads(apad, b, nt(shift[...], act).astype(bf16), side, points)

    def conv_one(b):
        lhs = jnp.concatenate(taps(apad, b, 1, side, points), axis=1)
        sum_one[b] = nn(lhs, w1[...].reshape(9 * chans, chans)) + time_add[b : b + 1]

    def norm_two(b):
        mean, rstd = moments(sum_one[b], width, size)
        stats2.append((mean, rstd))
        hat = (sum_one[b] - mean) * rstd
        pre = hat * row(SECOND_GAIN) + row(SECOND_SHIFT)
        act = pre * sigmoid(pre)
        act_t[b] = jnp.transpose(act.astype(bf16))
        put_moved(bpad, b, act, side, points)

    def conv_two(b):
        if b == 0:
            wait_all(w2_cp)
        lhs = jnp.concatenate(taps(bpad, b, 1, side, points), axis=1)
        val = nn(lhs, w2[...].reshape(9 * chans, chans)) + row(SECOND_BIAS)
        resid[b] = val + nt(eye, xin[b])

    normed = []

    def norm_three(b):
        mean, rstd = moments(resid[b], width, size)
        stats3.append((mean, rstd))
        hat = (resid[b] - mean) * rstd
        normed.append((hat * row(THIRD_GAIN) + row(THIRD_SHIFT)).astype(bf16))

    pipelined([norm_one, conv_one, norm_two, conv_two, norm_three], count)
    outs += [cps.start(a1t, a1t_out), cps.start(sum_one, sum_out), cps.start(resid, resid_out)]
    stat_out[0, 0:count, :] = jnp.concatenate([m for m, _ in stats2], axis=0)
    stat_out[1, 0:count, :] = jnp.concatenate([r for _, r in stats2], axis=0)

    wait_all(pi_cp)
    wait_all(po_cp)
    wait_all(g_cp)
    outs += [cps.start(w2, w2_out), cps.start(po, po_out)]
    pi_row = jnp.concatenate([pi[0], pi[1], pi[2]], axis=1)
    pi_t = jnp.concatenate([jnp.transpose(pi[1]), jnp.transpose(pi[2])], axis=0)
    zero = jnp.zeros((1, chans), f32)
    normed_t = jnp.concatenate([jnp.transpose(v) for v in normed], axis=1)
    normed = jnp.concatenate(normed, axis=0)
    lin = nn(normed, pi_row)
    q = (lin[:, :chans] + row(QUERY_BIAS)).astype(bf16)
    k = lin[:, chans : 2 * chans].astype(bf16)
    v = (lin[:, 2 * chans :] + row(VALUE_BIAS)).astype(bf16)
    lin_t = nn(pi_t, normed_t)
    kt = lin_t[:chans].astype(bf16)
    vt = (lin_t[chans:] + col(VALUE_BIAS)).astype(bf16)
    grad_all = jnp.concatenate([gin[b] for b in images], axis=1)
    grad_mixed = nn(po[...], grad_all).astype(bf16)
    scores = [nt(part(k, b, points), part(q, b, points)) for b in images]
    grad_w = [nn(part(v, b, points), lane_part(grad_mixed, b, points)) for b in images]
    weights, grad_s = [], []
    for b in images:
        top = scores[b] * scale
        expo = jnp.exp(top - jnp.max(top, axis=0, keepdims=True))
        probs = expo * (1.0 / jnp.sum(expo, axis=0, keepdims=True))
        weights.append(probs.astype(bf16))
        inner = probs * grad_w[b]
        grad_s.append((inner - probs * jnp.sum(inner, axis=0, keepdims=True)).astype(bf16))
    mixed = []
    for b in images:
        mixed.append(nn(lane_part(vt, b, points), weights[b]).astype(bf16))
        mix[b] = mixed[b]
    outs.append(cps.start(mix, mix_out))
    grad_qt = [nn(lane_part(kt, b, points), grad_s[b]) * scale for b in images]
    grad_q = [jnp.transpose(t.astype(bf16)) for t in grad_qt]
    grad_k = [(nn(grad_s[b], part(q, b, points)) * scale).astype(bf16) for b in images]
    grad_v = [nt(weights[b], lane_part(grad_mixed, b, points)).astype(bf16) for b in images]
    lin_grad = jnp.concatenate(
        [jnp.concatenate([grad_q[b], grad_k[b], grad_v[b]], axis=1) for b in images], axis=0
    )
    qb_grad = col_sum(sum(t.astype(f32) for t in grad_q))
    vb_grad = col_sum(sum(t.astype(f32) for t in grad_v))
    dpo = nt(jnp.concatenate(mixed, axis=1), grad_all)
    grad_normed = nt(lin_grad, pi_row)

    gain3, shift3, means = [], [], []
    for b in images:
        hat = (resid[b] - stats3[b][0]) * stats3[b][1]
        val = part(grad_normed, b, points)
        gain3.append(col_sum(val * hat))
        shift3.append(col_sum(val))
        both = jnp.concatenate([shift3[b], gain3[b]], axis=0) * row(THIRD_GAIN)
        means.append(lane_groups(both, width) / size)
    sb_grad, ob_grad = zero, zero
    for b in images:
        hat = (resid[b] - stats3[b][0]) * stats3[b][1]
        h = part(grad_normed, b, points) * row(THIRD_GAIN)
        grad_out = nt(eye, gin[b])
        ob_grad = ob_grad + col_sum(grad_out)
        val = grad_out + stats3[b][1] * (h - means[b][0:1] - hat * means[b][1:2])
        gres[b] = val
        sb_grad = sb_grad + col_sum(val)
        put_moved(gpad, b, val, side, points)
    outs += [cps.start(gres, gres_out), cps.start(gpad, gpad_out)]

    dpi = nn(normed_t, lin_grad)
    at = 0
    if pieces == 2:
        at = pack_store(own, send, at, dpo, 0, places)
        for j in range(3):
            at = pack_store(own, send, at, dpi[:, j * chans : (j + 1) * chans], 1, places)
        outs += copy_rows(cps, [(send, send_out), (own, own_out)], 0, at)
    else:
        dpo_own[...] = dpo
        for j in range(3):
            dpi_own[j] = dpi[:, j * chans : (j + 1) * chans]

    a_all = jnp.concatenate(act_t, axis=1)
    moved = [taps(gpad, b, -1, side, points) for b in images]
    for tap in range(9):
        val = nn(a_all, jnp.concatenate([moved[b][tap] for b in images], axis=0))
        if pieces == 2:
            start = at if tap % 3 == 0 else start
            at = pack_store(own, send, at, val, 0, places)
            if tap % 3 == 2:
                outs += copy_rows(cps, [(send, send_out), (own, own_out)], start, at)
        else:
            dw2_own[tap] = val

    gain3 = jnp.concatenate(gain3, axis=0)
    shift3 = jnp.concatenate(shift3, axis=0)
    vec_out[...] = jnp.concatenate(
        [sb_grad, col_sum(gain3), col_sum(shift3), qb_grad, vb_grad, ob_grad, zero, zero], axis=0
    )
    wait_all(outs)


def copy_rows(cps, pairs, start, end):
    rows = slice(start, end)
    return [cps.start(src.at[rows], dst.at[rows]) for src, dst in pairs]


def back_kernel(pieces, count, *refs):
    it = iter(refs)

    def take(n):
        return [next(it) for _ in range(n)]

    kept = take(11)
    stat, vec_a, steps_ref = take(3)
    if pieces == 2:
        own_out, send_out, block_own_out, block_send_out, image_own_out, image_send_out = take(6)
    else:
        own, block_own_out, image_own_out = take(3)
        block_send_out = image_send_out = None
    small_out = next(it)
    w1, w2, po, vec, xin, gpad, sum_one, a1t, resid, gres, mix = take(11)
    if pieces == 2:
        own, send, block_own, block_send, image_own, image_send = take(6)
    else:
        block_own, image_own = take(2)
        block_send = image_send = None
    hpad, back, sems = take(3)
    cps = Copies(sems)
    places = places_of(pieces)
    points, chans = sum_one.shape[1], sum_one.shape[2]
    side = side_of(points)
    width = chans // GROUPS
    size = float(width * points)
    images = range(count)

    w1_in, w2_in, po_in, vec_in, x_in, gpad_in, sum_in, a1t_in, resid_in, gres_in, mix_in = kept
    w2_cp = cps.start(w2_in, w2)
    gpad_cp = [cps.start(gpad_in.at[:, b], gpad.at[:, b]) for b in images]
    vec_cp = cps.start(vec_in, vec)
    sum_cp = cps.start(sum_in, sum_one)
    a1t_cp = cps.start(a1t_in, a1t)
    later = [(w1_in, w1), (po_in, po), (x_in, xin), (resid_in, resid), (gres_in, gres), (mix_in, mix)]
    later = [cps.start(src, dst) for src, dst in later]

    def row(j):
        return vec[j : j + 1, :]

    zero_pads(hpad, side, points)
    w2_cp.wait()
    w2_cols = jnp.concatenate([w2[k] for k in range(9)], axis=1)
    gain, shift_g, times = [], [], []

    def conv_back(b):
        gpad_cp[b].wait()
        back[b] = nt(jnp.concatenate(taps(gpad, b, -1, side, points), axis=1), w2_cols)

    def norm_back(b):
        if b == 0:
            sum_cp.wait()
            vec_cp.wait()
        mean, rstd = stat[0, b : b + 1, :], stat[1, b : b + 1, :]
        hat = (sum_one[b] - mean) * rstd
        pre = hat * row(SECOND_GAIN) + row(SECOND_SHIFT)
        val = back[b] * silu_slope(pre, sigmoid(pre))
        gain.append(col_sum(val * hat))
        shift_g.append(col_sum(val))
        both = jnp.concatenate([shift_g[b], gain[b]], axis=0) * row(SECOND_GAIN)
        both = lane_groups(both, width) / size
        val = rstd * (val * row(SECOND_GAIN) - both[0:1] - hat * both[1:2])
        times.append(col_sum(val))
        put_moved(hpad, b, val, side, points)

    pipelined([conv_back, norm_back], count)

    a1t_cp.wait()
    a_all = jnp.concatenate([a1t[b] for b in images], axis=1)
    moved = [taps(hpad, b, -1, side, points) for b in images]
    at = 0
    outs = []
    for tap in range(9):
        val = nn(a_all, jnp.concatenate([moved[b][tap] for b in images], axis=0))
        if pieces == 2:
            start = at if tap % 3 == 0 else start
            at = pack_store(own, send, at, val, 1, places)
            if tap % 3 == 2:
                outs += copy_rows(cps, [(send, send_out), (own, own_out)], start, at)
        else:
            own[tap] = val

    wait_all(later)
    vcols = jnp.transpose(vec[...])

    def col(j):
        return vcols[:, j : j + 1]

    def put_out(own_ref, send_ref, own_dst, send_dst, b, val):
        split_store(own_ref, send_ref, b, val, 0, places)
        outs.append(cps.start(own_ref.at[b], own_dst.at[b]))
        if send_ref is not None:
            outs.append(cps.start(send_ref.at[b], send_dst.at[b]))

    proj = nn(jnp.transpose(po[...]), jnp.concatenate([mix[b] for b in images], axis=1))

    w1_cols = jnp.concatenate([w1[k] for k in range(9)], axis=1)
    zero = jnp.zeros((chans, 1), f32)
    gain_sum, shift_sum = [zero], [zero]
    first_back = [None] * count

    def groups(v):
        total = jnp.sum(v.reshape(GROUPS, width, 1), axis=1, keepdims=True) / size
        return jnp.broadcast_to(total, (GROUPS, width, 1)).reshape(chans, 1)

    def conv_first(b):
        first_back[b] = nt(w1_cols, jnp.concatenate(taps(hpad, b, -1, side, points), axis=1))

    def block_part(b):
        val = jnp.transpose(resid[b]) + lane_part(proj, b, points) + col(OUTPUT_BIAS)
        put_out(block_own, block_send, block_own_out, block_send_out, b, val)

    def norm_first_back(b):
        hat, rstd = norm_first(xin[b], size, width)
        rstd = jnp.broadcast_to(rstd, (GROUPS, width, 1)).reshape(chans, 1)
        pre = hat * col(FIRST_GAIN) + col(FIRST_SHIFT)
        val = first_back[b] * silu_slope(pre, sigmoid(pre))
        gain = jnp.sum(val * hat, axis=1, keepdims=True)
        shift = jnp.sum(val, axis=1, keepdims=True)
        gain_sum[0] = gain_sum[0] + gain
        shift_sum[0] = shift_sum[0] + shift
        first_mean = groups(shift * col(FIRST_GAIN))
        second_mean = groups(gain * col(FIRST_GAIN))
        val = rstd * (val * col(FIRST_GAIN) - first_mean - hat * second_mean)
        val = val + jnp.transpose(gres[b])
        put_out(image_own, image_send, image_own_out, image_send_out, b, val)

    pipelined([conv_first, block_part, norm_first_back], count)

    lane = lax.broadcasted_iota(jnp.int32, (chans, LANES), 1)
    both = jnp.where(lane == 0, gain_sum[0], 0.0) + jnp.where(lane == 1, shift_sum[0], 0.0)
    both = jnp.transpose(both)
    rows = [vec_a[j : j + 1, :] for j in range(6)]
    rows += [sum(gain), sum(shift_g), sum(times), both[0:1], both[1:2]]
    lane = lax.broadcasted_iota(jnp.int32, (1, LANES), 1)
    stamp = jnp.zeros((1, LANES), f32)
    for b in images:
        step = jnp.full((1, LANES), steps_ref[places[0] * count + b], jnp.int32)
        stamp = jnp.where(lane == b, (step >> 5).astype(f32), stamp)
        stamp = jnp.where(lane == LANES // 2 + b, (step & 31).astype(f32), stamp)
    flat = []
    for r in rows + times:
        flat += [r[:, i * LANES : (i + 1) * LANES] for i in range(chans // LANES)]
    flat.append(stamp)
    flat += [jnp.zeros((1, LANES), f32)] * (BLOCK - len(flat))
    small_out[...] = jnp.concatenate(flat, axis=0).astype(bf16)
    wait_all(outs)


def swap(value, axis, size, bit):
    return lax.ppermute(value, axis, [(i, i ^ bit) for i in range(size)])


def near_parts(part):
    me = lax.axis_index("batch") & 3
    return [part(me ^ j).astype(bf16) for j in range(1, 4)]


def after(values, *others):
    done = lax.optimization_barrier((tuple(values), others))
    return list(done[0])


def send_near(sent, batch):
    return [swap(v, "batch", batch, j + 1) for j, v in enumerate(sent)]


def sum_near(got, part):
    total = part(lax.axis_index("batch") & 3).astype(f32)
    for g in got:
        total = total + g.astype(f32)
    return total.astype(bf16)


def far_steps(batch):
    return batch.bit_length() - 3


def send_far(piece, extra, step, batch):
    steps = far_steps(batch)
    mine = piece if extra is None else jnp.concatenate([piece, extra], axis=0)
    tensor = lax.axis_size("tensor")
    pairs = []
    for i in range(batch):
        for core in range(tensor):
            bit = 4 << (step if core % 2 == 0 else steps - 1 - step)
            pairs.append((i * tensor + core, (i ^ bit) * tensor + core))
    return lax.ppermute(mine, ("batch", "tensor"), pairs)


def sum_far(piece, extra, got):
    rows = piece.shape[0]
    piece = (piece.astype(f32) + got[:rows].astype(f32)).astype(bf16)
    if extra is not None:
        extra = jnp.concatenate([extra, got[rows:]], axis=0)
    return piece, extra


def gather_near(piece, batch):
    return [piece] + [swap(piece, "batch", batch, j) for j in range(1, 4)]


def in_order(pieces):
    me = lax.axis_index("batch")
    parts = jnp.stack(pieces, axis=0)
    parts = parts.reshape((2, 2) + parts.shape[1:])
    parts = jnp.where((me & 1) == 1, jnp.flip(parts, axis=1), parts)
    parts = jnp.where((me & 2) == 2, jnp.flip(parts, axis=0), parts)
    return parts.reshape((-1, LANES))


def unpack(flat, shapes):
    out = []
    at = 0
    for shape in shapes:
        n = math.prod(shape) // 128
        out.append(flat[at : at + n].reshape(shape).astype(f32))
        at += n
    return out


def per_device(
    batch,
    tensor,
    images,
    timesteps,
    embed_table,
    first_gain,
    first_shift,
    first_conv,
    first_bias,
    time_weight,
    time_bias,
    second_gain,
    second_shift,
    second_conv,
    second_bias,
    third_gain,
    third_shift,
    project_in,
    query_bias,
    value_bias,
    project_out,
    output_bias,
    cotangent,
):
    per_batch, local, points = images.shape
    chans = local * tensor
    count = per_batch // tensor
    steps, embed = embed_table.shape
    pieces = 2 if tensor == 2 else 1
    me = lax.axis_index("tensor")
    vectors = [
        first_gain,
        first_shift,
        first_bias,
        time_bias,
        second_gain,
        second_shift,
        second_bias,
        third_gain,
        third_shift,
        query_bias,
        value_bias,
        output_bias,
    ]
    def in_hbm(array):
        return pltpu.with_memory_space_constraint(array, pltpu.HBM)

    n_vec = len(vectors)
    if pieces == 2:
        half = (count, local, points)
        vec, x_half, g_half = pl.pallas_call(
            functools.partial(pack_kernel, n_vec),
            out_shape=[
                jax.ShapeDtypeStruct((16, local), f32),
                jax.ShapeDtypeStruct(half, bf16),
                jax.ShapeDtypeStruct(half, bf16),
            ],
            in_specs=[ANY] * (n_vec + 2),
            out_specs=[VMEM] * 3,
            scratch_shapes=[pltpu.SemaphoreType.DMA((n_vec + 2,))],
            compiler_params=pltpu.CompilerParams(vmem_limit_bytes=4 * MIB),
            name="pack",
        )(*(in_hbm(v) for v in vectors + [images, cotangent]))
    else:
        vec = jnp.stack(vectors + [output_bias] * 4, axis=0)
        x_half = g_half = None

    def images_of(array, half):
        if pieces == 2:
            return [array, swap(half, "tensor", 2, 1)]
        return [lax.all_to_all(array, "tensor", 0, 1, tiled=True)]

    def whole(array, axis):
        if pieces == 2:
            return [array, swap(array, "tensor", 2, 1)]
        return [lax.all_gather(array, "tensor", axis=axis, tiled=True)]

    x_in = images_of(images, x_half)
    vec_in = whole(vec, 1)
    tw_in = whole(time_weight, 1)
    w1_in = whole(first_conv, 2)
    w2_in = whole(second_conv, 1)
    pi_in = whole(project_in, 2)
    po_in = whole(project_out, 0)
    g_in = images_of(cotangent, g_half)
    my_steps = timesteps if pieces == 2 else lax.dynamic_slice_in_dim(timesteps, me * count, count)

    side = side_of(points)
    image_b = (count, chans, points)
    image_p = (count, points, chans)
    pads = (3, count, points + 2 * side, chans)

    def shape(s, d):
        return jax.ShapeDtypeStruct(s, d)

    def params(mib):
        return pltpu.CompilerParams(vmem_limit_bytes=mib * MIB)

    def cost(units, moved):
        flops = 2 * units * count * points * chans * chans
        return pl.CostEstimate(flops=flops, bytes_accessed=moved, transcendentals=0)

    half_b = 9 * chans * chans // 2 // LANES
    half_a = half_b + 4 * chans * chans // 2 // LANES
    if pieces == 2:
        grads_a = [pltpu.HBM((half_a, LANES), bf16)] * 2
        grads_b = [pltpu.HBM((half_b, LANES), bf16)] * 2
    else:
        grads_a = [shape((9, chans, chans), f32), shape((chans, chans), f32)]
        grads_a.append(shape((3, chans, chans), f32))
        grads_b = [shape((9, chans, chans), f32)]
    n_grad = len(grads_a)
    steps_in = in_hbm(my_steps)
    kept = [
        ((9, chans, chans), bf16),
        ((9, chans, chans), bf16),
        ((chans, chans), bf16),
        ((16, chans), f32),
        (image_b, bf16),
        (pads, bf16),
        (image_p, f32),
        (image_b, bf16),
        (image_p, f32),
        (image_p, f32),
        (image_b, bf16),
    ]
    out_a = ANY if pieces == 2 else VMEM
    scratch_a = [pltpu.VMEM(v.shape, v.dtype) for v in grads_a] if pieces == 2 else []

    front = pl.pallas_call(
        functools.partial(front_kernel, pieces, count),
        out_shape=grads_a
        + [shape((8, chans), f32), shape((2, count, chans), f32)]
        + [pltpu.HBM(*v) for v in kept],
        in_specs=[ANY] * (8 * pieces) + [SMEM, ANY],
        out_specs=[out_a] * n_grad + [VMEM] * 2 + [ANY] * len(kept),
        scratch_shapes=scratch_a
        + [pltpu.VMEM(*v) for v in kept]
        + [
            pltpu.VMEM(image_b, bf16),
            pltpu.VMEM((3, chans, chans), bf16),
            pltpu.VMEM((embed, chans), bf16),
            pltpu.VMEM((count, 16, embed), bf16),
            pltpu.VMEM((3 * points, points), bf16),
            pltpu.VMEM(pads, bf16),
            pltpu.VMEM(pads, bf16),
            pltpu.SemaphoreType.DMA((8 * pieces + count + 19,)),
        ],
        compiler_params=params(32),
        cost_estimate=cost(54, 12 << 20),
        name="front",
    )(
        *(in_hbm(v) for v in x_in + g_in + w1_in + w2_in + pi_in + po_in + tw_in + vec_in),
        steps_in,
        in_hbm(embed_table),
    )
    sums_a = front[:n_grad]
    vec_a, stat, w1, w2, po, vec, xin = front[n_grad : n_grad + 7]
    gpad, sum_one, a1t, resid, gres, mix = front[n_grad + 7 :]

    def quarters(sums, axes):
        if pieces == 2:
            got = swap(sums[1], "tensor", 2, 1)
            rows = got.shape[0] // 4
            own4, got4 = (v.reshape(4, rows, LANES) for v in (sums[0], got))

            def part(q):
                pair = [lax.dynamic_index_in_dim(v, q, 0, False).astype(f32) for v in (own4, got4)]
                return pair[0] + pair[1]

            return part
        done = [
            lax.psum_scatter(v, "tensor", scatter_dimension=axis, tiled=True)
            for v, axis in zip(sums, axes, strict=True)
        ]
        flat = jnp.concatenate([v.reshape(-1, LANES) for v in done], axis=0)
        flat = jnp.pad(flat, ((0, -flat.shape[0] % 64), (0, 0)))
        rows = flat.shape[0] // 4
        flat = flat.reshape(4, rows, LANES)
        return lambda q: lax.dynamic_index_in_dim(flat, q, 0, False)

    part_a = quarters(sums_a, (1, 0, 2))
    sent_a = near_parts(part_a)

    got_a = send_near(sent_a, batch)
    (vec_a,) = after([vec_a], *sent_a)

    half = (count, chans // 2, points)
    if pieces == 2:
        outs_b = grads_b + [pltpu.HBM(half, f32), pltpu.HBM(half, bf16)] * 2
        scratch_b = [pltpu.VMEM(v.shape, v.dtype) for v in outs_b]
    else:
        outs_b = grads_b + [pltpu.HBM(image_b, f32)] * 2
        scratch_b = [pltpu.VMEM(image_b, f32)] * 2
    *outs_b, block = pl.pallas_call(
        functools.partial(back_kernel, pieces, count),
        out_shape=outs_b + [shape((BLOCK, LANES), bf16)],
        in_specs=[ANY] * len(kept) + [VMEM] * 2 + [SMEM],
        out_specs=[out_a] * pieces + [ANY] * (2 * pieces) + [VMEM],
        scratch_shapes=[pltpu.VMEM(*v) for v in kept]
        + scratch_b
        + [
            pltpu.VMEM(pads, bf16),
            pltpu.VMEM(image_p, f32),
            pltpu.SemaphoreType.DMA((6 + 5 * count + 10,)),
        ],
        compiler_params=params(36),
        cost_estimate=cost(33, 12 << 20),
        name="back",
    )(
        *(in_hbm(v) for v in (w1, w2, po, vec, xin, gpad, sum_one, a1t, resid, gres, mix)),
        stat,
        vec_a,
        steps_in,
    )
    sums_b, block_part, image_grad = outs_b[:pieces], outs_b[pieces : 2 * pieces], outs_b[2 * pieces :]
    got_a = after(got_a, block)
    sums_b = after(sums_b, *got_a)
    piece_a = sum_near(got_a, part_a)
    part_b = quarters(sums_b, (2,))
    sent_b = near_parts(part_b)
    got_b = send_near(sent_b, batch)
    (piece_a,) = after([piece_a], *sent_b)
    blocks = block
    for step in range(far_steps(batch)):
        piece_a, blocks = sum_far(piece_a, blocks, send_far(piece_a, blocks, step, batch))

    def placed(own, send):
        if pieces == 2:
            got = swap(send, "tensor", 2, 1).astype(f32)
            low = jnp.where(me == 0, own, got)
            high = jnp.where(me == 0, got, own)
            return jnp.concatenate([low, high], axis=0)
        return lax.all_to_all(own, "tensor", 1, 0, tiled=True)

    block_out = placed(block_part[0], block_part[-1])
    images_grad = placed(image_grad[0], image_grad[-1])

    piece_b = sum_near(got_b, part_b)
    for step in range(far_steps(batch)):
        piece_b, _ = sum_far(piece_b, None, send_far(piece_b, None, step, batch))
    rows_a = piece_a.shape[0]
    got_a = gather_near(jnp.concatenate([piece_a, blocks], axis=0), batch)
    got_a = after(got_a, piece_b)
    done_a = in_order([g[:rows_a] for g in got_a])
    blocks = jnp.concatenate([g[rows_a:] for g in got_a], axis=0)
    (piece_b,) = after([piece_b], *got_a)
    done_b = in_order(gather_near(piece_b, batch))

    if pieces == 2:
        n = chans * chans // 2 // LANES
        project_out_grad = done_a[:n].reshape(2, local, LANES)
        project_out_grad = jnp.concatenate([project_out_grad[0], project_out_grad[1]], axis=1)
        project_in_grad = done_a[n : 4 * n].reshape(3, chans, local)
        taps_grad = done_a[4 * n :].reshape(9, 2, local, LANES)
        second_conv_grad = jnp.concatenate([taps_grad[:, 0], taps_grad[:, 1]], axis=2)
        first_conv_grad = done_b.reshape(9, chans, local)
    else:
        second_conv_grad, project_out_grad, project_in_grad = unpack(
            done_a, [(9, local, chans), (local, chans), (3, chans, local)]
        )
        (first_conv_grad,) = unpack(done_b, [(9, chans, local)])

    if pieces == 2:
        blocks = jnp.concatenate([blocks, swap(blocks, "tensor", 2, 1)], axis=0)
        two = blocks.reshape(2, batch, BLOCK, LANES)
        blocks = jnp.where(me == 0, two, jnp.flip(two, axis=0))
    else:
        blocks = lax.all_gather(blocks, "tensor", axis=0, tiled=True)
    blocks = blocks.reshape(batch * tensor, BLOCK, LANES)
    wide = chans // LANES
    n_sum = 11 * wide
    sums = jnp.sum(blocks[:, :n_sum].astype(f32), axis=0).reshape(11, chans)
    mine = lax.dynamic_slice_in_dim(sums, me * local, local, axis=1)
    all_times = blocks[:, n_sum : n_sum + wide * count].reshape(-1, chans)
    stamps = blocks[:, n_sum + wide * count].astype(jnp.int32)
    all_steps = stamps[:, :count] * 32 + stamps[:, LANES // 2 : LANES // 2 + count]
    all_steps = all_steps.reshape(-1)
    one_hot = (all_steps[:, None] == jnp.arange(steps, dtype=jnp.int32)[None, :]).astype(bf16)
    emb = nn(one_hot, embed_table)
    sig = sigmoid(emb)
    act = (emb * sig).astype(bf16)
    my_times = lax.dynamic_slice_in_dim(all_times, me * local, local, axis=1)
    time_weight_grad = lax.dot_general(
        act, my_times, (((0,), (0,)), ((), ())), preferred_element_type=f32
    )
    if pieces == 2:
        tw = jnp.where(
            me == 0, jnp.concatenate(tw_in, axis=1), jnp.concatenate(tw_in[::-1], axis=1)
        )
    else:
        tw = tw_in[0]
    grad_emb = (nt(all_times, tw) * silu_slope(emb, sig)).astype(bf16)
    table_grad = lax.dot_general(
        one_hot, grad_emb, (((0,), (0,)), ((), ())), preferred_element_type=f32
    )
    return (
        block_out,
        images_grad,
        table_grad,
        mine[9],
        mine[10],
        first_conv_grad.astype(f32),
        mine[8],
        time_weight_grad,
        mine[8],
        mine[6],
        mine[7],
        second_conv_grad.astype(f32),
        mine[0],
        mine[1],
        mine[2],
        project_in_grad.astype(f32),
        mine[3],
        mine[4],
        project_out_grad.astype(f32),
        mine[5],
    )


def solution(mesh):
    in_specs = (
        P("batch", "tensor", None),
        P("batch"),
        P(),
        P("tensor"),
        P("tensor"),
        P(None, None, "tensor"),
        P("tensor"),
        P(None, "tensor"),
        P("tensor"),
        P("tensor"),
        P("tensor"),
        P(None, "tensor", None),
        P("tensor"),
        P("tensor"),
        P("tensor"),
        P(None, None, "tensor"),
        P("tensor"),
        P("tensor"),
        P("tensor", None),
        P("tensor"),
        P("batch", "tensor", None),
    )
    out_specs = (
        P("batch", "tensor", None),
        P("batch", "tensor", None),
        P(),
        P("tensor"),
        P("tensor"),
        P(None, None, "tensor"),
        P("tensor"),
        P(None, "tensor"),
        P("tensor"),
        P("tensor"),
        P("tensor"),
        P(None, "tensor", None),
        P("tensor"),
        P("tensor"),
        P("tensor"),
        P(None, None, "tensor"),
        P("tensor"),
        P("tensor"),
        P("tensor", None),
        P("tensor"),
    )
    sizes = dict(mesh.shape)
    return jax.shard_map(
        functools.partial(per_device, sizes["batch"], sizes["tensor"]),
        mesh=mesh,
        in_specs=in_specs,
        out_specs=out_specs,
        check_vma=False,
    )
```

```python
import functools
import math

import jax
import jax.numpy as jnp
from jax import lax
from jax.experimental import pallas as pl
from jax.experimental.pallas import tpu as pltpu
from jax.sharding import PartitionSpec as P

GROUPS = 32
LANES = 128
BLOCK = 32
EPS = 1e-06
MIB = 1024 * 1024
ANY = pl.BlockSpec(memory_space=pl.ANY)
VMEM = pl.BlockSpec(memory_space=pltpu.VMEM)
SMEM = pl.BlockSpec(memory_space=pltpu.SMEM)
f32 = jnp.float32
bf16 = jnp.bfloat16

(
    FIRST_GAIN,
    FIRST_SHIFT,
    FIRST_BIAS,
    TIME_BIAS,
    SECOND_GAIN,
    SECOND_SHIFT,
    SECOND_BIAS,
    THIRD_GAIN,
    THIRD_SHIFT,
    QUERY_BIAS,
    VALUE_BIAS,
    OUTPUT_BIAS,
) = range(12)


def nn(a, b):
    return lax.dot_general(a, b, (((1,), (0,)), ((), ())), preferred_element_type=f32)


def nt(a, b):
    return lax.dot_general(a, b, (((1,), (1,)), ((), ())), preferred_element_type=f32)


def sigmoid(v):
    return 0.5 * jnp.tanh(0.5 * v) + 0.5


def silu_slope(v, sig):
    return sig * (1.0 + v * (1.0 - sig))


def col_sum(v):
    return jnp.sum(v, axis=0, keepdims=True)


def lane_groups(v, width):
    lanes = v.shape[1]
    lane = lax.broadcasted_iota(jnp.int32, v.shape, 1)
    step = 1
    while step < width:
        up = pltpu.roll(v, step, 1)
        down = pltpu.roll(v, lanes - step, 1)
        v = v + jnp.where((lane & step) != 0, up, down)
        step *= 2
    return v


def fill_shift(shift_ref, side):
    points = shift_ref.shape[1]
    to = lax.broadcasted_iota(jnp.int32, (points, points), 0)
    of = lax.broadcasted_iota(jnp.int32, (points, points), 1)
    for d in range(3):
        s = d - 1
        col = (to & (side - 1)) + s
        hit = (of == to + s) & (col >= 0) & (col < side)
        shift_ref[d * points : (d + 1) * points, :] = jnp.where(hit, 1.0, 0.0).astype(bf16)


def zero_pads(pad_ref, side, points):
    images, chans = pad_ref.shape[1], pad_ref.shape[3]
    for d in range(3):
        for b in range(images):
            pad_ref[d, b, 0:side, :] = jnp.zeros((side, chans), bf16)
            pad_ref[d, b, side + points : 2 * side + points, :] = jnp.zeros((side, chans), bf16)


def put_moved(pad_ref, b, value, side, points):
    chans = value.shape[1]
    column = lax.broadcasted_iota(jnp.int32, (side, chans), 0)
    for d, edge in ((0, 0), (1, None), (2, side - 1)):
        moved = value
        if edge is not None:
            moved = pltpu.roll(value, (1 - d) % points, 0).reshape(side, side, chans)
            moved = jnp.where((column == edge)[None], 0.0, moved).reshape(points, chans)
        pad_ref[d, b, side : side + points, :] = moved.astype(bf16)


def put_pads(pad_ref, b, moved, side, points):
    for d in range(3):
        pad_ref[d, b, side : side + points, :] = moved[d * points : (d + 1) * points]


def taps(pad_ref, b, sign, side, points):
    out = []
    for dr in (-1, 0, 1):
        for dc in (-1, 0, 1):
            top = side + sign * dr * side
            out.append(pad_ref[1 + sign * dc, b, top : top + points, :])
    return out


class Copies:
    def __init__(self, sems):
        self.sems = sems
        self.used = 0

    def start(self, src, dst):
        copy = pltpu.make_async_copy(src, dst, self.sems.at[self.used])
        self.used += 1
        copy.start()
        return copy


def wait_all(copies):
    for c in copies:
        c.wait()


def side_of(points):
    return math.isqrt(points)


def load_split(cps, refs, dst, axis, places):
    out = []
    for ref, place in zip(refs, places, strict=True):
        size = ref.shape[axis]
        idx = [slice(None)] * len(ref.shape)
        idx[axis] = pl.ds(pl.multiple_of(place * size, size), size)
        out.append(cps.start(ref, dst.at[tuple(idx)]))
    return out


def load_images(cps, refs, dst, places, count):
    out = []
    for j, (ref, place) in enumerate(zip(refs, places, strict=True)):
        size = ref.shape[1]
        first = pl.multiple_of(places[0] * count, count) if j == 0 else 0
        out.append(
            cps.start(
                ref.at[pl.ds(first, count)],
                dst.at[:, pl.ds(pl.multiple_of(place * size, size), size), :],
            )
        )
    return out


def places_of(pieces):
    if pieces == 1:
        return [0]
    me = lax.axis_index("tensor")
    return [me, 1 - me]


def split_store(own_ref, send_ref, at, value, axis, places):
    if send_ref is None:
        own_ref[at] = value.astype(own_ref.dtype)
        return
    half = value.shape[axis] // 2
    low = lax.slice_in_dim(value, 0, half, axis=axis)
    high = lax.slice_in_dim(value, half, 2 * half, axis=axis)
    first = places[0] == 0
    own_ref[at] = jnp.where(first, low, high).astype(own_ref.dtype)
    send_ref[at] = jnp.where(first, high, low).astype(send_ref.dtype)


def pack_store(own_ref, send_ref, at, value, axis, places):
    half = value.shape[axis] // 2
    low = lax.slice_in_dim(value, 0, half, axis=axis)
    high = lax.slice_in_dim(value, half, 2 * half, axis=axis)
    first = places[0] == 0
    own = jnp.where(first, low, high).astype(own_ref.dtype)
    send = jnp.where(first, high, low).astype(send_ref.dtype)
    rows = own.shape[0]
    for i in range(own.shape[1] // LANES):
        lanes = slice(i * LANES, (i + 1) * LANES)
        own_ref[at : at + rows, :] = own[:, lanes]
        send_ref[at : at + rows, :] = send[:, lanes]
        at += rows
    return at


def pack_kernel(n_vec, *refs):
    vectors, arrays = refs[:n_vec], refs[n_vec : n_vec + 2]
    vec, x_half, g_half, sems = refs[n_vec + 2 :]
    cps = Copies(sems)
    count = x_half.shape[0]
    first = pl.multiple_of((1 - lax.axis_index("tensor")) * count, count)
    copies = [
        cps.start(src.at[pl.ds(first, count)], dst)
        for src, dst in zip(arrays, (x_half, g_half), strict=True)
    ]
    copies += [cps.start(v, vec.at[j]) for j, v in enumerate(vectors)]
    vec[n_vec:, :] = jnp.zeros((16 - n_vec, vec.shape[1]), f32)
    wait_all(copies)


def part(value, b, points):
    return value[b * points : (b + 1) * points]


def lane_part(value, b, points):
    return value[:, b * points : (b + 1) * points]


def norm_first(x, size, width):
    x3 = x.astype(f32).reshape(GROUPS, width, x.shape[1])
    mean = jnp.sum(jnp.sum(x3, axis=2, keepdims=True), axis=1, keepdims=True) / size
    off = x3 - mean
    var = jnp.sum(jnp.sum(off * off, axis=2, keepdims=True), axis=1, keepdims=True) / size
    rstd = lax.rsqrt(var + EPS)
    return (off * rstd).reshape(x.shape), rstd


def moments(value, width, size):
    mean = lane_groups(col_sum(value), width) / size
    off = value - mean
    return mean, lax.rsqrt(lane_groups(col_sum(off * off), width) / size + EPS)


def pipelined(stages, count):
    for t in range(count + len(stages) - 1):
        for i in reversed(range(len(stages))):
            if 0 <= t - i < count:
                stages[i](t - i)


def front_kernel(pieces, count, *refs):
    it = iter(refs)

    def take(n):
        return [next(it) for _ in range(n)]

    x_in, g_in, w1_in, w2_in, pi_in, po_in, tw_in, vec_in = (take(pieces) for _ in range(8))
    steps_ref, table_ref = take(2)
    if pieces == 2:
        own_out, send_out = take(2)
    else:
        dw2_own, dpo_own, dpi_own = take(3)
    w1_out, w2_out, po_out, all_vec_out, x_out = take(5)
    gpad_out, sum_out, a1t_out, resid_out, gres_out, mix_out = take(6)
    stat_out, sums_out = take(2)
    if pieces == 2:
        own, send = take(2)
    w1, w2, po, vec, xin = take(5)
    gpad, sum_one, a1t, resid, gres, mix = take(6)
    stat, sums = take(2)
    gin, pi, tw, rows, shift, apad, bpad = take(7)
    sems = next(it)

    cps = Copies(sems)
    places = places_of(pieces)
    chans, points = xin.shape[1], xin.shape[2]
    side = side_of(points)
    width = chans // GROUPS
    size = float(width * points)
    scale = chans ** (-0.5)
    images = range(count)

    x_cp = load_images(cps, x_in, xin, places, count)
    vec_cp = load_split(cps, vec_in, vec, 1, places)
    w1_cp = load_split(cps, w1_in, w1, 2, places)
    row_cp = []
    for b in images:
        step = steps_ref[places[0] * count + b]
        row_cp.append(
            cps.start(table_ref.at[pl.ds(pl.multiple_of(step // 16 * 16, 16), 16), :], rows.at[b])
        )
    tw_cp = load_split(cps, tw_in, tw, 1, places)
    w2_cp = load_split(cps, w2_in, w2, 1, places)
    pi_cp = load_split(cps, pi_in, pi, 2, places)
    po_cp = load_split(cps, po_in, po, 0, places)
    g_cp = load_images(cps, g_in, gin, places, count)

    fill_shift(shift, side)
    zero_pads(apad, side, points)
    zero_pads(bpad, side, points)
    zero_pads(gpad, side, points)
    eye = shift[points : 2 * points, :]

    wait_all(vec_cp)
    vcols = jnp.transpose(vec[...])

    def col(j):
        return vcols[:, j : j + 1]

    def row(j):
        return vec[j : j + 1, :]

    wait_all(x_cp)
    wait_all(row_cp)
    wait_all(tw_cp)
    wait_all(w1_cp)
    outs = [cps.start(vec, all_vec_out), cps.start(xin, x_out), cps.start(w1, w1_out)]
    picked = []
    for b in images:
        step = steps_ref[places[0] * count + b]
        r = lax.broadcasted_iota(jnp.int32, (16, rows.shape[2]), 0)
        picked.append(col_sum(jnp.where(r == lax.rem(step, 16), rows[b].astype(f32), 0.0)))
    emb = jnp.concatenate(picked + picked[:1] * (8 - count), axis=0)
    time_add = nn((emb * sigmoid(emb)).astype(bf16), tw[...]) + row(TIME_BIAS) + row(FIRST_BIAS)

    stats2, stats3 = [], []
    act_t = [None] * count

    def norm_one(b):
        hat, _ = norm_first(xin[b], size, width)
        pre = hat * col(FIRST_GAIN) + col(FIRST_SHIFT)
        act = (pre * sigmoid(pre)).astype(bf16)
        a1t[b] = act
        put_pads(apad, b, nt(shift[...], act).astype(bf16), side, points)

    def conv_one(b):
        lhs = jnp.concatenate(taps(apad, b, 1, side, points), axis=1)
        sum_one[b] = nn(lhs, w1[...].reshape(9 * chans, chans)) + time_add[b : b + 1]

    def norm_two(b):
        mean, rstd = moments(sum_one[b], width, size)
        stats2.append((mean, rstd))
        hat = (sum_one[b] - mean) * rstd
        pre = hat * row(SECOND_GAIN) + row(SECOND_SHIFT)
        act = pre * sigmoid(pre)
        act_t[b] = jnp.transpose(act.astype(bf16))
        put_moved(bpad, b, act, side, points)

    def conv_two(b):
        if b == 0:
            wait_all(w2_cp)
        lhs = jnp.concatenate(taps(bpad, b, 1, side, points), axis=1)
        val = nn(lhs, w2[...].reshape(9 * chans, chans)) + row(SECOND_BIAS)
        resid[b] = val + nt(eye, xin[b])

    normed = []

    def norm_three(b):
        mean, rstd = moments(resid[b], width, size)
        stats3.append((mean, rstd))
        hat = (resid[b] - mean) * rstd
        normed.append((hat * row(THIRD_GAIN) + row(THIRD_SHIFT)).astype(bf16))

    pipelined([norm_one, conv_one, norm_two, conv_two, norm_three], count)
    outs += [cps.start(a1t, a1t_out), cps.start(sum_one, sum_out), cps.start(resid, resid_out)]
    stat[0:count, :] = jnp.concatenate([m for m, _ in stats2], axis=0)
    stat[count : 2 * count, :] = jnp.concatenate([r for _, r in stats2], axis=0)
    outs.append(cps.start(stat, stat_out))

    wait_all(pi_cp)
    wait_all(po_cp)
    wait_all(g_cp)
    outs += [cps.start(w2, w2_out), cps.start(po, po_out)]
    pi_row = jnp.concatenate([pi[0], pi[1], pi[2]], axis=1)
    pi_t = jnp.concatenate([jnp.transpose(pi[1]), jnp.transpose(pi[2])], axis=0)
    zero = jnp.zeros((1, chans), f32)
    normed_t = jnp.concatenate([jnp.transpose(v) for v in normed], axis=1)
    normed = jnp.concatenate(normed, axis=0)
    lin = nn(normed, pi_row)
    q = (lin[:, :chans] + row(QUERY_BIAS)).astype(bf16)
    k = lin[:, chans : 2 * chans].astype(bf16)
    v = (lin[:, 2 * chans :] + row(VALUE_BIAS)).astype(bf16)
    lin_t = nn(pi_t, normed_t)
    kt = lin_t[:chans].astype(bf16)
    vt = (lin_t[chans:] + col(VALUE_BIAS)).astype(bf16)
    grad_all = jnp.concatenate([gin[b] for b in images], axis=1)
    grad_mixed = nn(po[...], grad_all).astype(bf16)
    scores = [nt(part(k, b, points), part(q, b, points)) for b in images]
    grad_w = [nn(part(v, b, points), lane_part(grad_mixed, b, points)) for b in images]
    weights, grad_s = [], []
    for b in images:
        top = scores[b] * scale
        expo = jnp.exp(top - jnp.max(top, axis=0, keepdims=True))
        probs = expo * (1.0 / jnp.sum(expo, axis=0, keepdims=True))
        weights.append(probs.astype(bf16))
        inner = probs * grad_w[b]
        grad_s.append((inner - probs * jnp.sum(inner, axis=0, keepdims=True)).astype(bf16))
    mixed = []
    for b in images:
        mixed.append(nn(lane_part(vt, b, points), weights[b]).astype(bf16))
        mix[b] = mixed[b]
    outs.append(cps.start(mix, mix_out))
    grad_qt = [nn(lane_part(kt, b, points), grad_s[b]) * scale for b in images]
    grad_q = [jnp.transpose(t.astype(bf16)) for t in grad_qt]
    grad_k = [(nn(grad_s[b], part(q, b, points)) * scale).astype(bf16) for b in images]
    grad_v = [nt(weights[b], lane_part(grad_mixed, b, points)).astype(bf16) for b in images]
    lin_grad = jnp.concatenate(
        [jnp.concatenate([grad_q[b], grad_k[b], grad_v[b]], axis=1) for b in images], axis=0
    )
    qb_grad = col_sum(sum(t.astype(f32) for t in grad_q))
    vb_grad = col_sum(sum(t.astype(f32) for t in grad_v))
    dpo = nt(jnp.concatenate(mixed, axis=1), grad_all)
    grad_normed = nt(lin_grad, pi_row)

    gain3, shift3, means = [], [], []
    for b in images:
        hat = (resid[b] - stats3[b][0]) * stats3[b][1]
        val = part(grad_normed, b, points)
        gain3.append(col_sum(val * hat))
        shift3.append(col_sum(val))
        both = jnp.concatenate([shift3[b], gain3[b]], axis=0) * row(THIRD_GAIN)
        means.append(lane_groups(both, width) / size)
    sb_grad, ob_grad = zero, zero
    for b in images:
        hat = (resid[b] - stats3[b][0]) * stats3[b][1]
        h = part(grad_normed, b, points) * row(THIRD_GAIN)
        grad_out = nt(eye, gin[b])
        ob_grad = ob_grad + col_sum(grad_out)
        val = grad_out + stats3[b][1] * (h - means[b][0:1] - hat * means[b][1:2])
        gres[b] = val
        sb_grad = sb_grad + col_sum(val)
        put_moved(gpad, b, val, side, points)
    lane = lax.broadcasted_iota(jnp.int32, (1, chans), 1)
    stamp = jnp.zeros((1, chans), f32)
    for b in images:
        step = jnp.full((1, chans), steps_ref[places[0] * count + b], jnp.int32)
        stamp = jnp.where(lane == b, (step >> 5).astype(f32), stamp)
        stamp = jnp.where(lane == LANES // 2 + b, (step & 31).astype(f32), stamp)
    sums[...] = jnp.concatenate(
        [sb_grad, sum(gain3), sum(shift3), qb_grad, vb_grad, ob_grad, stamp, zero], axis=0
    )
    outs += [cps.start(gres, gres_out), cps.start(gpad, gpad_out), cps.start(sums, sums_out)]

    dpi = nn(normed_t, lin_grad)
    at = 0
    if pieces == 2:
        at = pack_store(own, send, at, dpo, 0, places)
        for j in range(3):
            at = pack_store(own, send, at, dpi[:, j * chans : (j + 1) * chans], 1, places)
        outs += copy_rows(cps, [(send, send_out), (own, own_out)], 0, at)
    else:
        dpo_own[...] = dpo
        for j in range(3):
            dpi_own[j] = dpi[:, j * chans : (j + 1) * chans]

    a_all = jnp.concatenate(act_t, axis=1)
    moved = [taps(gpad, b, -1, side, points) for b in images]
    for tap in range(9):
        val = nn(a_all, jnp.concatenate([moved[b][tap] for b in images], axis=0))
        if pieces == 2:
            start = at if tap % 3 == 0 else start
            at = pack_store(own, send, at, val, 0, places)
            if tap % 3 == 2:
                outs += copy_rows(cps, [(send, send_out), (own, own_out)], start, at)
        else:
            dw2_own[tap] = val

    wait_all(outs)


def copy_rows(cps, pairs, start, end):
    rows = slice(start, end)
    return [cps.start(src.at[rows], dst.at[rows]) for src, dst in pairs]


def back_kernel(pieces, count, *refs):
    it = iter(refs)

    def take(n):
        return [next(it) for _ in range(n)]

    kept = take(13)
    if pieces == 2:
        own_out, send_out, block_own_out, block_send_out, image_own_out, image_send_out = take(6)
    else:
        own, block_own_out, image_own_out = take(3)
        block_send_out = image_send_out = None
    small_out = next(it)
    w1, w2, po, vec, xin, gpad, sum_one, a1t, resid, gres, mix, stat, front_sums = take(13)
    if pieces == 2:
        own, send, block_own, block_send, image_own, image_send = take(6)
    else:
        block_own, image_own = take(2)
        block_send = image_send = None
    small, hpad, back, sems = take(4)
    cps = Copies(sems)
    places = places_of(pieces)
    points, chans = sum_one.shape[1], sum_one.shape[2]
    side = side_of(points)
    width = chans // GROUPS
    size = float(width * points)
    images = range(count)

    w1_in, w2_in, po_in, vec_in, x_in, gpad_in, sum_in, a1t_in, resid_in, gres_in, mix_in = kept[:11]
    w2_cp = cps.start(w2_in, w2)
    gpad_cp = [cps.start(gpad_in.at[:, b], gpad.at[:, b]) for b in images]
    small_cp = [(vec_in, vec), (kept[11], stat), (kept[12], front_sums)]
    small_cp = [cps.start(src, dst) for src, dst in small_cp]
    sum_cp = cps.start(sum_in, sum_one)
    a1t_cp = cps.start(a1t_in, a1t)
    later = [(w1_in, w1), (po_in, po), (x_in, xin), (resid_in, resid), (gres_in, gres), (mix_in, mix)]
    later = [cps.start(src, dst) for src, dst in later]

    def row(j):
        return vec[j : j + 1, :]

    zero_pads(hpad, side, points)
    w2_cp.wait()
    w2_cols = jnp.concatenate([w2[k] for k in range(9)], axis=1)
    gain, shift_g, times = [], [], []

    def conv_back(b):
        gpad_cp[b].wait()
        back[b] = nt(jnp.concatenate(taps(gpad, b, -1, side, points), axis=1), w2_cols)

    def norm_back(b):
        if b == 0:
            sum_cp.wait()
            wait_all(small_cp)
        mean, rstd = stat[b : b + 1, :], stat[count + b : count + b + 1, :]
        hat = (sum_one[b] - mean) * rstd
        pre = hat * row(SECOND_GAIN) + row(SECOND_SHIFT)
        val = back[b] * silu_slope(pre, sigmoid(pre))
        gain.append(col_sum(val * hat))
        shift_g.append(col_sum(val))
        both = jnp.concatenate([shift_g[b], gain[b]], axis=0) * row(SECOND_GAIN)
        both = lane_groups(both, width) / size
        val = rstd * (val * row(SECOND_GAIN) - both[0:1] - hat * both[1:2])
        times.append(col_sum(val))
        put_moved(hpad, b, val, side, points)

    pipelined([conv_back, norm_back], count)

    a1t_cp.wait()
    a_all = jnp.concatenate([a1t[b] for b in images], axis=1)
    moved = [taps(hpad, b, -1, side, points) for b in images]
    at = 0
    outs = []
    for tap in range(9):
        val = nn(a_all, jnp.concatenate([moved[b][tap] for b in images], axis=0))
        if pieces == 2:
            start = at if tap % 3 == 0 else start
            at = pack_store(own, send, at, val, 1, places)
            if tap % 3 == 2:
                outs += copy_rows(cps, [(send, send_out), (own, own_out)], start, at)
        else:
            own[tap] = val

    wait_all(later)
    vcols = jnp.transpose(vec[...])

    def col(j):
        return vcols[:, j : j + 1]

    def put_out(own_ref, send_ref, own_dst, send_dst, b, val):
        split_store(own_ref, send_ref, b, val, 0, places)
        outs.append(cps.start(own_ref.at[b], own_dst.at[b]))
        if send_ref is not None:
            outs.append(cps.start(send_ref.at[b], send_dst.at[b]))

    proj = nn(jnp.transpose(po[...]), jnp.concatenate([mix[b] for b in images], axis=1))

    w1_cols = jnp.concatenate([w1[k] for k in range(9)], axis=1)
    zero = jnp.zeros((chans, 1), f32)
    gain_sum, shift_sum = [zero], [zero]
    first_back = [None] * count

    def groups(v):
        total = jnp.sum(v.reshape(GROUPS, width, 1), axis=1, keepdims=True) / size
        return jnp.broadcast_to(total, (GROUPS, width, 1)).reshape(chans, 1)

    def conv_first(b):
        first_back[b] = nt(w1_cols, jnp.concatenate(taps(hpad, b, -1, side, points), axis=1))

    def block_part(b):
        val = jnp.transpose(resid[b]) + lane_part(proj, b, points) + col(OUTPUT_BIAS)
        put_out(block_own, block_send, block_own_out, block_send_out, b, val)

    def norm_first_back(b):
        hat, rstd = norm_first(xin[b], size, width)
        rstd = jnp.broadcast_to(rstd, (GROUPS, width, 1)).reshape(chans, 1)
        pre = hat * col(FIRST_GAIN) + col(FIRST_SHIFT)
        val = first_back[b] * silu_slope(pre, sigmoid(pre))
        gain = jnp.sum(val * hat, axis=1, keepdims=True)
        shift = jnp.sum(val, axis=1, keepdims=True)
        gain_sum[0] = gain_sum[0] + gain
        shift_sum[0] = shift_sum[0] + shift
        first_mean = groups(shift * col(FIRST_GAIN))
        second_mean = groups(gain * col(FIRST_GAIN))
        val = rstd * (val * col(FIRST_GAIN) - first_mean - hat * second_mean)
        val = val + jnp.transpose(gres[b])
        put_out(image_own, image_send, image_own_out, image_send_out, b, val)

    pipelined([conv_first, block_part, norm_first_back], count)

    lane = lax.broadcasted_iota(jnp.int32, (chans, LANES), 1)
    both = jnp.where(lane == 0, gain_sum[0], 0.0) + jnp.where(lane == 1, shift_sum[0], 0.0)
    both = jnp.transpose(both)
    rows = [front_sums[j : j + 1, :] for j in range(6)]
    rows += [sum(gain), sum(shift_g), sum(times), both[0:1], both[1:2]]
    flat = []
    for r in rows + times:
        flat += [r[:, i * LANES : (i + 1) * LANES] for i in range(chans // LANES)]
    flat.append(front_sums[6:7, :LANES])
    flat += [jnp.zeros((1, LANES), f32)] * (BLOCK - len(flat))
    small[...] = jnp.concatenate(flat, axis=0).astype(bf16)
    outs.append(cps.start(small, small_out))
    wait_all(outs)


def put_quarters(quarters, flat):
    me = lax.axis_index("batch") & 3
    rows = quarters[0].shape[0]
    for j, ref in enumerate(quarters):
        flat[pl.ds(pl.multiple_of((me ^ j) * rows, 16), rows), :] = ref[...]


def unpack_first_kernel(*refs):
    quarters = refs[:4]
    dw1_out, flat, dw1, sems = refs[4:]
    cps = Copies(sems)
    put_quarters(quarters, flat)
    outs = []
    chans = dw1.shape[1]
    for tap in range(dw1.shape[0]):
        dw1[tap] = flat[tap * chans : (tap + 1) * chans, :].astype(f32)
        if tap % 3 == 2:
            part = slice(tap - 2, tap + 1)
            outs.append(cps.start(dw1.at[part], dw1_out.at[part]))
    wait_all(outs)


def unpack_second_kernel(*refs):
    quarters = refs[:4]
    dw2_out, dpo_out, dpi_out, flat, dw2, dpo, dpi, sems = refs[4:]
    cps = Copies(sems)
    put_quarters(quarters, flat)
    outs = []
    chans = dpi.shape[1]
    half = chans // 2
    for i in range(2):
        dpo[:, i * LANES : (i + 1) * LANES] = flat[i * half : (i + 1) * half, :].astype(f32)
    outs.append(cps.start(dpo, dpo_out))
    at = chans
    for j in range(3):
        dpi[j] = flat[at : at + chans, :].astype(f32)
        at += chans
    outs.append(cps.start(dpi, dpi_out))
    for tap in range(dw2.shape[0]):
        for i in range(2):
            dw2[tap, :, i * LANES : (i + 1) * LANES] = flat[at : at + half, :].astype(f32)
            at += half
        if tap % 3 == 2:
            part = slice(tap - 2, tap + 1)
            outs.append(cps.start(dw2.at[part], dw2_out.at[part]))
    wait_all(outs)


def swap(value, axis, size, bit):
    return lax.ppermute(value, axis, [(i, i ^ bit) for i in range(size)])


def near_parts(part):
    me = lax.axis_index("batch") & 3
    return [part(me ^ j).astype(bf16) for j in range(1, 4)]


def after(values, *others):
    done = lax.optimization_barrier((tuple(values), others))
    return list(done[0])


def send_near(sent, batch):
    return [swap(v, "batch", batch, j + 1) for j, v in enumerate(sent)]


def sum_near(got, part):
    total = part(lax.axis_index("batch") & 3).astype(f32)
    for g in got:
        total = total + g.astype(f32)
    return total.astype(bf16)


def far_steps(batch):
    return batch.bit_length() - 3


def send_far(piece, extra, step, batch):
    steps = far_steps(batch)
    mine = piece if extra is None else jnp.concatenate([piece, extra], axis=0)
    tensor = lax.axis_size("tensor")
    pairs = []
    for i in range(batch):
        for core in range(tensor):
            bit = 4 << (step if core % 2 == 0 else steps - 1 - step)
            pairs.append((i * tensor + core, (i ^ bit) * tensor + core))
    return lax.ppermute(mine, ("batch", "tensor"), pairs)


def sum_far(piece, extra, got):
    rows = piece.shape[0]
    piece = (piece.astype(f32) + got[:rows].astype(f32)).astype(bf16)
    if extra is not None:
        extra = jnp.concatenate([extra, got[rows:]], axis=0)
    return piece, extra


def gather_near(piece, batch):
    return [piece] + [swap(piece, "batch", batch, j) for j in range(1, 4)]


def in_order(pieces):
    me = lax.axis_index("batch")
    parts = jnp.stack(pieces, axis=0)
    parts = parts.reshape((2, 2) + parts.shape[1:])
    parts = jnp.where((me & 1) == 1, jnp.flip(parts, axis=1), parts)
    parts = jnp.where((me & 2) == 2, jnp.flip(parts, axis=0), parts)
    return parts.reshape((-1, LANES))


def unpack(flat, shapes):
    out = []
    at = 0
    for shape in shapes:
        n = math.prod(shape) // 128
        out.append(flat[at : at + n].reshape(shape).astype(f32))
        at += n
    return out


def per_device(
    batch,
    tensor,
    images,
    timesteps,
    embed_table,
    first_gain,
    first_shift,
    first_conv,
    first_bias,
    time_weight,
    time_bias,
    second_gain,
    second_shift,
    second_conv,
    second_bias,
    third_gain,
    third_shift,
    project_in,
    query_bias,
    value_bias,
    project_out,
    output_bias,
    cotangent,
):
    per_batch, local, points = images.shape
    chans = local * tensor
    count = per_batch // tensor
    steps, embed = embed_table.shape
    pieces = 2 if tensor == 2 else 1
    me = lax.axis_index("tensor")
    vectors = [
        first_gain,
        first_shift,
        first_bias,
        time_bias,
        second_gain,
        second_shift,
        second_bias,
        third_gain,
        third_shift,
        query_bias,
        value_bias,
        output_bias,
    ]
    def in_hbm(array):
        return pltpu.with_memory_space_constraint(array, pltpu.HBM)

    n_vec = len(vectors)
    if pieces == 2:
        half = (count, local, points)
        vec, x_half, g_half = pl.pallas_call(
            functools.partial(pack_kernel, n_vec),
            out_shape=[
                jax.ShapeDtypeStruct((16, local), f32),
                jax.ShapeDtypeStruct(half, bf16),
                jax.ShapeDtypeStruct(half, bf16),
            ],
            in_specs=[ANY] * (n_vec + 2),
            out_specs=[VMEM] * 3,
            scratch_shapes=[pltpu.SemaphoreType.DMA((n_vec + 2,))],
            compiler_params=pltpu.CompilerParams(vmem_limit_bytes=4 * MIB),
            name="pack",
        )(*(in_hbm(v) for v in vectors + [images, cotangent]))
    else:
        vec = jnp.stack(vectors + [output_bias] * 4, axis=0)
        x_half = g_half = None

    def images_of(array, half):
        if pieces == 2:
            return [array, swap(half, "tensor", 2, 1)]
        return [lax.all_to_all(array, "tensor", 0, 1, tiled=True)]

    def whole(array, axis):
        if pieces == 2:
            return [array, swap(array, "tensor", 2, 1)]
        return [lax.all_gather(array, "tensor", axis=axis, tiled=True)]

    x_in = images_of(images, x_half)
    vec_in = whole(vec, 1)
    tw_in = whole(time_weight, 1)
    w1_in = whole(first_conv, 2)
    w2_in = whole(second_conv, 1)
    pi_in = whole(project_in, 2)
    po_in = whole(project_out, 0)
    g_in = images_of(cotangent, g_half)
    my_steps = timesteps if pieces == 2 else lax.dynamic_slice_in_dim(timesteps, me * count, count)

    side = side_of(points)
    image_b = (count, chans, points)
    image_p = (count, points, chans)
    pads = (3, count, points + 2 * side, chans)

    def shape(s, d):
        return jax.ShapeDtypeStruct(s, d)

    def params(mib):
        return pltpu.CompilerParams(vmem_limit_bytes=mib * MIB)

    def cost(units, moved):
        flops = 2 * units * count * points * chans * chans
        return pl.CostEstimate(flops=flops, bytes_accessed=moved, transcendentals=0)

    half_b = 9 * chans * chans // 2 // LANES
    half_a = half_b + 4 * chans * chans // 2 // LANES
    if pieces == 2:
        grads_a = [pltpu.HBM((half_a, LANES), bf16)] * 2
        grads_b = [pltpu.HBM((half_b, LANES), bf16)] * 2
    else:
        grads_a = [shape((9, chans, chans), f32), shape((chans, chans), f32)]
        grads_a.append(shape((3, chans, chans), f32))
        grads_b = [shape((9, chans, chans), f32)]
    n_grad = len(grads_a)
    steps_in = in_hbm(my_steps)
    kept = [
        ((9, chans, chans), bf16),
        ((9, chans, chans), bf16),
        ((chans, chans), bf16),
        ((16, chans), f32),
        (image_b, bf16),
        (pads, bf16),
        (image_p, f32),
        (image_b, bf16),
        (image_p, f32),
        (image_p, f32),
        (image_b, bf16),
        ((2 * count, chans), f32),
        ((8, chans), f32),
    ]
    out_a = ANY if pieces == 2 else VMEM
    scratch_a = [pltpu.VMEM(v.shape, v.dtype) for v in grads_a] if pieces == 2 else []

    front = pl.pallas_call(
        functools.partial(front_kernel, pieces, count),
        out_shape=grads_a
        + [pltpu.HBM(*v) for v in kept],
        in_specs=[ANY, VMEM][:pieces] * 8 + [SMEM, ANY],
        out_specs=[out_a] * n_grad + [ANY] * len(kept),
        scratch_shapes=scratch_a
        + [pltpu.VMEM(*v) for v in kept]
        + [
            pltpu.VMEM(image_b, bf16),
            pltpu.VMEM((3, chans, chans), bf16),
            pltpu.VMEM((embed, chans), bf16),
            pltpu.VMEM((count, 16, embed), bf16),
            pltpu.VMEM((3 * points, points), bf16),
            pltpu.VMEM(pads, bf16),
            pltpu.VMEM(pads, bf16),
            pltpu.SemaphoreType.DMA((8 * pieces + count + 21,)),
        ],
        compiler_params=params(32),
        cost_estimate=cost(54, 12 << 20),
        name="front",
    )(
        *(
            place(v)
            for pair in (x_in, g_in, w1_in, w2_in, pi_in, po_in, tw_in, vec_in)
            for v, place in zip(pair, (in_hbm, lambda v: v))
        ),
        steps_in,
        in_hbm(embed_table),
    )
    sums_a = front[:n_grad]
    kept_now = list(front[n_grad:])

    def quarters(sums, axes, beside=None):
        if pieces == 2:
            got = swap(sums[1], "tensor", 2, 1)
            if beside is not None:
                (got,) = after([got], beside)
            rows = got.shape[0] // 4
            own4, got4 = (v.reshape(4, rows, LANES) for v in (sums[0], got))

            def part(q):
                pair = [lax.dynamic_index_in_dim(v, q, 0, False).astype(f32) for v in (own4, got4)]
                return pair[0] + pair[1]

            return part
        done = [
            lax.psum_scatter(v, "tensor", scatter_dimension=axis, tiled=True)
            for v, axis in zip(sums, axes, strict=True)
        ]
        flat = jnp.concatenate([v.reshape(-1, LANES) for v in done], axis=0)
        flat = jnp.pad(flat, ((0, -flat.shape[0] % 64), (0, 0)))
        rows = flat.shape[0] // 4
        flat = flat.reshape(4, rows, LANES)
        return lambda q: lax.dynamic_index_in_dim(flat, q, 0, False)

    part_a = quarters(sums_a, (1, 0, 2))
    sent_a = near_parts(part_a)

    got_a = send_near(sent_a, batch)
    kept_now[-2:] = after(kept_now[-2:], *sent_a)

    half = (count, chans // 2, points)
    if pieces == 2:
        outs_b = grads_b + [pltpu.HBM(half, f32), pltpu.HBM(half, bf16)] * 2
        scratch_b = [pltpu.VMEM(v.shape, v.dtype) for v in outs_b]
    else:
        outs_b = grads_b + [pltpu.HBM(image_b, f32)] * 2
        scratch_b = [pltpu.VMEM(image_b, f32)] * 2
    *outs_b, block = pl.pallas_call(
        functools.partial(back_kernel, pieces, count),
        out_shape=outs_b + [pltpu.HBM((BLOCK, LANES), bf16)],
        in_specs=[ANY] * len(kept),
        out_specs=[out_a] * pieces + [ANY] * (2 * pieces + 1),
        scratch_shapes=[pltpu.VMEM(*v) for v in kept]
        + scratch_b
        + [
            pltpu.VMEM((BLOCK, LANES), bf16),
            pltpu.VMEM(pads, bf16),
            pltpu.VMEM(image_p, f32),
            pltpu.SemaphoreType.DMA((6 + 5 * count + 13,)),
        ],
        compiler_params=params(36),
        cost_estimate=cost(33, 12 << 20),
        name="back",
    )(*(in_hbm(v) for v in kept_now))
    sums_b, block_part, image_grad = outs_b[:pieces], outs_b[pieces : 2 * pieces], outs_b[2 * pieces :]
    got_a = after(got_a, block)
    sums_b = after(sums_b, *got_a)
    piece_a = sum_near(got_a, part_a)
    part_b = quarters(sums_b, (2,), piece_a)
    sent_b = near_parts(part_b)
    got_b = send_near([jnp.concatenate([v, block], axis=0) for v in sent_b], batch)
    piece_a, _ = sum_far(piece_a, None, send_far(piece_a, None, 0, batch))
    got_b = after(got_b, piece_a)
    rows_b = sent_b[0].shape[0]
    blocks = jnp.concatenate([block] + [g[rows_b:] for g in got_b], axis=0)
    piece_b = sum_near([g[:rows_b] for g in got_b], part_b)
    for step in range(1, far_steps(batch)):
        piece_a, _ = sum_far(piece_a, None, send_far(piece_a, None, step, batch))
    block_part = after(block_part, piece_b)
    image_grad = after(image_grad, piece_b)

    def placed(own, send):
        if pieces == 2:
            got = swap(send, "tensor", 2, 1).astype(f32)
            low = jnp.where(me == 0, own, got)
            high = jnp.where(me == 0, got, own)
            return jnp.concatenate([low, high], axis=0)
        return lax.all_to_all(own, "tensor", 1, 0, tiled=True)

    block_out = placed(block_part[0], block_part[-1])
    images_grad = placed(image_grad[0], image_grad[-1])

    got_a = gather_near(piece_a, batch)
    for step in range(far_steps(batch)):
        far_b = send_far(piece_b, blocks, step, batch)
        if step > 0:
            (far_b,) = after([far_b], got_a[0])
        piece_b, blocks = sum_far(piece_b, blocks, far_b)
    got_b = gather_near(piece_b, batch)
    got_a = after(got_a, piece_b)

    if pieces == 2:

        def unpacked(kernel, name, got, rows, shapes):
            outs = [shape(v, f32) for v in shapes]
            return pl.pallas_call(
                kernel,
                out_shape=outs,
                in_specs=[VMEM] * 4,
                out_specs=[ANY] * len(outs),
                scratch_shapes=[pltpu.VMEM((rows, LANES), bf16)]
                + [pltpu.VMEM(v.shape, v.dtype) for v in outs]
                + [pltpu.SemaphoreType.DMA((len(outs) + 2,))],
                compiler_params=params(12),
                name=name,
            )(*got)

        second_conv_grad, project_out_grad, project_in_grad = unpacked(
            unpack_second_kernel,
            "unpack_second",
            got_a,
            half_a,
            [(9, local, chans), (local, chans), (3, chans, local)],
        )
        (first_conv_grad,) = unpacked(
            unpack_first_kernel, "unpack_first", got_b, half_b, [(9, chans, local)]
        )
    else:
        second_conv_grad, project_out_grad, project_in_grad = unpack(
            in_order(got_a), [(9, local, chans), (local, chans), (3, chans, local)]
        )
        (first_conv_grad,) = unpack(in_order(got_b), [(9, chans, local)])

    if pieces == 2:
        blocks = jnp.concatenate([blocks, swap(blocks, "tensor", 2, 1)], axis=0)
        two = blocks.reshape(2, batch, BLOCK, LANES)
        blocks = jnp.where(me == 0, two, jnp.flip(two, axis=0))
    else:
        blocks = lax.all_gather(blocks, "tensor", axis=0, tiled=True)
    blocks = blocks.reshape(batch * tensor, BLOCK, LANES)
    wide = chans // LANES
    n_sum = 11 * wide
    sums = jnp.sum(blocks[:, :n_sum].astype(f32), axis=0).reshape(11, chans)
    sums = jnp.concatenate([sums, sums[8:9]], axis=0)
    mine = lax.dynamic_slice_in_dim(sums, me * local, local, axis=1)
    all_times = blocks[:, n_sum : n_sum + wide * count].reshape(-1, chans)
    stamps = blocks[:, n_sum + wide * count].astype(jnp.int32)
    all_steps = stamps[:, :count] * 32 + stamps[:, LANES // 2 : LANES // 2 + count]
    all_steps = all_steps.reshape(-1)
    one_hot = (all_steps[:, None] == jnp.arange(steps, dtype=jnp.int32)[None, :]).astype(bf16)
    emb = nn(one_hot, embed_table)
    sig = sigmoid(emb)
    act = (emb * sig).astype(bf16)
    my_times = lax.dynamic_slice_in_dim(all_times, me * local, local, axis=1)
    time_weight_grad = lax.dot_general(
        act, my_times, (((0,), (0,)), ((), ())), preferred_element_type=f32
    )
    if pieces == 2:
        tw = jnp.where(
            me == 0, jnp.concatenate(tw_in, axis=1), jnp.concatenate(tw_in[::-1], axis=1)
        )
    else:
        tw = tw_in[0]
    grad_emb = (nt(all_times, tw) * silu_slope(emb, sig)).astype(bf16)
    table_grad = lax.dot_general(
        one_hot, grad_emb, (((0,), (0,)), ((), ())), preferred_element_type=f32
    )
    return (
        block_out,
        images_grad,
        table_grad,
        mine[9],
        mine[10],
        first_conv_grad,
        mine[8],
        time_weight_grad,
        mine[11],
        mine[6],
        mine[7],
        second_conv_grad,
        mine[0],
        mine[1],
        mine[2],
        project_in_grad,
        mine[3],
        mine[4],
        project_out_grad,
        mine[5],
    )


def solution(mesh):
    in_specs = (
        P("batch", "tensor", None),
        P("batch"),
        P(),
        P("tensor"),
        P("tensor"),
        P(None, None, "tensor"),
        P("tensor"),
        P(None, "tensor"),
        P("tensor"),
        P("tensor"),
        P("tensor"),
        P(None, "tensor", None),
        P("tensor"),
        P("tensor"),
        P("tensor"),
        P(None, None, "tensor"),
        P("tensor"),
        P("tensor"),
        P("tensor", None),
        P("tensor"),
        P("batch", "tensor", None),
    )
    out_specs = (
        P("batch", "tensor", None),
        P("batch", "tensor", None),
        P(),
        P("tensor"),
        P("tensor"),
        P(None, None, "tensor"),
        P("tensor"),
        P(None, "tensor"),
        P("tensor"),
        P("tensor"),
        P("tensor"),
        P(None, "tensor", None),
        P("tensor"),
        P("tensor"),
        P("tensor"),
        P(None, None, "tensor"),
        P("tensor"),
        P("tensor"),
        P("tensor", None),
        P("tensor"),
    )
    sizes = dict(mesh.shape)
    return jax.shard_map(
        functools.partial(per_device, sizes["batch"], sizes["tensor"]),
        mesh=mesh,
        in_specs=in_specs,
        out_specs=out_specs,
        check_vma=False,
    )
```

```python
import functools
import math

import jax
import jax.numpy as jnp
from jax import lax
from jax.experimental import pallas as pl
from jax.experimental.pallas import tpu as pltpu
from jax.sharding import PartitionSpec as P

GROUPS = 32
LANES = 128
BLOCK = 32
EPS = 1e-06
MIB = 1024 * 1024
ANY = pl.BlockSpec(memory_space=pl.ANY)
VMEM = pl.BlockSpec(memory_space=pltpu.VMEM)
SMEM = pl.BlockSpec(memory_space=pltpu.SMEM)
f32 = jnp.float32
bf16 = jnp.bfloat16

(
    FIRST_GAIN,
    FIRST_SHIFT,
    FIRST_BIAS,
    TIME_BIAS,
    SECOND_GAIN,
    SECOND_SHIFT,
    SECOND_BIAS,
    THIRD_GAIN,
    THIRD_SHIFT,
    QUERY_BIAS,
    VALUE_BIAS,
    OUTPUT_BIAS,
) = range(12)


def nn(a, b):
    return lax.dot_general(a, b, (((1,), (0,)), ((), ())), preferred_element_type=f32)


def nt(a, b):
    return lax.dot_general(a, b, (((1,), (1,)), ((), ())), preferred_element_type=f32)


def sigmoid(v):
    return 0.5 * jnp.tanh(0.5 * v) + 0.5


def silu_slope(v, sig):
    return sig * (1.0 + v * (1.0 - sig))


def col_sum(v):
    return jnp.sum(v, axis=0, keepdims=True)


def lane_groups(v, width):
    lanes = v.shape[1]
    lane = lax.broadcasted_iota(jnp.int32, v.shape, 1)
    step = 1
    while step < width:
        up = pltpu.roll(v, step, 1)
        down = pltpu.roll(v, lanes - step, 1)
        v = v + jnp.where((lane & step) != 0, up, down)
        step *= 2
    return v


def zero_pads(pad_ref, side, points):
    images, chans = pad_ref.shape[1], pad_ref.shape[3]
    for d in range(3):
        for b in range(images):
            pad_ref[d, b, 0:side, :] = jnp.zeros((side, chans), bf16)
            pad_ref[d, b, side + points : 2 * side + points, :] = jnp.zeros((side, chans), bf16)


def put_moved(pad_ref, b, value, side, points):
    chans = value.shape[1]
    column = lax.broadcasted_iota(jnp.int32, (side, chans), 0)
    for d, edge in ((0, 0), (1, None), (2, side - 1)):
        moved = value
        if edge is not None:
            moved = pltpu.roll(value, (1 - d) % points, 0).reshape(side, side, chans)
            moved = jnp.where((column == edge)[None], 0.0, moved).reshape(points, chans)
        pad_ref[d, b, side : side + points, :] = moved.astype(bf16)


def taps(pad_ref, b, sign, side, points):
    out = []
    for dr in (-1, 0, 1):
        for dc in (-1, 0, 1):
            top = side + sign * dr * side
            out.append(pad_ref[1 + sign * dc, b, top : top + points, :])
    return out


class Copies:
    def __init__(self, sems):
        self.sems = sems
        self.used = 0

    def start(self, src, dst):
        copy = pltpu.make_async_copy(src, dst, self.sems.at[self.used])
        self.used += 1
        copy.start()
        return copy


def wait_all(copies):
    for c in copies:
        c.wait()


def side_of(points):
    return math.isqrt(points)


def load_split(cps, refs, dst, axis, places):
    out = []
    for ref, place in zip(refs, places, strict=True):
        size = ref.shape[axis]
        idx = [slice(None)] * len(ref.shape)
        idx[axis] = pl.ds(pl.multiple_of(place * size, size), size)
        out.append(cps.start(ref, dst.at[tuple(idx)]))
    return out


def load_images(cps, refs, dst, places, count):
    out = []
    for j, (ref, place) in enumerate(zip(refs, places, strict=True)):
        size = ref.shape[1]
        first = pl.multiple_of(places[0] * count, count) if j == 0 else 0
        out.append(
            cps.start(
                ref.at[pl.ds(first, count)],
                dst.at[:, pl.ds(pl.multiple_of(place * size, size), size), :],
            )
        )
    return out


def places_of(pieces):
    if pieces == 1:
        return [0]
    me = lax.axis_index("tensor")
    return [me, 1 - me]


def split_store(own_ref, send_ref, at, value, axis, places):
    if send_ref is None:
        own_ref[at] = value.astype(own_ref.dtype)
        return
    half = value.shape[axis] // 2
    low = lax.slice_in_dim(value, 0, half, axis=axis)
    high = lax.slice_in_dim(value, half, 2 * half, axis=axis)
    first = places[0] == 0
    own_ref[at] = jnp.where(first, low, high).astype(own_ref.dtype)
    send_ref[at] = jnp.where(first, high, low).astype(send_ref.dtype)


def pack_store(own_ref, send_ref, at, value, axis, places):
    half = value.shape[axis] // 2
    low = lax.slice_in_dim(value, 0, half, axis=axis)
    high = lax.slice_in_dim(value, half, 2 * half, axis=axis)
    first = places[0] == 0
    own = jnp.where(first, low, high).astype(own_ref.dtype)
    send = jnp.where(first, high, low).astype(send_ref.dtype)
    rows = own.shape[0]
    for i in range(own.shape[1] // LANES):
        lanes = slice(i * LANES, (i + 1) * LANES)
        own_ref[at : at + rows, :] = own[:, lanes]
        send_ref[at : at + rows, :] = send[:, lanes]
        at += rows
    return at


def pack_kernel(n_vec, *refs):
    vectors, arrays = refs[:n_vec], refs[n_vec : n_vec + 2]
    vec, halves, sems = refs[n_vec + 2 :]
    cps = Copies(sems)
    count = halves.shape[1]
    first = pl.multiple_of((1 - lax.axis_index("tensor")) * count, count)
    copies = [
        cps.start(src.at[pl.ds(first, count)], halves.at[j])
        for j, src in enumerate(arrays)
    ]
    copies += [cps.start(v, vec.at[j]) for j, v in enumerate(vectors)]
    vec[n_vec:, :] = jnp.zeros((16 - n_vec, vec.shape[1]), f32)
    wait_all(copies)


def part(value, b, points):
    return value[b * points : (b + 1) * points]


def lane_part(value, b, points):
    return value[:, b * points : (b + 1) * points]


def norm_first(x, size, width):
    x3 = x.astype(f32).reshape(GROUPS, width, x.shape[1])
    mean = jnp.sum(jnp.sum(x3, axis=2, keepdims=True), axis=1, keepdims=True) / size
    off = x3 - mean
    var = jnp.sum(jnp.sum(off * off, axis=2, keepdims=True), axis=1, keepdims=True) / size
    rstd = lax.rsqrt(var + EPS)
    return (off * rstd).reshape(x.shape), rstd


def moments(value, width, size):
    mean = lane_groups(col_sum(value), width) / size
    off = value - mean
    return mean, lax.rsqrt(lane_groups(col_sum(off * off), width) / size + EPS)


def pipelined(stages, count):
    for s in stages:
        for b in range(count):
            s(b)


def front_kernel(pieces, count, *refs):
    it = iter(refs)

    def take(n):
        return [next(it) for _ in range(n)]

    x_in, g_in = take(pieces), take(1)
    w1_in, w2_in, pi_in, po_in, tw_in, vec_in = (take(pieces) for _ in range(6))
    if pieces == 2:
        x_in, g_in = [x_in[0], x_in[1].at[0]], [g_in[0], x_in[1].at[1]]
    steps_ref, table_ref = take(2)
    if pieces == 2:
        own, send = take(2)
    else:
        dw2_own, dpo_own, dpi_own = take(3)
    w1_out, w2_out, po_out, all_vec_out, x_out = take(5)
    gpad_out, sum_out, a1t_out, resid_out, gres_out, mix_out = take(6)
    stat_out, sums_out = take(2)
    w1, w2, po, vec, xin = take(5)
    gpad, sum_one, a1t, resid, gres, mix = take(6)
    stat, sums = take(2)
    gin, pi, tw, rows, apad, bpad = take(6)
    sems = next(it)

    cps = Copies(sems)
    places = places_of(pieces)
    chans, points = xin.shape[1], xin.shape[2]
    side = side_of(points)
    width = chans // GROUPS
    size = float(width * points)
    scale = chans ** (-0.5)
    images = range(count)

    x_cp = load_images(cps, x_in, xin, places, count)
    vec_cp = load_split(cps, vec_in, vec, 1, places)
    w1_cp = load_split(cps, w1_in, w1, 2, places)
    row_cp = []
    for b in images:
        step = steps_ref[places[0] * count + b]
        row_cp.append(
            cps.start(table_ref.at[pl.ds(pl.multiple_of(step // 16 * 16, 16), 16), :], rows.at[b])
        )
    tw_cp = load_split(cps, tw_in, tw, 1, places)
    w2_cp = load_split(cps, w2_in, w2, 1, places)
    pi_cp = load_split(cps, pi_in, pi, 2, places)
    po_cp = load_split(cps, po_in, po, 0, places)
    g_cp = load_images(cps, g_in, gin, places, count)

    zero_pads(apad, side, points)
    zero_pads(bpad, side, points)
    zero_pads(gpad, side, points)

    wait_all(vec_cp)
    vcols = jnp.transpose(vec[...])

    def col(j):
        return vcols[:, j : j + 1]

    def row(j):
        return vec[j : j + 1, :]

    wait_all(x_cp)
    for b in images:
        hat, _ = norm_first(xin[b], size, width)
        pre = hat * col(FIRST_GAIN) + col(FIRST_SHIFT)
        act = (pre * sigmoid(pre)).astype(bf16)
        a1t[b] = act
        put_moved(apad, b, jnp.transpose(act).astype(f32), side, points)

    wait_all(row_cp)
    wait_all(tw_cp)
    wait_all(w1_cp)
    wait_all(w2_cp)
    wait_all(pi_cp)
    wait_all(po_cp)
    wait_all(g_cp)
    outs = [cps.start(vec, all_vec_out), cps.start(xin, x_out), cps.start(w1, w1_out)]
    outs += [cps.start(a1t, a1t_out), cps.start(w2, w2_out), cps.start(po, po_out)]
    picked = []
    for b in images:
        step = steps_ref[places[0] * count + b]
        r = lax.broadcasted_iota(jnp.int32, (16, rows.shape[2]), 0)
        picked.append(col_sum(jnp.where(r == lax.rem(step, 16), rows[b].astype(f32), 0.0)))
    emb = jnp.concatenate(picked + picked[:1] * (8 - count), axis=0)
    time_add = nn((emb * sigmoid(emb)).astype(bf16), tw[...]) + row(TIME_BIAS) + row(FIRST_BIAS)

    stats2, stats3 = [], []
    act_t = [None] * count

    def conv_one(b):
        lhs = jnp.concatenate(taps(apad, b, 1, side, points), axis=1)
        sum_one[b] = nn(lhs, w1[...].reshape(9 * chans, chans)) + time_add[b : b + 1]

    def norm_two(b):
        mean, rstd = moments(sum_one[b], width, size)
        stats2.append((mean, rstd))
        hat = (sum_one[b] - mean) * rstd
        pre = hat * row(SECOND_GAIN) + row(SECOND_SHIFT)
        act = pre * sigmoid(pre)
        act_t[b] = jnp.transpose(act.astype(bf16))
        put_moved(bpad, b, act, side, points)

    def conv_two(b):
        lhs = jnp.concatenate(taps(bpad, b, 1, side, points), axis=1)
        val = nn(lhs, w2[...].reshape(9 * chans, chans)) + row(SECOND_BIAS)
        resid[b] = val + jnp.transpose(xin[b]).astype(f32)

    normed = []

    def norm_three(b):
        mean, rstd = moments(resid[b], width, size)
        stats3.append((mean, rstd))
        hat = (resid[b] - mean) * rstd
        normed.append((hat * row(THIRD_GAIN) + row(THIRD_SHIFT)).astype(bf16))

    pipelined([conv_one, norm_two, conv_two, norm_three], count)
    outs += [cps.start(sum_one, sum_out), cps.start(resid, resid_out)]
    stat[0:count, :] = jnp.concatenate([m for m, _ in stats2], axis=0)
    stat[count : 2 * count, :] = jnp.concatenate([r for _, r in stats2], axis=0)
    outs.append(cps.start(stat, stat_out))

    pi_row = jnp.concatenate([pi[0], pi[1], pi[2]], axis=1)
    pi_t = jnp.concatenate([jnp.transpose(pi[1]), jnp.transpose(pi[2])], axis=0)
    zero = jnp.zeros((1, chans), f32)
    normed_t = jnp.concatenate([jnp.transpose(v) for v in normed], axis=1)
    normed = jnp.concatenate(normed, axis=0)
    lin = nn(normed, pi_row)
    q = (lin[:, :chans] + row(QUERY_BIAS)).astype(bf16)
    k = lin[:, chans : 2 * chans].astype(bf16)
    v = (lin[:, 2 * chans :] + row(VALUE_BIAS)).astype(bf16)
    lin_t = nn(pi_t, normed_t)
    kt = lin_t[:chans].astype(bf16)
    vt = (lin_t[chans:] + col(VALUE_BIAS)).astype(bf16)
    grad_all = jnp.concatenate([gin[b] for b in images], axis=1)
    grad_mixed = nn(po[...], grad_all).astype(bf16)
    scores = [nt(part(k, b, points), part(q, b, points)) for b in images]
    grad_w = [nn(part(v, b, points), lane_part(grad_mixed, b, points)) for b in images]
    weights, grad_s = [], []
    for b in images:
        top = scores[b] * scale
        expo = jnp.exp(top - jnp.max(top, axis=0, keepdims=True))
        probs = expo * (1.0 / jnp.sum(expo, axis=0, keepdims=True))
        weights.append(probs.astype(bf16))
        inner = probs * grad_w[b]
        grad_s.append((inner - probs * jnp.sum(inner, axis=0, keepdims=True)).astype(bf16))
    mixed = []
    for b in images:
        mixed.append(nn(lane_part(vt, b, points), weights[b]).astype(bf16))
        mix[b] = mixed[b]
    outs.append(cps.start(mix, mix_out))
    grad_qt = [nn(lane_part(kt, b, points), grad_s[b]) * scale for b in images]
    grad_q = [jnp.transpose(t.astype(bf16)) for t in grad_qt]
    grad_k = [(nn(grad_s[b], part(q, b, points)) * scale).astype(bf16) for b in images]
    grad_v = [nt(weights[b], lane_part(grad_mixed, b, points)).astype(bf16) for b in images]
    lin_grad = jnp.concatenate(
        [jnp.concatenate([grad_q[b], grad_k[b], grad_v[b]], axis=1) for b in images], axis=0
    )
    qb_grad = col_sum(sum(t.astype(f32) for t in grad_q))
    vb_grad = col_sum(sum(t.astype(f32) for t in grad_v))
    dpo = nt(jnp.concatenate(mixed, axis=1), grad_all)
    grad_normed = nt(lin_grad, pi_row)

    gain3, shift3, means = [], [], []
    for b in images:
        hat = (resid[b] - stats3[b][0]) * stats3[b][1]
        val = part(grad_normed, b, points)
        gain3.append(col_sum(val * hat))
        shift3.append(col_sum(val))
        both = jnp.concatenate([shift3[b], gain3[b]], axis=0) * row(THIRD_GAIN)
        means.append(lane_groups(both, width) / size)
    sb_grad, ob_grad = zero, zero
    for b in images:
        hat = (resid[b] - stats3[b][0]) * stats3[b][1]
        h = part(grad_normed, b, points) * row(THIRD_GAIN)
        grad_out = jnp.transpose(gin[b]).astype(f32)
        ob_grad = ob_grad + col_sum(grad_out)
        val = grad_out + stats3[b][1] * (h - means[b][0:1] - hat * means[b][1:2])
        gres[b] = val
        sb_grad = sb_grad + col_sum(val)
        put_moved(gpad, b, val, side, points)
        outs.append(cps.start(gres.at[b], gres_out.at[b]))
        outs.append(cps.start(gpad.at[:, b], gpad_out.at[:, b]))
    lane = lax.broadcasted_iota(jnp.int32, (1, chans), 1)
    stamp = jnp.zeros((1, chans), f32)
    for b in images:
        step = jnp.full((1, chans), steps_ref[places[0] * count + b], jnp.int32)
        stamp = jnp.where(lane == b, (step >> 5).astype(f32), stamp)
        stamp = jnp.where(lane == LANES // 2 + b, (step & 31).astype(f32), stamp)
    sums[...] = jnp.concatenate(
        [sb_grad, sum(gain3), sum(shift3), qb_grad, vb_grad, ob_grad, stamp, zero], axis=0
    )
    outs.append(cps.start(sums, sums_out))

    dpi = nn(normed_t, lin_grad)
    at = 0
    if pieces == 2:
        at = pack_store(own, send, at, dpo, 0, places)
        for j in range(3):
            at = pack_store(own, send, at, dpi[:, j * chans : (j + 1) * chans], 1, places)
    else:
        dpo_own[...] = dpo
        for j in range(3):
            dpi_own[j] = dpi[:, j * chans : (j + 1) * chans]

    a_all = jnp.concatenate(act_t, axis=1)
    moved = [taps(gpad, b, -1, side, points) for b in images]
    for tap in range(9):
        val = nn(a_all, jnp.concatenate([moved[b][tap] for b in images], axis=0))
        if pieces == 2:
            at = pack_store(own, send, at, val, 0, places)
        else:
            dw2_own[tap] = val

    wait_all(outs)


def copy_rows(cps, pairs, start, end):
    rows = slice(start, end)
    return [cps.start(src.at[rows], dst.at[rows]) for src, dst in pairs]


def back_kernel(pieces, count, *refs):
    it = iter(refs)

    def take(n):
        return [next(it) for _ in range(n)]

    kept = take(13)
    if pieces == 2:
        own, send_out, block_own_out, block_send_out, image_own_out, image_send_out = take(6)
    else:
        own, block_own_out, image_own_out = take(3)
        block_send_out = image_send_out = None
    small = next(it)
    w1, w2, po, vec, xin, gpad, sum_one, a1t, resid, gres, mix, stat, front_sums = take(13)
    if pieces == 2:
        send, block_own, block_send, image_own, image_send = take(5)
    else:
        block_own, image_own = take(2)
        block_send = image_send = None
    hpad, back, first_hat, first_slope, sems = take(5)
    cps = Copies(sems)
    places = places_of(pieces)
    points, chans = sum_one.shape[1], sum_one.shape[2]
    side = side_of(points)
    width = chans // GROUPS
    size = float(width * points)
    images = range(count)

    w1_in, w2_in, po_in, vec_in, x_in, gpad_in, sum_in, a1t_in, resid_in, gres_in, mix_in = kept[:11]
    early = [(vec_in, vec), (x_in, xin)]
    early = [cps.start(src, dst) for src, dst in early]
    w2_cp = cps.start(w2_in, w2)
    gpad_cp = [cps.start(gpad_in.at[:, b], gpad.at[:, b]) for b in images]
    small_cp = [(kept[11], stat), (kept[12], front_sums)]
    small_cp = [cps.start(src, dst) for src, dst in small_cp]
    sum_cp = cps.start(sum_in, sum_one)
    a1t_cp = cps.start(a1t_in, a1t)
    later = [(w1_in, w1), (po_in, po), (resid_in, resid), (gres_in, gres), (mix_in, mix)]
    later = [cps.start(src, dst) for src, dst in later]

    def row(j):
        return vec[j : j + 1, :]

    zero_pads(hpad, side, points)
    wait_all(early)
    vcols = jnp.transpose(vec[...])

    def col(j):
        return vcols[:, j : j + 1]

    first_rstd = []
    for b in images:
        hat, rstd = norm_first(xin[b], size, width)
        first_rstd.append(jnp.broadcast_to(rstd, (GROUPS, width, 1)).reshape(chans, 1))
        pre = hat * col(FIRST_GAIN) + col(FIRST_SHIFT)
        first_hat[b] = hat
        first_slope[b] = silu_slope(pre, sigmoid(pre))

    w2_cp.wait()
    wait_all(gpad_cp)
    sum_cp.wait()
    wait_all(small_cp)
    w2_cols = jnp.concatenate([w2[k] for k in range(9)], axis=1)
    gain, shift_g, times = [], [], []

    def conv_back(b):
        back[b] = nt(jnp.concatenate(taps(gpad, b, -1, side, points), axis=1), w2_cols)

    def norm_back(b):
        mean, rstd = stat[b : b + 1, :], stat[count + b : count + b + 1, :]
        hat = (sum_one[b] - mean) * rstd
        pre = hat * row(SECOND_GAIN) + row(SECOND_SHIFT)
        val = back[b] * silu_slope(pre, sigmoid(pre))
        gain.append(col_sum(val * hat))
        shift_g.append(col_sum(val))
        both = jnp.concatenate([shift_g[b], gain[b]], axis=0) * row(SECOND_GAIN)
        both = lane_groups(both, width) / size
        val = rstd * (val * row(SECOND_GAIN) - both[0:1] - hat * both[1:2])
        times.append(col_sum(val))
        put_moved(hpad, b, val, side, points)

    pipelined([conv_back, norm_back], count)
    a1t_cp.wait()
    wait_all(later)
    outs = []


    def put_out(own_ref, send_ref, own_dst, send_dst, b, val):
        split_store(own_ref, send_ref, b, val, 0, places)
        outs.append(cps.start(own_ref.at[b], own_dst.at[b]))
        if send_ref is not None:
            outs.append(cps.start(send_ref.at[b], send_dst.at[b]))

    proj = nn(jnp.transpose(po[...]), jnp.concatenate([mix[b] for b in images], axis=1))
    a_all = jnp.concatenate([a1t[b] for b in images], axis=1)
    moved = [taps(hpad, b, -1, side, points) for b in images]
    at = 0
    for tap in range(9):
        val = nn(a_all, jnp.concatenate([moved[b][tap] for b in images], axis=0))
        if pieces == 2:
            at = pack_store(own, send, at, val, 1, places)
        else:
            own[tap] = val
        if tap % 2 == 1 and tap // 2 < count:
            b = tap // 2
            val = jnp.transpose(resid[b]) + lane_part(proj, b, points) + col(OUTPUT_BIAS)
            split_store(block_own, block_send, b, val, 0, places)
    if pieces == 2:
        outs += copy_rows(cps, [(send, send_out)], 0, at)
        outs.append(cps.start(block_send, block_send_out))
    outs.append(cps.start(block_own, block_own_out))

    w1_cols = jnp.concatenate([w1[k] for k in range(9)], axis=1)
    zero = jnp.zeros((chans, 1), f32)
    gain_sum, shift_sum = [zero], [zero]
    first_back = [None] * count

    def groups(v):
        total = jnp.sum(v.reshape(GROUPS, width, 1), axis=1, keepdims=True) / size
        return jnp.broadcast_to(total, (GROUPS, width, 1)).reshape(chans, 1)

    def conv_first(b):
        first_back[b] = nt(w1_cols, jnp.concatenate(taps(hpad, b, -1, side, points), axis=1))

    def norm_first_back(b):
        hat, rstd = first_hat[b], first_rstd[b]
        val = first_back[b] * first_slope[b]
        gain = jnp.sum(val * hat, axis=1, keepdims=True)
        shift = jnp.sum(val, axis=1, keepdims=True)
        gain_sum[0] = gain_sum[0] + gain
        shift_sum[0] = shift_sum[0] + shift
        first_mean = groups(shift * col(FIRST_GAIN))
        second_mean = groups(gain * col(FIRST_GAIN))
        val = rstd * (val * col(FIRST_GAIN) - first_mean - hat * second_mean)
        val = val + jnp.transpose(gres[b])
        put_out(image_own, image_send, image_own_out, image_send_out, b, val)

    pipelined([conv_first, norm_first_back], count)

    lane = lax.broadcasted_iota(jnp.int32, (chans, LANES), 1)
    both = jnp.where(lane == 0, gain_sum[0], 0.0) + jnp.where(lane == 1, shift_sum[0], 0.0)
    both = jnp.transpose(both)
    rows = [front_sums[j : j + 1, :] for j in range(6)]
    rows += [sum(gain), sum(shift_g), sum(times), both[0:1], both[1:2]]
    flat = []
    for r in rows + times:
        flat += [r[:, i * LANES : (i + 1) * LANES] for i in range(chans // LANES)]
    flat.append(front_sums[6:7, :LANES])
    flat += [jnp.zeros((1, LANES), f32)] * (BLOCK - len(flat))
    small[...] = jnp.concatenate(flat, axis=0).astype(bf16)
    wait_all(outs)


def put_quarters(quarters, flat):
    me = lax.axis_index("batch") & 3
    rows = quarters[0].shape[0]
    if len(quarters) == 4:
        parts = [(j, ref, 0) for j, ref in enumerate(quarters)]
    else:
        odd = lax.axis_index("tensor") & 1
        mine, first, both = quarters
        parts = [(0, mine, 0), (1 + odd, first, 0), (2 - odd, both, 0), (3, both, rows)]
    for j, ref, at in parts:
        flat[pl.ds(pl.multiple_of((me ^ j) * rows, 16), rows), :] = ref[at : at + rows, :]


def unpack_first_kernel(*refs):
    quarters = refs[:-4]
    dw1_out, flat, dw1, sems = refs[-4:]
    cps = Copies(sems)
    put_quarters(quarters, flat)
    outs = []
    chans = dw1.shape[1]
    for tap in range(dw1.shape[0]):
        dw1[tap] = flat[tap * chans : (tap + 1) * chans, :].astype(f32)
        if tap % 3 == 2:
            part = slice(tap - 2, tap + 1)
            outs.append(cps.start(dw1.at[part], dw1_out.at[part]))
    wait_all(outs)


def unpack_second_kernel(*refs):
    quarters = refs[:-8]
    dw2_out, dpo_out, dpi_out, flat, dw2, dpo, dpi, sems = refs[-8:]
    cps = Copies(sems)
    put_quarters(quarters, flat)
    outs = []
    chans = dpi.shape[1]
    half = chans // 2
    for i in range(2):
        dpo[:, i * LANES : (i + 1) * LANES] = flat[i * half : (i + 1) * half, :].astype(f32)
    outs.append(cps.start(dpo, dpo_out))
    at = chans
    for j in range(3):
        dpi[j] = flat[at : at + chans, :].astype(f32)
        at += chans
    outs.append(cps.start(dpi, dpi_out))
    for tap in range(dw2.shape[0]):
        for i in range(2):
            dw2[tap, :, i * LANES : (i + 1) * LANES] = flat[at : at + half, :].astype(f32)
            at += half
        if tap % 3 == 2:
            part = slice(tap - 2, tap + 1)
            outs.append(cps.start(dw2.at[part], dw2_out.at[part]))
    wait_all(outs)


def swap(value, axis, size, bit):
    return lax.ppermute(value, axis, [(i, i ^ bit) for i in range(size)])


def near_parts(part):
    me = lax.axis_index("batch") & 3
    return [part(me ^ j).astype(bf16) for j in range(1, 4)]


def together(*groups):
    return [list(g) for g in lax.optimization_barrier(tuple(tuple(g) for g in groups))]


def send_near(sent, batch):
    return [swap(v, "batch", batch, j + 1) for j, v in enumerate(sent)]


def sum_near(got, part):
    total = part(lax.axis_index("batch") & 3).astype(f32)
    for g in got:
        total = total + g.astype(f32)
    return total.astype(bf16)


def far_steps(batch):
    return batch.bit_length() - 3


def send_far(piece, extra, step, batch):
    steps = far_steps(batch)
    mine = piece if extra is None else jnp.concatenate([piece, extra], axis=0)
    tensor = lax.axis_size("tensor")
    pairs = []
    for i in range(batch):
        for core in range(tensor):
            bit = 4 << (step if core % 2 == 0 else steps - 1 - step)
            pairs.append((i * tensor + core, (i ^ bit) * tensor + core))
    return lax.ppermute(mine, ("batch", "tensor"), pairs)


def sum_far(piece, extra, got):
    rows = piece.shape[0]
    piece = (piece.astype(f32) + got[:rows].astype(f32)).astype(bf16)
    if extra is not None:
        extra = jnp.concatenate([extra, got[rows:]], axis=0)
    return piece, extra


def gather_near(piece, batch):
    return [piece] + [swap(piece, "batch", batch, j) for j in range(1, 4)]


def plane_bit(step, core):
    return 1 if step == core % 2 else 2


def cross(value, step, batch):
    tensor = lax.axis_size("tensor")
    pairs = []
    for i in range(batch):
        for core in range(tensor):
            pairs.append((i * tensor + core, (i ^ plane_bit(step, core)) * tensor + core))
    return lax.ppermute(value, ("batch", "tensor"), pairs)


def by_difference(mine, first, both):
    rows = mine.shape[0]
    odd = (lax.axis_index("tensor") & 1) == 1
    near, far = both[:rows], both[rows:]
    return [mine, jnp.where(odd, near, first), jnp.where(odd, first, near), far]


def in_order(pieces):
    me = lax.axis_index("batch")
    parts = jnp.stack(pieces, axis=0)
    parts = parts.reshape((2, 2) + parts.shape[1:])
    parts = jnp.where((me & 1) == 1, jnp.flip(parts, axis=1), parts)
    parts = jnp.where((me & 2) == 2, jnp.flip(parts, axis=0), parts)
    return parts.reshape((-1, LANES))


def unpack(flat, shapes):
    out = []
    at = 0
    for shape in shapes:
        n = math.prod(shape) // 128
        out.append(flat[at : at + n].reshape(shape).astype(f32))
        at += n
    return out


def per_device(
    batch,
    tensor,
    images,
    timesteps,
    embed_table,
    first_gain,
    first_shift,
    first_conv,
    first_bias,
    time_weight,
    time_bias,
    second_gain,
    second_shift,
    second_conv,
    second_bias,
    third_gain,
    third_shift,
    project_in,
    query_bias,
    value_bias,
    project_out,
    output_bias,
    cotangent,
):
    per_batch, local, points = images.shape
    chans = local * tensor
    count = per_batch // tensor
    table_rows, embed = embed_table.shape
    pieces = 2 if tensor == 2 else 1
    me = lax.axis_index("tensor")
    vectors = [
        first_gain,
        first_shift,
        first_bias,
        time_bias,
        second_gain,
        second_shift,
        second_bias,
        third_gain,
        third_shift,
        query_bias,
        value_bias,
        output_bias,
    ]
    def in_hbm(array):
        return pltpu.with_memory_space_constraint(array, pltpu.HBM)

    n_vec = len(vectors)
    if pieces == 2:
        vec, halves = pl.pallas_call(
            functools.partial(pack_kernel, n_vec),
            out_shape=[
                jax.ShapeDtypeStruct((16, local), f32),
                jax.ShapeDtypeStruct((2, count, local, points), bf16),
            ],
            in_specs=[ANY] * (n_vec + 2),
            out_specs=[VMEM] * 2,
            scratch_shapes=[pltpu.SemaphoreType.DMA((n_vec + 2,))],
            compiler_params=pltpu.CompilerParams(vmem_limit_bytes=4 * MIB),
            name="pack",
        )(*(in_hbm(v) for v in vectors + [images, cotangent]))
    else:
        vec = jnp.stack(vectors + [output_bias] * 4, axis=0)

    def whole(array, axis):
        if pieces == 2:
            return [array, swap(array, "tensor", 2, 1)]
        return [lax.all_gather(array, "tensor", axis=axis, tiled=True)]

    if pieces == 2:
        x_in, g_in = [images, swap(halves, "tensor", 2, 1)], [cotangent]
    else:
        x_in, g_in = (
            [lax.all_to_all(v, "tensor", 0, 1, tiled=True)] for v in (images, cotangent)
        )
    vec_in = whole(vec, 1)
    tw_in = whole(time_weight, 1)
    w1_in = whole(first_conv, 2)
    w2_in = whole(second_conv, 1)
    pi_in = whole(project_in, 2)
    po_in = whole(project_out, 0)
    my_steps = timesteps if pieces == 2 else lax.dynamic_slice_in_dim(timesteps, me * count, count)

    side = side_of(points)
    image_b = (count, chans, points)
    image_p = (count, points, chans)
    pads = (3, count, points + 2 * side, chans)

    def shape(s, d):
        return jax.ShapeDtypeStruct(s, d)

    def params(mib):
        return pltpu.CompilerParams(vmem_limit_bytes=mib * MIB)

    def cost(units, moved):
        flops = 2 * units * count * points * chans * chans
        return pl.CostEstimate(flops=flops, bytes_accessed=moved, transcendentals=0)

    half_b = 9 * chans * chans // 2 // LANES
    half_a = half_b + 4 * chans * chans // 2 // LANES
    if pieces == 2:
        grads_a = [pltpu.VMEM((half_a, LANES), bf16)] * 2
        grads_b = [pltpu.VMEM((half_b, LANES), bf16), pltpu.HBM((half_b, LANES), bf16)]
    else:
        grads_a = [shape((9, chans, chans), f32), shape((chans, chans), f32)]
        grads_a.append(shape((3, chans, chans), f32))
        grads_b = [shape((9, chans, chans), f32)]
    n_grad = len(grads_a)
    steps_in = in_hbm(my_steps)
    kept = [
        ((9, chans, chans), bf16),
        ((9, chans, chans), bf16),
        ((chans, chans), bf16),
        ((16, chans), f32),
        (image_b, bf16),
        (pads, bf16),
        (image_p, f32),
        (image_b, bf16),
        (image_p, f32),
        (image_p, f32),
        (image_b, bf16),
        ((2 * count, chans), f32),
        ((8, chans), f32),
    ]
    out_a = ANY if pieces == 2 else VMEM
    scratch_a = []

    front = pl.pallas_call(
        functools.partial(front_kernel, pieces, count),
        out_shape=grads_a
        + [pltpu.HBM(*v) for v in kept],
        in_specs=[ANY, VMEM][:pieces] + [ANY] + [ANY, VMEM][:pieces] * 6 + [SMEM, ANY],
        out_specs=[VMEM] * n_grad + [ANY] * len(kept),
        scratch_shapes=scratch_a
        + [pltpu.VMEM(*v) for v in kept]
        + [
            pltpu.VMEM(image_b, bf16),
            pltpu.VMEM((3, chans, chans), bf16),
            pltpu.VMEM((embed, chans), bf16),
            pltpu.VMEM((count, 16, embed), bf16),
            pltpu.VMEM(pads, bf16),
            pltpu.VMEM(pads, bf16),
            pltpu.SemaphoreType.DMA((8 * pieces + 3 * count + 19,)),
        ],
        compiler_params=params(28),
        cost_estimate=cost(54, 12 << 20),
        name="front",
    )(
        *(
            place(v)
            for pair in (x_in, g_in, w1_in, w2_in, pi_in, po_in, tw_in, vec_in)
            for v, place in zip(pair, (in_hbm, lambda v: v))
        ),
        steps_in,
        in_hbm(embed_table),
    )
    sums_a = front[:n_grad]
    kept_now = list(front[n_grad:])

    def quarters(sums, axes, beside=None):
        if pieces == 2:
            got = swap(sums[1], "tensor", 2, 1)
            if beside is not None:
                (got,), (beside,) = together([got], [beside])
            rows = got.shape[0] // 4
            own4, got4 = (v.reshape(4, rows, LANES) for v in (sums[0], got))

            def part(q):
                pair = [lax.dynamic_index_in_dim(v, q, 0, False).astype(f32) for v in (own4, got4)]
                return pair[0] + pair[1]

            return part, beside
        done = [
            lax.psum_scatter(v, "tensor", scatter_dimension=axis, tiled=True)
            for v, axis in zip(sums, axes, strict=True)
        ]
        flat = jnp.concatenate([v.reshape(-1, LANES) for v in done], axis=0)
        flat = jnp.pad(flat, ((0, -flat.shape[0] % 64), (0, 0)))
        rows = flat.shape[0] // 4
        flat = flat.reshape(4, rows, LANES)
        return (lambda q: lax.dynamic_index_in_dim(flat, q, 0, False)), beside

    part_a, _ = quarters(sums_a, (1, 0, 2))
    sent_a = near_parts(part_a)

    kept_now[-2:], sent_a = together(kept_now[-2:], sent_a)
    got_a = send_near(sent_a, batch)

    half = (count, chans // 2, points)
    if pieces == 2:
        outs_b = grads_b + [pltpu.HBM(half, f32), pltpu.HBM(half, bf16)] * 2
        scratch_b = [pltpu.VMEM(v.shape, v.dtype) for v in outs_b[1:]]
    else:
        outs_b = grads_b + [pltpu.HBM(image_b, f32)] * 2
        scratch_b = [pltpu.VMEM(image_b, f32)] * 2
    *outs_b, block = pl.pallas_call(
        functools.partial(back_kernel, pieces, count),
        out_shape=outs_b + [pltpu.VMEM((BLOCK, LANES), bf16)],
        in_specs=[ANY] * len(kept),
        out_specs=[VMEM, out_a][:pieces] + [ANY] * (2 * pieces) + [VMEM],
        scratch_shapes=[pltpu.VMEM(*v) for v in kept]
        + scratch_b
        + [
            pltpu.VMEM(pads, bf16),
            pltpu.VMEM(image_p, f32),
            pltpu.VMEM(image_b, f32),
            pltpu.VMEM(image_b, f32),
            pltpu.SemaphoreType.DMA((16 + 3 * count,)),
        ],
        compiler_params=params(28),
        cost_estimate=cost(33, 12 << 20),
        name="back",
    )(*(in_hbm(v) for v in kept_now))
    sums_b, block_part, image_grad = outs_b[:pieces], outs_b[pieces : 2 * pieces], outs_b[2 * pieces :]
    got_a, sums_b, (block,) = together(got_a, sums_b, [block])
    piece_a = sum_near(got_a, part_a)
    steps = far_steps(batch)
    far_a = send_far(piece_a, None, 0, batch) if steps > 0 else None
    part_b, piece_a = quarters(sums_b, (2,), piece_a)
    sent_b = near_parts(part_b)
    got_b = send_near([jnp.concatenate([v, block], axis=0) for v in sent_b], batch)
    if steps > 0:
        piece_a, _ = sum_far(piece_a, None, far_a)
    if steps > 1:
        far_a = send_far(piece_a, None, 1, batch)
    got_b, (piece_a,) = together(got_b, [piece_a])
    rows_b = sent_b[0].shape[0]
    blocks = jnp.concatenate([block] + [g[rows_b:] for g in got_b], axis=0)
    piece_b = sum_near([g[:rows_b] for g in got_b], part_b)
    for step in range(1, steps):
        if step > 1:
            far_a = send_far(piece_a, None, step, batch)
        piece_a, _ = sum_far(piece_a, None, far_a)
    if steps > 0:
        far_b = send_far(piece_b, blocks, 0, batch)
    block_part, image_grad, (piece_b,) = together(block_part, image_grad, [piece_b])

    def placed(own, send):
        if pieces == 2:
            got = swap(send, "tensor", 2, 1).astype(f32)
            low = jnp.where(me == 0, own, got)
            high = jnp.where(me == 0, got, own)
            return jnp.concatenate([low, high], axis=0)
        return lax.all_to_all(own, "tensor", 1, 0, tiled=True)

    block_out = placed(block_part[0], block_part[-1])
    images_grad = placed(image_grad[0], image_grad[-1])

    first_a = cross(piece_a, 0, batch)
    both_a = cross(jnp.concatenate([piece_a, first_a], axis=0), 1, batch)
    for step in range(steps):
        if step > 0:
            far_b = send_far(piece_b, blocks, step, batch)
            (far_b,), (first_a,) = together([far_b], [first_a])
        piece_b, blocks = sum_far(piece_b, blocks, far_b)
    got_a = [piece_a, first_a, both_a]
    got_b = gather_near(piece_b, batch)

    if pieces == 2:

        def unpacked(kernel, name, got, rows, shapes):
            outs = [shape(v, f32) for v in shapes]
            return pl.pallas_call(
                kernel,
                out_shape=outs,
                in_specs=[VMEM] * len(got),
                out_specs=[ANY] * len(outs),
                scratch_shapes=[pltpu.VMEM((rows, LANES), bf16)]
                + [pltpu.VMEM(v.shape, v.dtype) for v in outs]
                + [pltpu.SemaphoreType.DMA((len(outs) + 2,))],
                compiler_params=params(12),
                name=name,
            )(*got)

        second_conv_grad, project_out_grad, project_in_grad = unpacked(
            unpack_second_kernel,
            "unpack_second",
            got_a,
            half_a,
            [(9, local, chans), (local, chans), (3, chans, local)],
        )
        got_b, (second_conv_grad,) = together(got_b, [second_conv_grad])
        (first_conv_grad,) = unpacked(
            unpack_first_kernel, "unpack_first", got_b, half_b, [(9, chans, local)]
        )
    else:
        second_conv_grad, project_out_grad, project_in_grad = unpack(
            in_order(by_difference(*got_a)), [(9, local, chans), (local, chans), (3, chans, local)]
        )
        (first_conv_grad,) = unpack(in_order(got_b), [(9, chans, local)])

    if pieces == 2:
        blocks = jnp.concatenate([blocks, swap(blocks, "tensor", 2, 1)], axis=0)
        two = blocks.reshape(2, batch, BLOCK, LANES)
        blocks = jnp.where(me == 0, two, jnp.flip(two, axis=0))
    else:
        blocks = lax.all_gather(blocks, "tensor", axis=0, tiled=True)
    blocks = blocks.reshape(batch * tensor, BLOCK, LANES)
    wide = chans // LANES
    n_sum = 11 * wide
    sums = jnp.sum(blocks[:, :n_sum].astype(f32), axis=0).reshape(11, chans)
    sums = jnp.concatenate([sums, sums[8:9]], axis=0)
    mine = lax.dynamic_slice_in_dim(sums, me * local, local, axis=1)
    all_times = blocks[:, n_sum : n_sum + wide * count].reshape(-1, chans)
    stamps = blocks[:, n_sum + wide * count].astype(jnp.int32)
    all_steps = stamps[:, :count] * 32 + stamps[:, LANES // 2 : LANES // 2 + count]
    all_steps = all_steps.reshape(-1)
    one_hot = (all_steps[:, None] == jnp.arange(table_rows, dtype=jnp.int32)[None, :]).astype(bf16)
    emb = nn(one_hot, embed_table)
    sig = sigmoid(emb)
    act = (emb * sig).astype(bf16)
    my_times = lax.dynamic_slice_in_dim(all_times, me * local, local, axis=1)
    time_weight_grad = lax.dot_general(
        act, my_times, (((0,), (0,)), ((), ())), preferred_element_type=f32
    )
    if pieces == 2:
        tw = jnp.where(
            me == 0, jnp.concatenate(tw_in, axis=1), jnp.concatenate(tw_in[::-1], axis=1)
        )
    else:
        tw = tw_in[0]
    grad_emb = (nt(all_times, tw) * silu_slope(emb, sig)).astype(bf16)
    table_grad = lax.dot_general(
        one_hot, grad_emb, (((0,), (0,)), ((), ())), preferred_element_type=f32
    )
    return (
        block_out,
        images_grad,
        table_grad,
        mine[9],
        mine[10],
        first_conv_grad,
        mine[8],
        time_weight_grad,
        mine[11],
        mine[6],
        mine[7],
        second_conv_grad,
        mine[0],
        mine[1],
        mine[2],
        project_in_grad,
        mine[3],
        mine[4],
        project_out_grad,
        mine[5],
    )


def solution(mesh):
    in_specs = (
        P("batch", "tensor", None),
        P("batch"),
        P(),
        P("tensor"),
        P("tensor"),
        P(None, None, "tensor"),
        P("tensor"),
        P(None, "tensor"),
        P("tensor"),
        P("tensor"),
        P("tensor"),
        P(None, "tensor", None),
        P("tensor"),
        P("tensor"),
        P("tensor"),
        P(None, None, "tensor"),
        P("tensor"),
        P("tensor"),
        P("tensor", None),
        P("tensor"),
        P("batch", "tensor", None),
    )
    out_specs = (
        P("batch", "tensor", None),
        P("batch", "tensor", None),
        P(),
        P("tensor"),
        P("tensor"),
        P(None, None, "tensor"),
        P("tensor"),
        P(None, "tensor"),
        P("tensor"),
        P("tensor"),
        P("tensor"),
        P(None, "tensor", None),
        P("tensor"),
        P("tensor"),
        P("tensor"),
        P(None, None, "tensor"),
        P("tensor"),
        P("tensor"),
        P("tensor", None),
        P("tensor"),
    )
    sizes = dict(mesh.shape)
    return jax.shard_map(
        functools.partial(per_device, sizes["batch"], sizes["tensor"]),
        mesh=mesh,
        in_specs=in_specs,
        out_specs=out_specs,
        check_vma=False,
    )
```

```python
import functools
import math

import jax
import jax.numpy as jnp
from jax import lax
from jax.experimental import pallas as pl
from jax.experimental.pallas import tpu as pltpu
from jax.sharding import PartitionSpec as P

GROUPS = 32
LANES = 128
BLOCK = 32
EPS = 1e-06
MIB = 1024 * 1024
ANY = pl.BlockSpec(memory_space=pl.ANY)
VMEM = pl.BlockSpec(memory_space=pltpu.VMEM)
SMEM = pl.BlockSpec(memory_space=pltpu.SMEM)
f32 = jnp.float32
bf16 = jnp.bfloat16

(
    FIRST_GAIN,
    FIRST_SHIFT,
    FIRST_BIAS,
    TIME_BIAS,
    SECOND_GAIN,
    SECOND_SHIFT,
    SECOND_BIAS,
    THIRD_GAIN,
    THIRD_SHIFT,
    QUERY_BIAS,
    VALUE_BIAS,
    OUTPUT_BIAS,
) = range(12)


def nn(a, b):
    return lax.dot_general(a, b, (((1,), (0,)), ((), ())), preferred_element_type=f32)


def nt(a, b):
    return lax.dot_general(a, b, (((1,), (1,)), ((), ())), preferred_element_type=f32)


def sigmoid(v):
    return 0.5 * jnp.tanh(0.5 * v) + 0.5


def silu_slope(v, sig):
    return sig * (1.0 + v * (1.0 - sig))


def col_sum(v):
    return jnp.sum(v, axis=0, keepdims=True)


def lane_groups(v, width):
    lanes = v.shape[1]
    lane = lax.broadcasted_iota(jnp.int32, v.shape, 1)
    step = 1
    while step < width:
        up = pltpu.roll(v, step, 1)
        down = pltpu.roll(v, lanes - step, 1)
        v = v + jnp.where((lane & step) != 0, up, down)
        step *= 2
    return v


def zero_pads(pad_ref, side, points):
    images, chans = pad_ref.shape[1], pad_ref.shape[3]
    for d in range(3):
        for b in range(images):
            pad_ref[d, b, 0:side, :] = jnp.zeros((side, chans), bf16)
            pad_ref[d, b, side + points : 2 * side + points, :] = jnp.zeros((side, chans), bf16)


def put_moved(pad_ref, b, value, side, points):
    chans = value.shape[1]
    column = lax.broadcasted_iota(jnp.int32, (side, chans), 0)
    for d, edge in ((0, 0), (1, None), (2, side - 1)):
        moved = value
        if edge is not None:
            moved = pltpu.roll(value, (1 - d) % points, 0).reshape(side, side, chans)
            moved = jnp.where((column == edge)[None], 0.0, moved).reshape(points, chans)
        pad_ref[d, b, side : side + points, :] = moved.astype(bf16)


def taps(pad_ref, b, sign, side, points):
    out = []
    for dr in (-1, 0, 1):
        for dc in (-1, 0, 1):
            top = side + sign * dr * side
            out.append(pad_ref[1 + sign * dc, b, top : top + points, :])
    return out


class Copies:
    def __init__(self, sems):
        self.sems = sems
        self.used = 0

    def start(self, src, dst):
        copy = pltpu.make_async_copy(src, dst, self.sems.at[self.used])
        self.used += 1
        copy.start()
        return copy


def wait_all(copies):
    for c in copies:
        c.wait()


def side_of(points):
    return math.isqrt(points)


def load_split(cps, refs, dst, axis, places):
    out = []
    for ref, place in zip(refs, places, strict=True):
        size = ref.shape[axis]
        idx = [slice(None)] * len(ref.shape)
        idx[axis] = pl.ds(pl.multiple_of(place * size, size), size)
        out.append(cps.start(ref, dst.at[tuple(idx)]))
    return out


def load_images(cps, refs, dst, places, count):
    out = []
    for j, (ref, place) in enumerate(zip(refs, places, strict=True)):
        size = ref.shape[1]
        first = pl.multiple_of(places[0] * count, count) if j == 0 else 0
        out.append(
            cps.start(
                ref.at[pl.ds(first, count)],
                dst.at[:, pl.ds(pl.multiple_of(place * size, size), size), :],
            )
        )
    return out


def places_of(pieces):
    if pieces == 1:
        return [0]
    me = lax.axis_index("tensor")
    return [me, 1 - me]


def split_store(own_ref, send_ref, at, value, axis, places):
    if send_ref is None:
        own_ref[at] = value.astype(own_ref.dtype)
        return
    half = value.shape[axis] // 2
    low = lax.slice_in_dim(value, 0, half, axis=axis)
    high = lax.slice_in_dim(value, half, 2 * half, axis=axis)
    first = places[0] == 0
    own_ref[at] = jnp.where(first, low, high).astype(own_ref.dtype)
    send_ref[at] = jnp.where(first, high, low).astype(send_ref.dtype)


def pack_store(own_ref, send_ref, at, value, axis, places):
    half = value.shape[axis] // 2
    low = lax.slice_in_dim(value, 0, half, axis=axis)
    high = lax.slice_in_dim(value, half, 2 * half, axis=axis)
    first = places[0] == 0
    own = jnp.where(first, low, high).astype(own_ref.dtype)
    send = jnp.where(first, high, low).astype(send_ref.dtype)
    rows = own.shape[0]
    for i in range(own.shape[1] // LANES):
        lanes = slice(i * LANES, (i + 1) * LANES)
        own_ref[at : at + rows, :] = own[:, lanes]
        send_ref[at : at + rows, :] = send[:, lanes]
        at += rows
    return at


def pack_kernel(n_vec, *refs):
    vectors, arrays = refs[:n_vec], refs[n_vec : n_vec + 2]
    tw, pi, po, vec, halves, small, sems = refs[n_vec + 2 :]
    cps = Copies(sems)
    count = halves.shape[1]
    first = pl.multiple_of((1 - lax.axis_index("tensor")) * count, count)
    copies = [
        cps.start(src.at[pl.ds(first, count)], halves.at[j])
        for j, src in enumerate(arrays)
    ]
    copies += [cps.start(v, vec.at[j]) for j, v in enumerate(vectors)]
    at = tw.shape[0]
    copies.append(cps.start(tw, small.at[0:at]))
    for j in range(3):
        copies.append(cps.start(pi.at[j], small.at[at : at + pi.shape[1]]))
        at += pi.shape[1]
    half = po.shape[0]
    for j in range(2):
        copies.append(cps.start(po.at[:, j * half : (j + 1) * half], small.at[at : at + half]))
        at += half
    vec[n_vec:, :] = jnp.zeros((16 - n_vec, vec.shape[1]), f32)
    wait_all(copies)


def part(value, b, points):
    return value[b * points : (b + 1) * points]


def lane_part(value, b, points):
    return value[:, b * points : (b + 1) * points]


def norm_first(x, size, width):
    x3 = x.astype(f32).reshape(GROUPS, width, x.shape[1])
    mean = jnp.sum(jnp.sum(x3, axis=2, keepdims=True), axis=1, keepdims=True) / size
    off = x3 - mean
    var = jnp.sum(jnp.sum(off * off, axis=2, keepdims=True), axis=1, keepdims=True) / size
    rstd = lax.rsqrt(var + EPS)
    return (off * rstd).reshape(x.shape), rstd


def moments(value, width, size):
    mean = lane_groups(col_sum(value), width) / size
    off = value - mean
    return mean, lax.rsqrt(lane_groups(col_sum(off * off), width) / size + EPS)


def pipelined(stages, count):
    for s in stages:
        for b in range(count):
            s(b)


def front_kernel(pieces, count, *refs):
    it = iter(refs)

    def take(n):
        return [next(it) for _ in range(n)]

    x_in, w1_in, w2_in, vec_in = (take(pieces) for _ in range(4))
    g_in, pi_in, po_in, tw_in = (take(1) for _ in range(4))
    small_in = take(pieces - 1)
    if pieces == 2:
        x_in, g_in = [x_in[0], x_in[1].at[0]], [g_in[0], x_in[1].at[1]]
    steps_ref, table_ref = take(2)
    if pieces == 2:
        own, send = take(2)
    else:
        dw2_own, dpo_own, dpi_own = take(3)
    w1_out, w2_out, po_out, all_vec_out, x_out = take(5)
    gpad_out, sum_out, a1t_out, resid_out, gres_out, mix_out = take(6)
    stat_out, sums_out = take(2)
    w1, w2, po, vec, xin = take(5)
    gpad, sum_one, a1t, resid, gres, mix = take(6)
    stat, sums = take(2)
    gin, pi, tw, rows, apad, bpad = take(6)
    sems = next(it)

    cps = Copies(sems)
    places = places_of(pieces)
    chans, points = xin.shape[1], xin.shape[2]
    side = side_of(points)
    width = chans // GROUPS
    size = float(width * points)
    scale = chans ** (-0.5)
    images = range(count)

    x_cp = load_images(cps, x_in, xin, places, count)
    vec_cp = load_split(cps, vec_in, vec, 1, places)
    w1_cp = load_split(cps, w1_in, w1, 2, places)
    row_cp = []
    for b in images:
        step = steps_ref[places[0] * count + b]
        row_cp.append(
            cps.start(table_ref.at[pl.ds(pl.multiple_of(step // 16 * 16, 16), 16), :], rows.at[b])
        )
    tw_cp = load_split(cps, tw_in, tw, 1, places[:1])
    w2_cp = load_split(cps, w2_in, w2, 1, places)
    pi_cp = load_split(cps, pi_in, pi, 2, places[:1])
    po_cp = load_split(cps, po_in, po, 0, places[:1])
    if pieces == 2:
        half = chans // 2
        theirs = pl.ds(pl.multiple_of(places[1] * half, half), half)
        embed = tw.shape[0]
        tw_cp.append(cps.start(small_in[0].at[0:embed], tw.at[:, theirs]))
        for j in range(3):
            rows_of = pl.ds(embed + j * chans, chans)
            pi_cp.append(cps.start(small_in[0].at[rows_of], pi.at[j, :, theirs]))
        for j in range(2):
            rows_of = pl.ds(embed + 3 * chans + j * half, half)
            lanes = pl.ds(j * half, half)
            po_cp.append(cps.start(small_in[0].at[rows_of], po.at[theirs, lanes]))
    g_cp = load_images(cps, g_in, gin, places, count)

    zero_pads(apad, side, points)
    zero_pads(bpad, side, points)
    zero_pads(gpad, side, points)

    wait_all(vec_cp)
    vcols = jnp.transpose(vec[...])

    def col(j):
        return vcols[:, j : j + 1]

    def row(j):
        return vec[j : j + 1, :]

    wait_all(x_cp)
    for b in images:
        hat, _ = norm_first(xin[b], size, width)
        pre = hat * col(FIRST_GAIN) + col(FIRST_SHIFT)
        act = (pre * sigmoid(pre)).astype(bf16)
        a1t[b] = act
        put_moved(apad, b, jnp.transpose(act).astype(f32), side, points)

    wait_all(row_cp)
    wait_all(tw_cp)
    wait_all(w1_cp)
    wait_all(w2_cp)
    wait_all(pi_cp)
    wait_all(po_cp)
    wait_all(g_cp)
    outs = [cps.start(vec, all_vec_out), cps.start(xin, x_out), cps.start(w1, w1_out)]
    outs += [cps.start(a1t, a1t_out), cps.start(w2, w2_out), cps.start(po, po_out)]
    picked = []
    for b in images:
        step = steps_ref[places[0] * count + b]
        r = lax.broadcasted_iota(jnp.int32, (16, rows.shape[2]), 0)
        picked.append(col_sum(jnp.where(r == lax.rem(step, 16), rows[b].astype(f32), 0.0)))
    emb = jnp.concatenate(picked + picked[:1] * (8 - count), axis=0)
    time_add = nn((emb * sigmoid(emb)).astype(bf16), tw[...]) + row(TIME_BIAS) + row(FIRST_BIAS)

    stats2, stats3 = [], []
    act_t = [None] * count

    def conv_one(b):
        lhs = jnp.concatenate(taps(apad, b, 1, side, points), axis=1)
        sum_one[b] = nn(lhs, w1[...].reshape(9 * chans, chans)) + time_add[b : b + 1]

    def norm_two(b):
        mean, rstd = moments(sum_one[b], width, size)
        stats2.append((mean, rstd))
        hat = (sum_one[b] - mean) * rstd
        pre = hat * row(SECOND_GAIN) + row(SECOND_SHIFT)
        act = pre * sigmoid(pre)
        act_t[b] = jnp.transpose(act.astype(bf16))
        put_moved(bpad, b, act, side, points)

    def conv_two(b):
        lhs = jnp.concatenate(taps(bpad, b, 1, side, points), axis=1)
        val = nn(lhs, w2[...].reshape(9 * chans, chans)) + row(SECOND_BIAS)
        resid[b] = val + jnp.transpose(xin[b]).astype(f32)

    normed = []

    def norm_three(b):
        mean, rstd = moments(resid[b], width, size)
        stats3.append((mean, rstd))
        hat = (resid[b] - mean) * rstd
        normed.append((hat * row(THIRD_GAIN) + row(THIRD_SHIFT)).astype(bf16))

    pipelined([conv_one, norm_two, conv_two, norm_three], count)
    outs += [cps.start(sum_one, sum_out), cps.start(resid, resid_out)]
    stat[0:count, :] = jnp.concatenate([m for m, _ in stats2], axis=0)
    stat[count : 2 * count, :] = jnp.concatenate([r for _, r in stats2], axis=0)
    outs.append(cps.start(stat, stat_out))

    pi_row = jnp.concatenate([pi[0], pi[1], pi[2]], axis=1)
    pi_t = jnp.concatenate([jnp.transpose(pi[1]), jnp.transpose(pi[2])], axis=0)
    zero = jnp.zeros((1, chans), f32)
    normed_t = jnp.concatenate([jnp.transpose(v) for v in normed], axis=1)
    normed = jnp.concatenate(normed, axis=0)
    lin = nn(normed, pi_row)
    q = (lin[:, :chans] + row(QUERY_BIAS)).astype(bf16)
    k = lin[:, chans : 2 * chans].astype(bf16)
    v = (lin[:, 2 * chans :] + row(VALUE_BIAS)).astype(bf16)
    lin_t = nn(pi_t, normed_t)
    kt = lin_t[:chans].astype(bf16)
    vt = (lin_t[chans:] + col(VALUE_BIAS)).astype(bf16)
    grad_all = jnp.concatenate([gin[b] for b in images], axis=1)
    grad_mixed = nn(po[...], grad_all).astype(bf16)
    scores = [nt(part(k, b, points), part(q, b, points)) for b in images]
    grad_w = [nn(part(v, b, points), lane_part(grad_mixed, b, points)) for b in images]
    weights, grad_s = [], []
    for b in images:
        top = scores[b] * scale
        expo = jnp.exp(top - jnp.max(top, axis=0, keepdims=True))
        probs = expo * (1.0 / jnp.sum(expo, axis=0, keepdims=True))
        weights.append(probs.astype(bf16))
        inner = probs * grad_w[b]
        grad_s.append((inner - probs * jnp.sum(inner, axis=0, keepdims=True)).astype(bf16))
    mixed = []
    for b in images:
        mixed.append(nn(lane_part(vt, b, points), weights[b]).astype(bf16))
        mix[b] = mixed[b]
    outs.append(cps.start(mix, mix_out))
    grad_qt = [nn(lane_part(kt, b, points), grad_s[b]) * scale for b in images]
    grad_q = [jnp.transpose(t.astype(bf16)) for t in grad_qt]
    grad_k = [(nn(grad_s[b], part(q, b, points)) * scale).astype(bf16) for b in images]
    grad_v = [nt(weights[b], lane_part(grad_mixed, b, points)).astype(bf16) for b in images]
    lin_grad = jnp.concatenate(
        [jnp.concatenate([grad_q[b], grad_k[b], grad_v[b]], axis=1) for b in images], axis=0
    )
    qb_grad = col_sum(sum(t.astype(f32) for t in grad_q))
    vb_grad = col_sum(sum(t.astype(f32) for t in grad_v))
    dpo = nt(jnp.concatenate(mixed, axis=1), grad_all)
    grad_normed = nt(lin_grad, pi_row)

    gain3, shift3, means = [], [], []
    for b in images:
        hat = (resid[b] - stats3[b][0]) * stats3[b][1]
        val = part(grad_normed, b, points)
        gain3.append(col_sum(val * hat))
        shift3.append(col_sum(val))
        both = jnp.concatenate([shift3[b], gain3[b]], axis=0) * row(THIRD_GAIN)
        means.append(lane_groups(both, width) / size)
    sb_grad, ob_grad = zero, zero
    for b in images:
        hat = (resid[b] - stats3[b][0]) * stats3[b][1]
        h = part(grad_normed, b, points) * row(THIRD_GAIN)
        grad_out = jnp.transpose(gin[b]).astype(f32)
        ob_grad = ob_grad + col_sum(grad_out)
        val = grad_out + stats3[b][1] * (h - means[b][0:1] - hat * means[b][1:2])
        gres[b] = val
        sb_grad = sb_grad + col_sum(val)
        put_moved(gpad, b, val, side, points)
        outs.append(cps.start(gres.at[b], gres_out.at[b]))
        outs.append(cps.start(gpad.at[:, b], gpad_out.at[:, b]))
    lane = lax.broadcasted_iota(jnp.int32, (1, chans), 1)
    stamp = jnp.zeros((1, chans), f32)
    for b in images:
        step = jnp.full((1, chans), steps_ref[places[0] * count + b], jnp.int32)
        stamp = jnp.where(lane == b, (step >> 5).astype(f32), stamp)
        stamp = jnp.where(lane == LANES // 2 + b, (step & 31).astype(f32), stamp)
    sums[...] = jnp.concatenate(
        [sb_grad, sum(gain3), sum(shift3), qb_grad, vb_grad, ob_grad, stamp, zero], axis=0
    )
    outs.append(cps.start(sums, sums_out))

    dpi = nn(normed_t, lin_grad)
    at = 0
    if pieces == 2:
        at = pack_store(own, send, at, dpo, 0, places)
        for j in range(3):
            at = pack_store(own, send, at, dpi[:, j * chans : (j + 1) * chans], 1, places)
    else:
        dpo_own[...] = dpo
        for j in range(3):
            dpi_own[j] = dpi[:, j * chans : (j + 1) * chans]

    a_all = jnp.concatenate(act_t, axis=1)
    moved = [taps(gpad, b, -1, side, points) for b in images]
    for tap in range(9):
        val = nn(a_all, jnp.concatenate([moved[b][tap] for b in images], axis=0))
        if pieces == 2:
            at = pack_store(own, send, at, val, 0, places)
        else:
            dw2_own[tap] = val

    wait_all(outs)


def copy_rows(cps, pairs, start, end):
    rows = slice(start, end)
    return [cps.start(src.at[rows], dst.at[rows]) for src, dst in pairs]


def back_kernel(pieces, count, *refs):
    it = iter(refs)

    def take(n):
        return [next(it) for _ in range(n)]

    kept = take(13)
    if pieces == 2:
        own, send_out, block_own_out, block_send_out, image_own_out, image_send_out = take(6)
    else:
        own, block_own_out, image_own_out = take(3)
        block_send_out = image_send_out = None
    small = next(it)
    w1, w2, po, vec, xin, gpad, sum_one, a1t, resid, gres, mix, stat, front_sums = take(13)
    if pieces == 2:
        send, block_own, block_send, image_own, image_send = take(5)
    else:
        block_own, image_own = take(2)
        block_send = image_send = None
    hpad, back, first_hat, first_slope, sems = take(5)
    cps = Copies(sems)
    places = places_of(pieces)
    points, chans = sum_one.shape[1], sum_one.shape[2]
    side = side_of(points)
    width = chans // GROUPS
    size = float(width * points)
    images = range(count)

    w1_in, w2_in, po_in, vec_in, x_in, gpad_in, sum_in, a1t_in, resid_in, gres_in, mix_in = kept[:11]
    early = [(vec_in, vec), (x_in, xin)]
    early = [cps.start(src, dst) for src, dst in early]
    w2_cp = cps.start(w2_in, w2)
    gpad_cp = [cps.start(gpad_in.at[:, b], gpad.at[:, b]) for b in images]
    small_cp = [(kept[11], stat), (kept[12], front_sums)]
    small_cp = [cps.start(src, dst) for src, dst in small_cp]
    sum_cp = cps.start(sum_in, sum_one)
    a1t_cp = cps.start(a1t_in, a1t)
    later = [(w1_in, w1), (po_in, po), (resid_in, resid), (gres_in, gres), (mix_in, mix)]
    later = [cps.start(src, dst) for src, dst in later]

    def row(j):
        return vec[j : j + 1, :]

    zero_pads(hpad, side, points)
    wait_all(early)
    vcols = jnp.transpose(vec[...])

    def col(j):
        return vcols[:, j : j + 1]

    first_rstd = []
    for b in images:
        hat, rstd = norm_first(xin[b], size, width)
        first_rstd.append(jnp.broadcast_to(rstd, (GROUPS, width, 1)).reshape(chans, 1))
        pre = hat * col(FIRST_GAIN) + col(FIRST_SHIFT)
        first_hat[b] = hat
        first_slope[b] = silu_slope(pre, sigmoid(pre))

    w2_cp.wait()
    wait_all(gpad_cp)
    sum_cp.wait()
    wait_all(small_cp)
    w2_cols = jnp.concatenate([w2[k] for k in range(9)], axis=1)
    gain, shift_g, times = [], [], []

    def conv_back(b):
        back[b] = nt(jnp.concatenate(taps(gpad, b, -1, side, points), axis=1), w2_cols)

    def norm_back(b):
        mean, rstd = stat[b : b + 1, :], stat[count + b : count + b + 1, :]
        hat = (sum_one[b] - mean) * rstd
        pre = hat * row(SECOND_GAIN) + row(SECOND_SHIFT)
        val = back[b] * silu_slope(pre, sigmoid(pre))
        gain.append(col_sum(val * hat))
        shift_g.append(col_sum(val))
        both = jnp.concatenate([shift_g[b], gain[b]], axis=0) * row(SECOND_GAIN)
        both = lane_groups(both, width) / size
        val = rstd * (val * row(SECOND_GAIN) - both[0:1] - hat * both[1:2])
        times.append(col_sum(val))
        put_moved(hpad, b, val, side, points)

    pipelined([conv_back, norm_back], count)
    a1t_cp.wait()
    wait_all(later)
    outs = []


    def put_out(own_ref, send_ref, own_dst, send_dst, b, val):
        split_store(own_ref, send_ref, b, val, 0, places)
        outs.append(cps.start(own_ref.at[b], own_dst.at[b]))
        if send_ref is not None:
            outs.append(cps.start(send_ref.at[b], send_dst.at[b]))

    proj = nn(jnp.transpose(po[...]), jnp.concatenate([mix[b] for b in images], axis=1))
    a_all = jnp.concatenate([a1t[b] for b in images], axis=1)
    moved = [taps(hpad, b, -1, side, points) for b in images]
    at = 0
    for tap in range(9):
        val = nn(a_all, jnp.concatenate([moved[b][tap] for b in images], axis=0))
        if pieces == 2:
            at = pack_store(own, send, at, val, 1, places)
        else:
            own[tap] = val
        if tap % 2 == 1 and tap // 2 < count:
            b = tap // 2
            val = jnp.transpose(resid[b]) + lane_part(proj, b, points) + col(OUTPUT_BIAS)
            split_store(block_own, block_send, b, val, 0, places)
    if pieces == 2:
        outs += copy_rows(cps, [(send, send_out)], 0, at)
        outs.append(cps.start(block_send, block_send_out))
    outs.append(cps.start(block_own, block_own_out))

    w1_cols = jnp.concatenate([w1[k] for k in range(9)], axis=1)
    zero = jnp.zeros((chans, 1), f32)
    gain_sum, shift_sum = [zero], [zero]
    first_back = [None] * count

    def groups(v):
        total = jnp.sum(v.reshape(GROUPS, width, 1), axis=1, keepdims=True) / size
        return jnp.broadcast_to(total, (GROUPS, width, 1)).reshape(chans, 1)

    def conv_first(b):
        first_back[b] = nt(w1_cols, jnp.concatenate(taps(hpad, b, -1, side, points), axis=1))

    def norm_first_back(b):
        hat, rstd = first_hat[b], first_rstd[b]
        val = first_back[b] * first_slope[b]
        gain = jnp.sum(val * hat, axis=1, keepdims=True)
        shift = jnp.sum(val, axis=1, keepdims=True)
        gain_sum[0] = gain_sum[0] + gain
        shift_sum[0] = shift_sum[0] + shift
        first_mean = groups(shift * col(FIRST_GAIN))
        second_mean = groups(gain * col(FIRST_GAIN))
        val = rstd * (val * col(FIRST_GAIN) - first_mean - hat * second_mean)
        val = val + jnp.transpose(gres[b])
        put_out(image_own, image_send, image_own_out, image_send_out, b, val)

    pipelined([conv_first, norm_first_back], count)

    lane = lax.broadcasted_iota(jnp.int32, (chans, LANES), 1)
    both = jnp.where(lane == 0, gain_sum[0], 0.0) + jnp.where(lane == 1, shift_sum[0], 0.0)
    both = jnp.transpose(both)
    rows = [front_sums[j : j + 1, :] for j in range(6)]
    rows += [sum(gain), sum(shift_g), sum(times), both[0:1], both[1:2]]
    flat = []
    for r in rows + times:
        flat += [r[:, i * LANES : (i + 1) * LANES] for i in range(chans // LANES)]
    flat.append(front_sums[6:7, :LANES])
    flat += [jnp.zeros((1, LANES), f32)] * (BLOCK - len(flat))
    small[...] = jnp.concatenate(flat, axis=0).astype(bf16)
    wait_all(outs)


def put_quarters(quarters, flat):
    me = lax.axis_index("batch") & 3
    rows = quarters[0].shape[0]
    if len(quarters) == 4:
        parts = [(j, ref, 0) for j, ref in enumerate(quarters)]
    else:
        odd = lax.axis_index("tensor") & 1
        mine, first, both = quarters
        parts = [(0, mine, 0), (1 + odd, first, 0), (2 - odd, both, 0), (3, both, rows)]
    for j, ref, at in parts:
        flat[pl.ds(pl.multiple_of((me ^ j) * rows, 16), rows), :] = ref[at : at + rows, :]


def unpack_first_kernel(*refs):
    quarters = refs[:-4]
    dw1_out, flat, dw1, sems = refs[-4:]
    cps = Copies(sems)
    put_quarters(quarters, flat)
    outs = []
    chans = dw1.shape[1]
    for tap in range(dw1.shape[0]):
        dw1[tap] = flat[tap * chans : (tap + 1) * chans, :].astype(f32)
        if tap % 3 == 2:
            part = slice(tap - 2, tap + 1)
            outs.append(cps.start(dw1.at[part], dw1_out.at[part]))
    wait_all(outs)


def unpack_second_kernel(*refs):
    quarters = refs[:-8]
    dw2_out, dpo_out, dpi_out, flat, dw2, dpo, dpi, sems = refs[-8:]
    cps = Copies(sems)
    put_quarters(quarters, flat)
    outs = []
    chans = dpi.shape[1]
    half = chans // 2
    for i in range(2):
        dpo[:, i * LANES : (i + 1) * LANES] = flat[i * half : (i + 1) * half, :].astype(f32)
    outs.append(cps.start(dpo, dpo_out))
    at = chans
    for j in range(3):
        dpi[j] = flat[at : at + chans, :].astype(f32)
        at += chans
    outs.append(cps.start(dpi, dpi_out))
    for tap in range(dw2.shape[0]):
        for i in range(2):
            dw2[tap, :, i * LANES : (i + 1) * LANES] = flat[at : at + half, :].astype(f32)
            at += half
        if tap % 3 == 2:
            part = slice(tap - 2, tap + 1)
            outs.append(cps.start(dw2.at[part], dw2_out.at[part]))
    wait_all(outs)


def swap(value, axis, size, bit):
    return lax.ppermute(value, axis, [(i, i ^ bit) for i in range(size)])


def near_parts(part):
    me = lax.axis_index("batch") & 3
    return [part(me ^ j).astype(bf16) for j in range(1, 4)]


def together(*groups):
    return [list(g) for g in lax.optimization_barrier(tuple(tuple(g) for g in groups))]


def send_near(sent, batch):
    return [swap(v, "batch", batch, j + 1) for j, v in enumerate(sent)]


def sum_near(got, part):
    total = part(lax.axis_index("batch") & 3).astype(f32)
    for g in got:
        total = total + g.astype(f32)
    return total.astype(bf16)


def far_steps(batch):
    return batch.bit_length() - 3


def send_far(piece, extra, step, batch):
    steps = far_steps(batch)
    mine = piece if extra is None else jnp.concatenate([piece, extra], axis=0)
    tensor = lax.axis_size("tensor")
    pairs = []
    for i in range(batch):
        for core in range(tensor):
            bit = 4 << (step if core % 2 == 0 else steps - 1 - step)
            pairs.append((i * tensor + core, (i ^ bit) * tensor + core))
    return lax.ppermute(mine, ("batch", "tensor"), pairs)


def sum_far(piece, extra, got):
    rows = piece.shape[0]
    piece = (piece.astype(f32) + got[:rows].astype(f32)).astype(bf16)
    if extra is not None:
        extra = jnp.concatenate([extra, got[rows:]], axis=0)
    return piece, extra


def gather_near(piece, batch):
    return [piece] + [swap(piece, "batch", batch, j) for j in range(1, 4)]


def plane_bit(step, core):
    return 1 if step == core % 2 else 2


def cross(value, step, batch):
    tensor = lax.axis_size("tensor")
    pairs = []
    for i in range(batch):
        for core in range(tensor):
            pairs.append((i * tensor + core, (i ^ plane_bit(step, core)) * tensor + core))
    return lax.ppermute(value, ("batch", "tensor"), pairs)


def by_difference(mine, first, both):
    rows = mine.shape[0]
    odd = (lax.axis_index("tensor") & 1) == 1
    near, far = both[:rows], both[rows:]
    return [mine, jnp.where(odd, near, first), jnp.where(odd, first, near), far]


def in_order(pieces):
    me = lax.axis_index("batch")
    parts = jnp.stack(pieces, axis=0)
    parts = parts.reshape((2, 2) + parts.shape[1:])
    parts = jnp.where((me & 1) == 1, jnp.flip(parts, axis=1), parts)
    parts = jnp.where((me & 2) == 2, jnp.flip(parts, axis=0), parts)
    return parts.reshape((-1, LANES))


def unpack(flat, shapes):
    out = []
    at = 0
    for shape in shapes:
        n = math.prod(shape) // 128
        out.append(flat[at : at + n].reshape(shape).astype(f32))
        at += n
    return out


def per_device(
    batch,
    tensor,
    images,
    timesteps,
    embed_table,
    first_gain,
    first_shift,
    first_conv,
    first_bias,
    time_weight,
    time_bias,
    second_gain,
    second_shift,
    second_conv,
    second_bias,
    third_gain,
    third_shift,
    project_in,
    query_bias,
    value_bias,
    project_out,
    output_bias,
    cotangent,
):
    per_batch, local, points = images.shape
    chans = local * tensor
    count = per_batch // tensor
    table_rows, embed = embed_table.shape
    pieces = 2 if tensor == 2 else 1
    me = lax.axis_index("tensor")
    vectors = [
        first_gain,
        first_shift,
        first_bias,
        time_bias,
        second_gain,
        second_shift,
        second_bias,
        third_gain,
        third_shift,
        query_bias,
        value_bias,
        output_bias,
    ]
    def in_hbm(array):
        return pltpu.with_memory_space_constraint(array, pltpu.HBM)

    n_vec = len(vectors)
    if pieces == 2:
        vec, halves, small = pl.pallas_call(
            functools.partial(pack_kernel, n_vec),
            out_shape=[
                jax.ShapeDtypeStruct((16, local), f32),
                jax.ShapeDtypeStruct((2, count, local, points), bf16),
                jax.ShapeDtypeStruct((embed + 4 * chans, local), bf16),
            ],
            in_specs=[ANY] * (n_vec + 5),
            out_specs=[VMEM] * 3,
            scratch_shapes=[pltpu.SemaphoreType.DMA((n_vec + 8,))],
            compiler_params=pltpu.CompilerParams(vmem_limit_bytes=4 * MIB),
            name="pack",
        )(*(in_hbm(v) for v in vectors + [images, cotangent, time_weight, project_in, project_out]))
    else:
        vec = jnp.stack(vectors + [output_bias] * 4, axis=0)

    def whole(array, axis):
        if pieces == 2:
            return [array, swap(array, "tensor", 2, 1)]
        return [lax.all_gather(array, "tensor", axis=axis, tiled=True)]

    if pieces == 2:
        x_in, g_in = [images, swap(halves, "tensor", 2, 1)], [cotangent]
        tw_in, pi_in, po_in = [time_weight], [project_in], [project_out]
        small_in = [swap(small, "tensor", 2, 1)]
    else:
        x_in, g_in = (
            [lax.all_to_all(v, "tensor", 0, 1, tiled=True)] for v in (images, cotangent)
        )
        tw_in, pi_in, po_in = whole(time_weight, 1), whole(project_in, 2), whole(project_out, 0)
        small_in = []
    vec_in = whole(vec, 1)
    w1_in = whole(first_conv, 2)
    w2_in = whole(second_conv, 1)
    my_steps = timesteps if pieces == 2 else lax.dynamic_slice_in_dim(timesteps, me * count, count)

    side = side_of(points)
    image_b = (count, chans, points)
    image_p = (count, points, chans)
    pads = (3, count, points + 2 * side, chans)

    def shape(s, d):
        return jax.ShapeDtypeStruct(s, d)

    def params(mib):
        return pltpu.CompilerParams(vmem_limit_bytes=mib * MIB)

    def cost(units, moved):
        flops = 2 * units * count * points * chans * chans
        return pl.CostEstimate(flops=flops, bytes_accessed=moved, transcendentals=0)

    half_b = 9 * chans * chans // 2 // LANES
    half_a = half_b + 4 * chans * chans // 2 // LANES
    if pieces == 2:
        grads_a = [pltpu.VMEM((half_a, LANES), bf16)] * 2
        grads_b = [pltpu.VMEM((half_b, LANES), bf16), pltpu.HBM((half_b, LANES), bf16)]
    else:
        grads_a = [shape((9, chans, chans), f32), shape((chans, chans), f32)]
        grads_a.append(shape((3, chans, chans), f32))
        grads_b = [shape((9, chans, chans), f32)]
    n_grad = len(grads_a)
    steps_in = in_hbm(my_steps)
    kept = [
        ((9, chans, chans), bf16),
        ((9, chans, chans), bf16),
        ((chans, chans), bf16),
        ((16, chans), f32),
        (image_b, bf16),
        (pads, bf16),
        (image_p, f32),
        (image_b, bf16),
        (image_p, f32),
        (image_p, f32),
        (image_b, bf16),
        ((2 * count, chans), f32),
        ((8, chans), f32),
    ]
    out_a = ANY if pieces == 2 else VMEM
    scratch_a = []

    front = pl.pallas_call(
        functools.partial(front_kernel, pieces, count),
        out_shape=grads_a
        + [pltpu.HBM(*v) for v in kept],
        in_specs=[ANY, VMEM][:pieces] * 4 + [ANY] * 4 + [VMEM] * (pieces - 1) + [SMEM, ANY],
        out_specs=[VMEM] * n_grad + [ANY] * len(kept),
        scratch_shapes=scratch_a
        + [pltpu.VMEM(*v) for v in kept]
        + [
            pltpu.VMEM(image_b, bf16),
            pltpu.VMEM((3, chans, chans), bf16),
            pltpu.VMEM((embed, chans), bf16),
            pltpu.VMEM((count, 16, embed), bf16),
            pltpu.VMEM(pads, bf16),
            pltpu.VMEM(pads, bf16),
            pltpu.SemaphoreType.DMA((8 * pieces + 3 * count + 22,)),
        ],
        compiler_params=params(28),
        cost_estimate=cost(54, 12 << 20),
        name="front",
    )(
        *(
            place(v)
            for pair in (x_in, w1_in, w2_in, vec_in)
            for v, place in zip(pair, (in_hbm, lambda v: v))
        ),
        *(in_hbm(v) for v in g_in + pi_in + po_in + tw_in),
        *small_in,
        steps_in,
        in_hbm(embed_table),
    )
    sums_a = front[:n_grad]
    kept_now = list(front[n_grad:])

    def quarters(sums, axes, beside=None):
        if pieces == 2:
            got = swap(sums[1], "tensor", 2, 1)
            if beside is not None:
                (got,), (beside,) = together([got], [beside])
            rows = got.shape[0] // 4
            own4, got4 = (v.reshape(4, rows, LANES) for v in (sums[0], got))

            def part(q):
                pair = [lax.dynamic_index_in_dim(v, q, 0, False).astype(f32) for v in (own4, got4)]
                return pair[0] + pair[1]

            return part, beside
        done = [
            lax.psum_scatter(v, "tensor", scatter_dimension=axis, tiled=True)
            for v, axis in zip(sums, axes, strict=True)
        ]
        flat = jnp.concatenate([v.reshape(-1, LANES) for v in done], axis=0)
        flat = jnp.pad(flat, ((0, -flat.shape[0] % 64), (0, 0)))
        rows = flat.shape[0] // 4
        flat = flat.reshape(4, rows, LANES)
        return (lambda q: lax.dynamic_index_in_dim(flat, q, 0, False)), beside

    part_a, _ = quarters(sums_a, (1, 0, 2))
    sent_a = near_parts(part_a)

    kept_now[-2:], sent_a = together(kept_now[-2:], sent_a)
    got_a = send_near(sent_a, batch)

    half = (count, chans // 2, points)
    if pieces == 2:
        outs_b = grads_b + [pltpu.HBM(half, f32), pltpu.HBM(half, bf16)] * 2
        scratch_b = [pltpu.VMEM(v.shape, v.dtype) for v in outs_b[1:]]
    else:
        outs_b = grads_b + [pltpu.HBM(image_b, f32)] * 2
        scratch_b = [pltpu.VMEM(image_b, f32)] * 2
    *outs_b, block = pl.pallas_call(
        functools.partial(back_kernel, pieces, count),
        out_shape=outs_b + [pltpu.VMEM((BLOCK, LANES), bf16)],
        in_specs=[ANY] * len(kept),
        out_specs=[VMEM, out_a][:pieces] + [ANY] * (2 * pieces) + [VMEM],
        scratch_shapes=[pltpu.VMEM(*v) for v in kept]
        + scratch_b
        + [
            pltpu.VMEM(pads, bf16),
            pltpu.VMEM(image_p, f32),
            pltpu.VMEM(image_b, f32),
            pltpu.VMEM(image_b, f32),
            pltpu.SemaphoreType.DMA((16 + 3 * count,)),
        ],
        compiler_params=params(28),
        cost_estimate=cost(33, 12 << 20),
        name="back",
    )(*(in_hbm(v) for v in kept_now))
    sums_b, block_part, image_grad = outs_b[:pieces], outs_b[pieces : 2 * pieces], outs_b[2 * pieces :]
    got_a, sums_b, (block,) = together(got_a, sums_b, [block])
    piece_a = sum_near(got_a, part_a)
    steps = far_steps(batch)
    far_a = send_far(piece_a, None, 0, batch) if steps > 0 else None
    part_b, piece_a = quarters(sums_b, (2,), piece_a)
    sent_b = near_parts(part_b)
    got_b = send_near([jnp.concatenate([v, block], axis=0) for v in sent_b], batch)
    if steps > 0:
        piece_a, _ = sum_far(piece_a, None, far_a)
    if steps > 1:
        far_a = send_far(piece_a, None, 1, batch)
    got_b, (piece_a,) = together(got_b, [piece_a])
    rows_b = sent_b[0].shape[0]
    blocks = jnp.concatenate([block] + [g[rows_b:] for g in got_b], axis=0)
    piece_b = sum_near([g[:rows_b] for g in got_b], part_b)
    for step in range(1, steps):
        if step > 1:
            far_a = send_far(piece_a, None, step, batch)
        piece_a, _ = sum_far(piece_a, None, far_a)
    if steps > 0:
        far_b = send_far(piece_b, blocks, 0, batch)
    block_part, image_grad, (piece_b,) = together(block_part, image_grad, [piece_b])

    def placed(own, send):
        if pieces == 2:
            got = swap(send, "tensor", 2, 1).astype(f32)
            low = jnp.where(me == 0, own, got)
            high = jnp.where(me == 0, got, own)
            return jnp.concatenate([low, high], axis=0)
        return lax.all_to_all(own, "tensor", 1, 0, tiled=True)

    block_out = placed(block_part[0], block_part[-1])
    images_grad = placed(image_grad[0], image_grad[-1])

    first_a = cross(piece_a, 0, batch)
    both_a = cross(jnp.concatenate([piece_a, first_a], axis=0), 1, batch)
    for step in range(steps):
        if step > 0:
            far_b = send_far(piece_b, blocks, step, batch)
            (far_b,), (first_a,) = together([far_b], [first_a])
        piece_b, blocks = sum_far(piece_b, blocks, far_b)
    got_a = [piece_a, first_a, both_a]
    got_b = gather_near(piece_b, batch)

    if pieces == 2:

        def unpacked(kernel, name, got, rows, shapes):
            outs = [shape(v, f32) for v in shapes]
            return pl.pallas_call(
                kernel,
                out_shape=outs,
                in_specs=[VMEM] * len(got),
                out_specs=[ANY] * len(outs),
                scratch_shapes=[pltpu.VMEM((rows, LANES), bf16)]
                + [pltpu.VMEM(v.shape, v.dtype) for v in outs]
                + [pltpu.SemaphoreType.DMA((len(outs) + 2,))],
                compiler_params=params(12),
                name=name,
            )(*got)

        second_conv_grad, project_out_grad, project_in_grad = unpacked(
            unpack_second_kernel,
            "unpack_second",
            got_a,
            half_a,
            [(9, local, chans), (local, chans), (3, chans, local)],
        )
        got_b, (second_conv_grad,) = together(got_b, [second_conv_grad])
        (first_conv_grad,) = unpacked(
            unpack_first_kernel, "unpack_first", got_b, half_b, [(9, chans, local)]
        )
    else:
        second_conv_grad, project_out_grad, project_in_grad = unpack(
            in_order(by_difference(*got_a)), [(9, local, chans), (local, chans), (3, chans, local)]
        )
        (first_conv_grad,) = unpack(in_order(got_b), [(9, chans, local)])

    if pieces == 2:
        blocks = jnp.concatenate([blocks, swap(blocks, "tensor", 2, 1)], axis=0)
        two = blocks.reshape(2, batch, BLOCK, LANES)
        blocks = jnp.where(me == 0, two, jnp.flip(two, axis=0))
    else:
        blocks = lax.all_gather(blocks, "tensor", axis=0, tiled=True)
    blocks = blocks.reshape(batch * tensor, BLOCK, LANES)
    wide = chans // LANES
    n_sum = 11 * wide
    sums = jnp.sum(blocks[:, :n_sum].astype(f32), axis=0).reshape(11, chans)
    sums = jnp.concatenate([sums, sums[8:9]], axis=0)
    mine = lax.dynamic_slice_in_dim(sums, me * local, local, axis=1)
    all_times = blocks[:, n_sum : n_sum + wide * count].reshape(-1, chans)
    stamps = blocks[:, n_sum + wide * count].astype(jnp.int32)
    all_steps = stamps[:, :count] * 32 + stamps[:, LANES // 2 : LANES // 2 + count]
    all_steps = all_steps.reshape(-1)
    one_hot = (all_steps[:, None] == jnp.arange(table_rows, dtype=jnp.int32)[None, :]).astype(bf16)
    emb = nn(one_hot, embed_table)
    sig = sigmoid(emb)
    act = (emb * sig).astype(bf16)
    my_times = lax.dynamic_slice_in_dim(all_times, me * local, local, axis=1)
    time_weight_grad = lax.dot_general(
        act, my_times, (((0,), (0,)), ((), ())), preferred_element_type=f32
    )
    if pieces == 2:
        theirs = small_in[0][:embed]
        tw = jnp.where(
            me == 0,
            jnp.concatenate([time_weight, theirs], axis=1),
            jnp.concatenate([theirs, time_weight], axis=1),
        )
    else:
        tw = tw_in[0]
    grad_emb = (nt(all_times, tw) * silu_slope(emb, sig)).astype(bf16)
    table_grad = lax.dot_general(
        one_hot, grad_emb, (((0,), (0,)), ((), ())), preferred_element_type=f32
    )
    return (
        block_out,
        images_grad,
        table_grad,
        mine[9],
        mine[10],
        first_conv_grad,
        mine[8],
        time_weight_grad,
        mine[11],
        mine[6],
        mine[7],
        second_conv_grad,
        mine[0],
        mine[1],
        mine[2],
        project_in_grad,
        mine[3],
        mine[4],
        project_out_grad,
        mine[5],
    )


def solution(mesh):
    in_specs = (
        P("batch", "tensor", None),
        P("batch"),
        P(),
        P("tensor"),
        P("tensor"),
        P(None, None, "tensor"),
        P("tensor"),
        P(None, "tensor"),
        P("tensor"),
        P("tensor"),
        P("tensor"),
        P(None, "tensor", None),
        P("tensor"),
        P("tensor"),
        P("tensor"),
        P(None, None, "tensor"),
        P("tensor"),
        P("tensor"),
        P("tensor", None),
        P("tensor"),
        P("batch", "tensor", None),
    )
    out_specs = (
        P("batch", "tensor", None),
        P("batch", "tensor", None),
        P(),
        P("tensor"),
        P("tensor"),
        P(None, None, "tensor"),
        P("tensor"),
        P(None, "tensor"),
        P("tensor"),
        P("tensor"),
        P("tensor"),
        P(None, "tensor", None),
        P("tensor"),
        P("tensor"),
        P("tensor"),
        P(None, None, "tensor"),
        P("tensor"),
        P("tensor"),
        P("tensor", None),
        P("tensor"),
    )
    sizes = dict(mesh.shape)
    return jax.shard_map(
        functools.partial(per_device, sizes["batch"], sizes["tensor"]),
        mesh=mesh,
        in_specs=in_specs,
        out_specs=out_specs,
        check_vma=False,
    )
```

```python
import functools
import math

import jax
import jax.numpy as jnp
from jax import lax
from jax.experimental import pallas as pl
from jax.experimental.pallas import tpu as pltpu
from jax.sharding import PartitionSpec as P

GROUPS = 32
LANES = 128
BLOCK = 32
EPS = 1e-06
MIB = 1024 * 1024
ANY = pl.BlockSpec(memory_space=pl.ANY)
VMEM = pl.BlockSpec(memory_space=pltpu.VMEM)
f32 = jnp.float32
bf16 = jnp.bfloat16

(
    FIRST_GAIN,
    FIRST_SHIFT,
    FIRST_BIAS,
    TIME_BIAS,
    SECOND_GAIN,
    SECOND_SHIFT,
    SECOND_BIAS,
    THIRD_GAIN,
    THIRD_SHIFT,
    QUERY_BIAS,
    VALUE_BIAS,
    OUTPUT_BIAS,
) = range(12)


def nn(a, b):
    return lax.dot_general(a, b, (((1,), (0,)), ((), ())), preferred_element_type=f32)


def nt(a, b):
    return lax.dot_general(a, b, (((1,), (1,)), ((), ())), preferred_element_type=f32)


def sigmoid(v):
    return 0.5 * jnp.tanh(0.5 * v) + 0.5


def silu_slope(v, sig):
    return sig * (1.0 + v * (1.0 - sig))


def col_sum(v):
    return jnp.sum(v, axis=0, keepdims=True)


def lane_groups(v, width):
    lanes = v.shape[1]
    lane = lax.broadcasted_iota(jnp.int32, v.shape, 1)
    step = 1
    while step < width:
        up = pltpu.roll(v, step, 1)
        down = pltpu.roll(v, lanes - step, 1)
        v = v + jnp.where((lane & step) != 0, up, down)
        step *= 2
    return v


def zero_pads(pad_ref, side, points):
    images, chans = pad_ref.shape[1], pad_ref.shape[3]
    for d in range(3):
        for b in range(images):
            pad_ref[d, b, 0:side, :] = jnp.zeros((side, chans), bf16)
            pad_ref[d, b, side + points : 2 * side + points, :] = jnp.zeros((side, chans), bf16)


def put_moved(pad_ref, b, value, side, points):
    chans = value.shape[1]
    column = lax.broadcasted_iota(jnp.int32, (side, chans), 0)
    for d, edge in ((0, 0), (1, None), (2, side - 1)):
        moved = value
        if edge is not None:
            moved = pltpu.roll(value, (1 - d) % points, 0).reshape(side, side, chans)
            moved = jnp.where((column == edge)[None], 0.0, moved).reshape(points, chans)
        pad_ref[d, b, side : side + points, :] = moved.astype(bf16)


def taps(pad_ref, b, sign, side, points):
    out = []
    for dr in (-1, 0, 1):
        for dc in (-1, 0, 1):
            top = side + sign * dr * side
            out.append(pad_ref[1 + sign * dc, b, top : top + points, :])
    return out


class Copies:
    def __init__(self, sems):
        self.sems = sems
        self.used = 0

    def start(self, src, dst):
        copy = pltpu.make_async_copy(src, dst, self.sems.at[self.used])
        self.used += 1
        copy.start()
        return copy


def wait_all(copies):
    for c in copies:
        c.wait()


def side_of(points):
    return math.isqrt(points)


def load_split(cps, refs, dst, axis, places):
    out = []
    for ref, place in zip(refs, places, strict=True):
        size = ref.shape[axis]
        idx = [slice(None)] * len(ref.shape)
        idx[axis] = pl.ds(pl.multiple_of(place * size, size), size)
        out.append(cps.start(ref, dst.at[tuple(idx)]))
    return out


def load_images(cps, refs, dst, places, count):
    out = []
    for j, (ref, place) in enumerate(zip(refs, places, strict=True)):
        size = ref.shape[1]
        first = pl.multiple_of(places[0] * count, count) if j == 0 else 0
        out.append(
            cps.start(
                ref.at[pl.ds(first, count)],
                dst.at[:, pl.ds(pl.multiple_of(place * size, size), size), :],
            )
        )
    return out


def places_of(pieces):
    if pieces == 1:
        return [0]
    me = lax.axis_index("tensor")
    return [me, 1 - me]


def split_store(own_ref, send_ref, at, value, axis, places):
    if send_ref is None:
        own_ref[at] = value.astype(own_ref.dtype)
        return
    half = value.shape[axis] // 2
    low = lax.slice_in_dim(value, 0, half, axis=axis)
    high = lax.slice_in_dim(value, half, 2 * half, axis=axis)
    first = places[0] == 0
    own_ref[at] = jnp.where(first, low, high).astype(own_ref.dtype)
    send_ref[at] = jnp.where(first, high, low).astype(send_ref.dtype)


def pack_store(own_ref, send_ref, at, value, axis, places):
    half = value.shape[axis] // 2
    low = lax.slice_in_dim(value, 0, half, axis=axis)
    high = lax.slice_in_dim(value, half, 2 * half, axis=axis)
    first = places[0] == 0
    own = jnp.where(first, low, high).astype(own_ref.dtype)
    send = jnp.where(first, high, low).astype(send_ref.dtype)
    rows = own.shape[0]
    for i in range(own.shape[1] // LANES):
        lanes = slice(i * LANES, (i + 1) * LANES)
        own_ref[at : at + rows, :] = own[:, lanes]
        send_ref[at : at + rows, :] = send[:, lanes]
        at += rows
    return at


def pack_kernel(n_vec, *refs):
    vectors, arrays = refs[:n_vec], refs[n_vec : n_vec + 2]
    tw, pi, po, vec, halves, small, sems = refs[n_vec + 2 :]
    cps = Copies(sems)
    count = halves.shape[1]
    first = pl.multiple_of((1 - lax.axis_index("tensor")) * count, count)
    copies = [
        cps.start(src.at[pl.ds(first, count)], halves.at[j])
        for j, src in enumerate(arrays)
    ]
    copies += [cps.start(v, vec.at[j]) for j, v in enumerate(vectors)]
    at = tw.shape[0]
    copies.append(cps.start(tw, small.at[0:at]))
    for j in range(3):
        copies.append(cps.start(pi.at[j], small.at[at : at + pi.shape[1]]))
        at += pi.shape[1]
    half = po.shape[0]
    for j in range(2):
        copies.append(cps.start(po.at[:, j * half : (j + 1) * half], small.at[at : at + half]))
        at += half
    vec[n_vec:, :] = jnp.zeros((16 - n_vec, vec.shape[1]), f32)
    wait_all(copies)


def part(value, b, points):
    return value[b * points : (b + 1) * points]


def lane_part(value, b, points):
    return value[:, b * points : (b + 1) * points]


def norm_first(x, size, width):
    x3 = x.astype(f32).reshape(GROUPS, width, x.shape[1])
    mean = jnp.sum(jnp.sum(x3, axis=2, keepdims=True), axis=1, keepdims=True) / size
    off = x3 - mean
    var = jnp.sum(jnp.sum(off * off, axis=2, keepdims=True), axis=1, keepdims=True) / size
    rstd = lax.rsqrt(var + EPS)
    return (off * rstd).reshape(x.shape), rstd


def moments(value, width, size):
    mean = lane_groups(col_sum(value), width) / size
    off = value - mean
    return mean, lax.rsqrt(lane_groups(col_sum(off * off), width) / size + EPS)


def pipelined(stages, count):
    for s in stages:
        for b in range(count):
            s(b)


def front_kernel(pieces, count, *refs):
    it = iter(refs)

    def take(n):
        return [next(it) for _ in range(n)]

    x_in, w1_in, w2_in, vec_in = (take(pieces) for _ in range(4))
    g_in, pi_in, po_in, tw_in = (take(1) for _ in range(4))
    small_in = take(pieces - 1)
    if pieces == 2:
        x_in, g_in = [x_in[0], x_in[1].at[0]], [g_in[0], x_in[1].at[1]]
    steps_in, table_ref = take(2)
    if pieces == 2:
        own, send = take(2)
    else:
        dw2_own, dpo_own, dpi_own = take(3)
    w1_out, w2_out, po_out, all_vec_out, x_out = take(5)
    gpad_out, sum_out, a1t_out, resid_out, gres_out, mix_out = take(6)
    stat_out, sums_out = take(2)
    w1, w2, po, vec, xin = take(5)
    gpad, sum_one, a1t, resid, gres, mix = take(6)
    stat, sums = take(2)
    gin, pi, tw, rows, apad, bpad, steps_ref = take(7)
    sems = next(it)

    cps = Copies(sems)
    places = places_of(pieces)
    chans, points = xin.shape[1], xin.shape[2]
    side = side_of(points)
    width = chans // GROUPS
    size = float(width * points)
    scale = chans ** (-0.5)
    images = range(count)

    steps_cp = cps.start(steps_in, steps_ref)
    x_cp = load_images(cps, x_in, xin, places, count)
    vec_cp = load_split(cps, vec_in, vec, 1, places)
    w1_cp = load_split(cps, w1_in, w1, 2, places)
    w2_cp = load_split(cps, w2_in, w2, 1, places)
    steps_cp.wait()
    row_cp = []
    for b in images:
        step = steps_ref[places[0] * count + b]
        row_cp.append(
            cps.start(table_ref.at[pl.ds(pl.multiple_of(step // 16 * 16, 16), 16), :], rows.at[b])
        )
    tw_cp = load_split(cps, tw_in, tw, 1, places[:1])
    pi_cp = load_split(cps, pi_in, pi, 2, places[:1])
    po_cp = load_split(cps, po_in, po, 0, places[:1])
    if pieces == 2:
        half = chans // 2
        theirs = pl.ds(pl.multiple_of(places[1] * half, half), half)
        embed = tw.shape[0]
        tw_cp.append(cps.start(small_in[0].at[0:embed], tw.at[:, theirs]))
        for j in range(3):
            rows_of = pl.ds(embed + j * chans, chans)
            pi_cp.append(cps.start(small_in[0].at[rows_of], pi.at[j, :, theirs]))
        for j in range(2):
            rows_of = pl.ds(embed + 3 * chans + j * half, half)
            lanes = pl.ds(j * half, half)
            po_cp.append(cps.start(small_in[0].at[rows_of], po.at[theirs, lanes]))
    g_cp = load_images(cps, g_in, gin, places, count)

    zero_pads(apad, side, points)
    zero_pads(bpad, side, points)
    zero_pads(gpad, side, points)

    wait_all(vec_cp)
    vcols = jnp.transpose(vec[...])

    def col(j):
        return vcols[:, j : j + 1]

    def row(j):
        return vec[j : j + 1, :]

    wait_all(x_cp)
    for b in images:
        hat, _ = norm_first(xin[b], size, width)
        pre = hat * col(FIRST_GAIN) + col(FIRST_SHIFT)
        act = (pre * sigmoid(pre)).astype(bf16)
        a1t[b] = act
        put_moved(apad, b, jnp.transpose(act).astype(f32), side, points)

    wait_all(row_cp)
    wait_all(tw_cp)
    wait_all(w1_cp)
    wait_all(w2_cp)
    wait_all(pi_cp)
    wait_all(po_cp)
    wait_all(g_cp)
    outs = [cps.start(vec, all_vec_out), cps.start(xin, x_out), cps.start(w1, w1_out)]
    outs += [cps.start(a1t, a1t_out), cps.start(w2, w2_out), cps.start(po, po_out)]
    picked = []
    for b in images:
        step = steps_ref[places[0] * count + b]
        r = lax.broadcasted_iota(jnp.int32, (16, rows.shape[2]), 0)
        picked.append(col_sum(jnp.where(r == lax.rem(step, 16), rows[b].astype(f32), 0.0)))
    emb = jnp.concatenate(picked + picked[:1] * (8 - count), axis=0)
    time_add = nn((emb * sigmoid(emb)).astype(bf16), tw[...]) + row(TIME_BIAS) + row(FIRST_BIAS)

    stats2, stats3 = [], []
    act_t = [None] * count

    def conv_one(b):
        lhs = jnp.concatenate(taps(apad, b, 1, side, points), axis=1)
        sum_one[b] = nn(lhs, w1[...].reshape(9 * chans, chans)) + time_add[b : b + 1]

    def norm_two(b):
        mean, rstd = moments(sum_one[b], width, size)
        stats2.append((mean, rstd))
        hat = (sum_one[b] - mean) * rstd
        pre = hat * row(SECOND_GAIN) + row(SECOND_SHIFT)
        act = pre * sigmoid(pre)
        act_t[b] = jnp.transpose(act.astype(bf16))
        put_moved(bpad, b, act, side, points)

    def conv_two(b):
        lhs = jnp.concatenate(taps(bpad, b, 1, side, points), axis=1)
        val = nn(lhs, w2[...].reshape(9 * chans, chans)) + row(SECOND_BIAS)
        resid[b] = val + jnp.transpose(xin[b]).astype(f32)

    normed = []

    def norm_three(b):
        mean, rstd = moments(resid[b], width, size)
        stats3.append((mean, rstd))
        hat = (resid[b] - mean) * rstd
        normed.append((hat * row(THIRD_GAIN) + row(THIRD_SHIFT)).astype(bf16))

    pipelined([conv_one, norm_two, conv_two, norm_three], count)
    outs += [cps.start(sum_one, sum_out), cps.start(resid, resid_out)]
    stat[0:count, :] = jnp.concatenate([m for m, _ in stats2], axis=0)
    stat[count : 2 * count, :] = jnp.concatenate([r for _, r in stats2], axis=0)
    outs.append(cps.start(stat, stat_out))

    pi_row = jnp.concatenate([pi[0], pi[1], pi[2]], axis=1)
    pi_t = jnp.concatenate([jnp.transpose(pi[1]), jnp.transpose(pi[2])], axis=0)
    zero = jnp.zeros((1, chans), f32)
    normed_t = jnp.concatenate([jnp.transpose(v) for v in normed], axis=1)
    normed = jnp.concatenate(normed, axis=0)
    lin = nn(normed, pi_row)
    q = (lin[:, :chans] + row(QUERY_BIAS)).astype(bf16)
    k = lin[:, chans : 2 * chans].astype(bf16)
    v = (lin[:, 2 * chans :] + row(VALUE_BIAS)).astype(bf16)
    lin_t = nn(pi_t, normed_t)
    kt = lin_t[:chans].astype(bf16)
    vt = (lin_t[chans:] + col(VALUE_BIAS)).astype(bf16)
    grad_all = jnp.concatenate([gin[b] for b in images], axis=1)
    grad_mixed = nn(po[...], grad_all).astype(bf16)
    scores = [nt(part(k, b, points), part(q, b, points)) for b in images]
    grad_w = [nn(part(v, b, points), lane_part(grad_mixed, b, points)) for b in images]
    weights, grad_s = [], []
    for b in images:
        top = scores[b] * scale
        expo = jnp.exp(top - jnp.max(top, axis=0, keepdims=True))
        probs = expo * (1.0 / jnp.sum(expo, axis=0, keepdims=True))
        weights.append(probs.astype(bf16))
        inner = probs * grad_w[b]
        grad_s.append((inner - probs * jnp.sum(inner, axis=0, keepdims=True)).astype(bf16))
    mixed = []
    for b in images:
        mixed.append(nn(lane_part(vt, b, points), weights[b]).astype(bf16))
        mix[b] = mixed[b]
    outs.append(cps.start(mix, mix_out))
    grad_qt = [nn(lane_part(kt, b, points), grad_s[b]) * scale for b in images]
    grad_q = [jnp.transpose(t.astype(bf16)) for t in grad_qt]
    grad_k = [(nn(grad_s[b], part(q, b, points)) * scale).astype(bf16) for b in images]
    grad_v = [nt(weights[b], lane_part(grad_mixed, b, points)).astype(bf16) for b in images]
    lin_grad = jnp.concatenate(
        [jnp.concatenate([grad_q[b], grad_k[b], grad_v[b]], axis=1) for b in images], axis=0
    )
    qb_grad = col_sum(sum(t.astype(f32) for t in grad_q))
    vb_grad = col_sum(sum(t.astype(f32) for t in grad_v))
    dpo = nt(jnp.concatenate(mixed, axis=1), grad_all)
    grad_normed = nt(lin_grad, pi_row)

    gain3, shift3, means = [], [], []
    for b in images:
        hat = (resid[b] - stats3[b][0]) * stats3[b][1]
        val = part(grad_normed, b, points)
        gain3.append(col_sum(val * hat))
        shift3.append(col_sum(val))
        both = jnp.concatenate([shift3[b], gain3[b]], axis=0) * row(THIRD_GAIN)
        means.append(lane_groups(both, width) / size)
    sb_grad, ob_grad = zero, zero
    for b in images:
        hat = (resid[b] - stats3[b][0]) * stats3[b][1]
        h = part(grad_normed, b, points) * row(THIRD_GAIN)
        grad_out = jnp.transpose(gin[b]).astype(f32)
        ob_grad = ob_grad + col_sum(grad_out)
        val = grad_out + stats3[b][1] * (h - means[b][0:1] - hat * means[b][1:2])
        gres[b] = val
        sb_grad = sb_grad + col_sum(val)
        put_moved(gpad, b, val, side, points)
        outs.append(cps.start(gres.at[b], gres_out.at[b]))
        outs.append(cps.start(gpad.at[:, b], gpad_out.at[:, b]))
    lane = lax.broadcasted_iota(jnp.int32, (1, chans), 1)
    stamp = jnp.zeros((1, chans), f32)
    for b in images:
        step = jnp.full((1, chans), steps_ref[places[0] * count + b], jnp.int32)
        stamp = jnp.where(lane == b, (step >> 5).astype(f32), stamp)
        stamp = jnp.where(lane == LANES // 2 + b, (step & 31).astype(f32), stamp)
    sums[...] = jnp.concatenate(
        [sb_grad, sum(gain3), sum(shift3), qb_grad, vb_grad, ob_grad, stamp, zero], axis=0
    )
    outs.append(cps.start(sums, sums_out))

    dpi = nn(normed_t, lin_grad)
    at = 0
    if pieces == 2:
        at = pack_store(own, send, at, dpo, 0, places)
        for j in range(3):
            at = pack_store(own, send, at, dpi[:, j * chans : (j + 1) * chans], 1, places)
    else:
        dpo_own[...] = dpo
        for j in range(3):
            dpi_own[j] = dpi[:, j * chans : (j + 1) * chans]

    a_all = jnp.concatenate(act_t, axis=1)
    moved = [taps(gpad, b, -1, side, points) for b in images]
    for tap in range(9):
        val = nn(a_all, jnp.concatenate([moved[b][tap] for b in images], axis=0))
        if pieces == 2:
            at = pack_store(own, send, at, val, 0, places)
        else:
            dw2_own[tap] = val

    wait_all(outs)


def copy_rows(cps, pairs, start, end):
    rows = slice(start, end)
    return [cps.start(src.at[rows], dst.at[rows]) for src, dst in pairs]


def back_kernel(pieces, count, *refs):
    it = iter(refs)

    def take(n):
        return [next(it) for _ in range(n)]

    kept = take(13)
    if pieces == 2:
        own, send_out, block_own_out, block_send_out, image_own_out, image_send_out = take(6)
    else:
        own, block_own_out, image_own_out = take(3)
        block_send_out = image_send_out = None
    small = next(it)
    w1, w2, po, vec, xin, gpad, sum_one, a1t, resid, gres, mix, stat, front_sums = take(13)
    if pieces == 2:
        send, block_own, block_send, image_own, image_send = take(5)
    else:
        block_own, image_own = take(2)
        block_send = image_send = None
    hpad, back, first_hat, first_slope, sems = take(5)
    cps = Copies(sems)
    places = places_of(pieces)
    points, chans = sum_one.shape[1], sum_one.shape[2]
    side = side_of(points)
    width = chans // GROUPS
    size = float(width * points)
    images = range(count)

    w1_in, w2_in, po_in, vec_in, x_in, gpad_in, sum_in, a1t_in, resid_in, gres_in, mix_in = kept[:11]
    early = [(vec_in, vec), (x_in, xin)]
    early = [cps.start(src, dst) for src, dst in early]
    w2_cp = cps.start(w2_in, w2)
    gpad_cp = [cps.start(gpad_in.at[:, b], gpad.at[:, b]) for b in images]
    small_cp = [(kept[11], stat), (kept[12], front_sums)]
    small_cp = [cps.start(src, dst) for src, dst in small_cp]
    sum_cp = cps.start(sum_in, sum_one)
    a1t_cp = cps.start(a1t_in, a1t)
    later = [(w1_in, w1), (po_in, po), (resid_in, resid), (gres_in, gres), (mix_in, mix)]
    later = [cps.start(src, dst) for src, dst in later]

    def row(j):
        return vec[j : j + 1, :]

    zero_pads(hpad, side, points)
    wait_all(early)
    vcols = jnp.transpose(vec[...])

    def col(j):
        return vcols[:, j : j + 1]

    first_rstd = []
    for b in images:
        hat, rstd = norm_first(xin[b], size, width)
        first_rstd.append(jnp.broadcast_to(rstd, (GROUPS, width, 1)).reshape(chans, 1))
        pre = hat * col(FIRST_GAIN) + col(FIRST_SHIFT)
        first_hat[b] = hat
        first_slope[b] = silu_slope(pre, sigmoid(pre))

    w2_cp.wait()
    wait_all(gpad_cp)
    sum_cp.wait()
    wait_all(small_cp)
    w2_cols = jnp.concatenate([w2[k] for k in range(9)], axis=1)
    gain, shift_g, times = [], [], []

    def conv_back(b):
        back[b] = nt(jnp.concatenate(taps(gpad, b, -1, side, points), axis=1), w2_cols)

    def norm_back(b):
        mean, rstd = stat[b : b + 1, :], stat[count + b : count + b + 1, :]
        hat = (sum_one[b] - mean) * rstd
        pre = hat * row(SECOND_GAIN) + row(SECOND_SHIFT)
        val = back[b] * silu_slope(pre, sigmoid(pre))
        gain.append(col_sum(val * hat))
        shift_g.append(col_sum(val))
        both = jnp.concatenate([shift_g[b], gain[b]], axis=0) * row(SECOND_GAIN)
        both = lane_groups(both, width) / size
        val = rstd * (val * row(SECOND_GAIN) - both[0:1] - hat * both[1:2])
        times.append(col_sum(val))
        put_moved(hpad, b, val, side, points)

    pipelined([conv_back, norm_back], count)
    a1t_cp.wait()
    wait_all(later)
    outs = []


    def put_out(own_ref, send_ref, own_dst, send_dst, b, val):
        split_store(own_ref, send_ref, b, val, 0, places)
        outs.append(cps.start(own_ref.at[b], own_dst.at[b]))
        if send_ref is not None:
            outs.append(cps.start(send_ref.at[b], send_dst.at[b]))

    proj = nn(jnp.transpose(po[...]), jnp.concatenate([mix[b] for b in images], axis=1))
    a_all = jnp.concatenate([a1t[b] for b in images], axis=1)
    moved = [taps(hpad, b, -1, side, points) for b in images]
    at = 0
    for tap in range(9):
        val = nn(a_all, jnp.concatenate([moved[b][tap] for b in images], axis=0))
        if pieces == 2:
            at = pack_store(own, send, at, val, 1, places)
        else:
            own[tap] = val
        if tap % 2 == 1 and tap // 2 < count:
            b = tap // 2
            val = jnp.transpose(resid[b]) + lane_part(proj, b, points) + col(OUTPUT_BIAS)
            split_store(block_own, block_send, b, val, 0, places)
    if pieces == 2:
        outs += copy_rows(cps, [(send, send_out)], 0, at)
        outs.append(cps.start(block_send, block_send_out))
    outs.append(cps.start(block_own, block_own_out))

    w1_cols = jnp.concatenate([w1[k] for k in range(9)], axis=1)
    zero = jnp.zeros((chans, 1), f32)
    gain_sum, shift_sum = [zero], [zero]
    first_back = [None] * count

    def groups(v):
        total = jnp.sum(v.reshape(GROUPS, width, 1), axis=1, keepdims=True) / size
        return jnp.broadcast_to(total, (GROUPS, width, 1)).reshape(chans, 1)

    def conv_first(b):
        first_back[b] = nt(w1_cols, jnp.concatenate(taps(hpad, b, -1, side, points), axis=1))

    def norm_first_back(b):
        hat, rstd = first_hat[b], first_rstd[b]
        val = first_back[b] * first_slope[b]
        gain = jnp.sum(val * hat, axis=1, keepdims=True)
        shift = jnp.sum(val, axis=1, keepdims=True)
        gain_sum[0] = gain_sum[0] + gain
        shift_sum[0] = shift_sum[0] + shift
        first_mean = groups(shift * col(FIRST_GAIN))
        second_mean = groups(gain * col(FIRST_GAIN))
        val = rstd * (val * col(FIRST_GAIN) - first_mean - hat * second_mean)
        val = val + jnp.transpose(gres[b])
        put_out(image_own, image_send, image_own_out, image_send_out, b, val)

    pipelined([conv_first, norm_first_back], count)

    lane = lax.broadcasted_iota(jnp.int32, (chans, LANES), 1)
    both = jnp.where(lane == 0, gain_sum[0], 0.0) + jnp.where(lane == 1, shift_sum[0], 0.0)
    both = jnp.transpose(both)
    rows = [front_sums[j : j + 1, :] for j in range(6)]
    rows += [sum(gain), sum(shift_g), sum(times), both[0:1], both[1:2]]
    flat = []
    for r in rows + times:
        flat += [r[:, i * LANES : (i + 1) * LANES] for i in range(chans // LANES)]
    flat.append(front_sums[6:7, :LANES])
    flat += [jnp.zeros((1, LANES), f32)] * (BLOCK - len(flat))
    small[...] = jnp.concatenate(flat, axis=0).astype(bf16)
    wait_all(outs)


def put_quarters(quarters, flat):
    me = lax.axis_index("batch") & 3
    rows = quarters[0].shape[0]
    if len(quarters) == 4:
        parts = [(j, ref, 0) for j, ref in enumerate(quarters)]
    else:
        odd = lax.axis_index("tensor") & 1
        mine, first, both = quarters
        parts = [(0, mine, 0), (1 + odd, first, 0), (2 - odd, both, 0), (3, both, rows)]
    for j, ref, at in parts:
        flat[pl.ds(pl.multiple_of((me ^ j) * rows, 16), rows), :] = ref[at : at + rows, :]


def unpack_first_kernel(*refs):
    quarters = refs[:-4]
    dw1_out, flat, dw1, sems = refs[-4:]
    cps = Copies(sems)
    put_quarters(quarters, flat)
    outs = []
    chans = dw1.shape[1]
    for tap in range(dw1.shape[0]):
        dw1[tap] = flat[tap * chans : (tap + 1) * chans, :].astype(f32)
        if tap % 3 == 2:
            part = slice(tap - 2, tap + 1)
            outs.append(cps.start(dw1.at[part], dw1_out.at[part]))
    wait_all(outs)


def unpack_second_kernel(*refs):
    quarters = refs[:-8]
    dw2_out, dpo_out, dpi_out, flat, dw2, dpo, dpi, sems = refs[-8:]
    cps = Copies(sems)
    put_quarters(quarters, flat)
    outs = []
    chans = dpi.shape[1]
    half = chans // 2
    for i in range(2):
        dpo[:, i * LANES : (i + 1) * LANES] = flat[i * half : (i + 1) * half, :].astype(f32)
    outs.append(cps.start(dpo, dpo_out))
    at = chans
    for j in range(3):
        dpi[j] = flat[at : at + chans, :].astype(f32)
        at += chans
    outs.append(cps.start(dpi, dpi_out))
    for tap in range(dw2.shape[0]):
        for i in range(2):
            dw2[tap, :, i * LANES : (i + 1) * LANES] = flat[at : at + half, :].astype(f32)
            at += half
        if tap % 3 == 2:
            part = slice(tap - 2, tap + 1)
            outs.append(cps.start(dw2.at[part], dw2_out.at[part]))
    wait_all(outs)


def swap(value, axis, size, bit):
    return lax.ppermute(value, axis, [(i, i ^ bit) for i in range(size)])


def near_parts(part):
    me = lax.axis_index("batch") & 3
    return [part(me ^ j).astype(bf16) for j in range(1, 4)]


def together(*groups):
    return [list(g) for g in lax.optimization_barrier(tuple(tuple(g) for g in groups))]


def send_near(sent, batch):
    return [swap(v, "batch", batch, j + 1) for j, v in enumerate(sent)]


def sum_near(got, part):
    total = part(lax.axis_index("batch") & 3).astype(f32)
    for g in got:
        total = total + g.astype(f32)
    return total.astype(bf16)


def far_steps(batch):
    return batch.bit_length() - 3


def send_far(piece, extra, step, batch):
    steps = far_steps(batch)
    mine = piece if extra is None else jnp.concatenate([piece, extra], axis=0)
    tensor = lax.axis_size("tensor")
    pairs = []
    for i in range(batch):
        for core in range(tensor):
            bit = 4 << (step if core % 2 == 0 else steps - 1 - step)
            pairs.append((i * tensor + core, (i ^ bit) * tensor + core))
    return lax.ppermute(mine, ("batch", "tensor"), pairs)


def sum_far(piece, extra, got):
    rows = piece.shape[0]
    piece = (piece.astype(f32) + got[:rows].astype(f32)).astype(bf16)
    if extra is not None:
        extra = jnp.concatenate([extra, got[rows:]], axis=0)
    return piece, extra


def gather_near(piece, batch):
    return [piece] + [swap(piece, "batch", batch, j) for j in range(1, 4)]


def plane_bit(step, core):
    return 1 if step == core % 2 else 2


def cross(value, step, batch):
    tensor = lax.axis_size("tensor")
    pairs = []
    for i in range(batch):
        for core in range(tensor):
            pairs.append((i * tensor + core, (i ^ plane_bit(step, core)) * tensor + core))
    return lax.ppermute(value, ("batch", "tensor"), pairs)


def by_difference(mine, first, both):
    rows = mine.shape[0]
    odd = (lax.axis_index("tensor") & 1) == 1
    near, far = both[:rows], both[rows:]
    return [mine, jnp.where(odd, near, first), jnp.where(odd, first, near), far]


def in_order(pieces):
    me = lax.axis_index("batch")
    parts = jnp.stack(pieces, axis=0)
    parts = parts.reshape((2, 2) + parts.shape[1:])
    parts = jnp.where((me & 1) == 1, jnp.flip(parts, axis=1), parts)
    parts = jnp.where((me & 2) == 2, jnp.flip(parts, axis=0), parts)
    return parts.reshape((-1, LANES))


def unpack(flat, shapes):
    out = []
    at = 0
    for shape in shapes:
        n = math.prod(shape) // 128
        out.append(flat[at : at + n].reshape(shape).astype(f32))
        at += n
    return out


def per_device(
    batch,
    tensor,
    images,
    timesteps,
    embed_table,
    first_gain,
    first_shift,
    first_conv,
    first_bias,
    time_weight,
    time_bias,
    second_gain,
    second_shift,
    second_conv,
    second_bias,
    third_gain,
    third_shift,
    project_in,
    query_bias,
    value_bias,
    project_out,
    output_bias,
    cotangent,
):
    per_batch, local, points = images.shape
    chans = local * tensor
    count = per_batch // tensor
    table_rows, embed = embed_table.shape
    pieces = 2 if tensor == 2 else 1
    me = lax.axis_index("tensor")
    vectors = [
        first_gain,
        first_shift,
        first_bias,
        time_bias,
        second_gain,
        second_shift,
        second_bias,
        third_gain,
        third_shift,
        query_bias,
        value_bias,
        output_bias,
    ]
    def in_hbm(array):
        return pltpu.with_memory_space_constraint(array, pltpu.HBM)

    n_vec = len(vectors)
    if pieces == 2:
        vec, halves, small = pl.pallas_call(
            functools.partial(pack_kernel, n_vec),
            out_shape=[
                jax.ShapeDtypeStruct((16, local), f32),
                jax.ShapeDtypeStruct((2, count, local, points), bf16),
                jax.ShapeDtypeStruct((embed + 4 * chans, local), bf16),
            ],
            in_specs=[ANY] * (n_vec + 5),
            out_specs=[VMEM] * 3,
            scratch_shapes=[pltpu.SemaphoreType.DMA((n_vec + 8,))],
            compiler_params=pltpu.CompilerParams(vmem_limit_bytes=4 * MIB),
            name="pack",
        )(*(in_hbm(v) for v in vectors + [images, cotangent, time_weight, project_in, project_out]))
    else:
        vec = jnp.stack(vectors + [output_bias] * 4, axis=0)

    def whole(array, axis):
        if pieces == 2:
            return [array, swap(array, "tensor", 2, 1)]
        return [lax.all_gather(array, "tensor", axis=axis, tiled=True)]

    if pieces == 2:
        x_in, g_in = [images, swap(halves, "tensor", 2, 1)], [cotangent]
        tw_in, pi_in, po_in = [time_weight], [project_in], [project_out]
        small_in = [swap(small, "tensor", 2, 1)]
    else:
        x_in, g_in = (
            [lax.all_to_all(v, "tensor", 0, 1, tiled=True)] for v in (images, cotangent)
        )
        tw_in, pi_in, po_in = whole(time_weight, 1), whole(project_in, 2), whole(project_out, 0)
        small_in = []
    vec_in = whole(vec, 1)
    w1_in = whole(first_conv, 2)
    w2_in = whole(second_conv, 1)
    my_steps = timesteps if pieces == 2 else lax.dynamic_slice_in_dim(timesteps, me * count, count)

    side = side_of(points)
    image_b = (count, chans, points)
    image_p = (count, points, chans)
    pads = (3, count, points + 2 * side, chans)

    def shape(s, d):
        return jax.ShapeDtypeStruct(s, d)

    def params(mib):
        return pltpu.CompilerParams(vmem_limit_bytes=mib * MIB)

    def cost(units, moved):
        flops = 2 * units * count * points * chans * chans
        return pl.CostEstimate(flops=flops, bytes_accessed=moved, transcendentals=0)

    half_b = 9 * chans * chans // 2 // LANES
    half_a = half_b + 4 * chans * chans // 2 // LANES
    if pieces == 2:
        grads_a = [pltpu.VMEM((half_a, LANES), bf16)] * 2
        grads_b = [pltpu.VMEM((half_b, LANES), bf16), pltpu.HBM((half_b, LANES), bf16)]
    else:
        grads_a = [shape((9, chans, chans), f32), shape((chans, chans), f32)]
        grads_a.append(shape((3, chans, chans), f32))
        grads_b = [shape((9, chans, chans), f32)]
    n_grad = len(grads_a)
    steps_in = in_hbm(my_steps)
    kept = [
        ((9, chans, chans), bf16),
        ((9, chans, chans), bf16),
        ((chans, chans), bf16),
        ((16, chans), f32),
        (image_b, bf16),
        (pads, bf16),
        (image_p, f32),
        (image_b, bf16),
        (image_p, f32),
        (image_p, f32),
        (image_b, bf16),
        ((2 * count, chans), f32),
        ((8, chans), f32),
    ]
    out_a = ANY if pieces == 2 else VMEM
    scratch_a = []

    front = pl.pallas_call(
        functools.partial(front_kernel, pieces, count),
        out_shape=grads_a
        + [pltpu.HBM(*v) for v in kept],
        in_specs=[ANY, VMEM][:pieces] * 4 + [ANY] * 4 + [VMEM] * (pieces - 1) + [ANY] * 2,
        out_specs=[VMEM] * n_grad + [ANY] * len(kept),
        scratch_shapes=scratch_a
        + [pltpu.VMEM(*v) for v in kept]
        + [
            pltpu.VMEM(image_b, bf16),
            pltpu.VMEM((3, chans, chans), bf16),
            pltpu.VMEM((embed, chans), bf16),
            pltpu.VMEM((count, 16, embed), bf16),
            pltpu.VMEM(pads, bf16),
            pltpu.VMEM(pads, bf16),
            pltpu.SMEM(my_steps.shape, jnp.int32),
            pltpu.SemaphoreType.DMA((8 * pieces + 3 * count + 23,)),
        ],
        compiler_params=params(28),
        cost_estimate=cost(54, 12 << 20),
        name="front",
    )(
        *(
            place(v)
            for pair in (x_in, w1_in, w2_in, vec_in)
            for v, place in zip(pair, (in_hbm, lambda v: v))
        ),
        *(in_hbm(v) for v in g_in + pi_in + po_in + tw_in),
        *small_in,
        steps_in,
        in_hbm(embed_table),
    )
    sums_a = front[:n_grad]
    kept_now = list(front[n_grad:])

    def quarters(sums, axes, beside=None):
        if pieces == 2:
            got = swap(sums[1], "tensor", 2, 1)
            if beside is not None:
                (got,), (beside,) = together([got], [beside])
            rows = got.shape[0] // 4
            own4, got4 = (v.reshape(4, rows, LANES) for v in (sums[0], got))

            def part(q):
                pair = [lax.dynamic_index_in_dim(v, q, 0, False).astype(f32) for v in (own4, got4)]
                return pair[0] + pair[1]

            return part, beside
        done = [
            lax.psum_scatter(v, "tensor", scatter_dimension=axis, tiled=True)
            for v, axis in zip(sums, axes, strict=True)
        ]
        flat = jnp.concatenate([v.reshape(-1, LANES) for v in done], axis=0)
        flat = jnp.pad(flat, ((0, -flat.shape[0] % 64), (0, 0)))
        rows = flat.shape[0] // 4
        flat = flat.reshape(4, rows, LANES)
        return (lambda q: lax.dynamic_index_in_dim(flat, q, 0, False)), beside

    part_a, _ = quarters(sums_a, (1, 0, 2))
    sent_a = near_parts(part_a)

    kept_now[-2:], sent_a = together(kept_now[-2:], sent_a)
    got_a = send_near(sent_a, batch)

    half = (count, chans // 2, points)
    if pieces == 2:
        outs_b = grads_b + [pltpu.HBM(half, f32), pltpu.HBM(half, bf16)] * 2
        scratch_b = [pltpu.VMEM(v.shape, v.dtype) for v in outs_b[1:]]
    else:
        outs_b = grads_b + [pltpu.HBM(image_b, f32)] * 2
        scratch_b = [pltpu.VMEM(image_b, f32)] * 2
    *outs_b, block = pl.pallas_call(
        functools.partial(back_kernel, pieces, count),
        out_shape=outs_b + [pltpu.VMEM((BLOCK, LANES), bf16)],
        in_specs=[ANY] * len(kept),
        out_specs=[VMEM, out_a][:pieces] + [ANY] * (2 * pieces) + [VMEM],
        scratch_shapes=[pltpu.VMEM(*v) for v in kept]
        + scratch_b
        + [
            pltpu.VMEM(pads, bf16),
            pltpu.VMEM(image_p, f32),
            pltpu.VMEM(image_b, f32),
            pltpu.VMEM(image_b, f32),
            pltpu.SemaphoreType.DMA((16 + 3 * count,)),
        ],
        compiler_params=params(28),
        cost_estimate=cost(33, 12 << 20),
        name="back",
    )(*(in_hbm(v) for v in kept_now))
    sums_b, block_part, image_grad = outs_b[:pieces], outs_b[pieces : 2 * pieces], outs_b[2 * pieces :]
    got_a, sums_b, (block,) = together(got_a, sums_b, [block])
    piece_a = sum_near(got_a, part_a)
    steps = far_steps(batch)
    far_a = send_far(piece_a, None, 0, batch) if steps > 0 else None
    part_b, piece_a = quarters(sums_b, (2,), piece_a)
    sent_b = near_parts(part_b)
    got_b = send_near([jnp.concatenate([v, block], axis=0) for v in sent_b], batch)
    if steps > 0:
        piece_a, _ = sum_far(piece_a, None, far_a)
    if steps > 1:
        far_a = send_far(piece_a, None, 1, batch)
    got_b, (piece_a,) = together(got_b, [piece_a])
    rows_b = sent_b[0].shape[0]
    blocks = jnp.concatenate([block] + [g[rows_b:] for g in got_b], axis=0)
    piece_b = sum_near([g[:rows_b] for g in got_b], part_b)
    for step in range(1, steps):
        if step > 1:
            far_a = send_far(piece_a, None, step, batch)
        piece_a, _ = sum_far(piece_a, None, far_a)
    if steps > 0:
        far_b = send_far(piece_b, blocks, 0, batch)
    block_part, image_grad, (piece_b,) = together(block_part, image_grad, [piece_b])

    def placed(own, send):
        if pieces == 2:
            got = swap(send, "tensor", 2, 1).astype(f32)
            low = jnp.where(me == 0, own, got)
            high = jnp.where(me == 0, got, own)
            return jnp.concatenate([low, high], axis=0)
        return lax.all_to_all(own, "tensor", 1, 0, tiled=True)

    block_out = placed(block_part[0], block_part[-1])
    images_grad = placed(image_grad[0], image_grad[-1])

    first_a = cross(piece_a, 0, batch)
    both_a = cross(jnp.concatenate([piece_a, first_a], axis=0), 1, batch)
    for step in range(steps):
        if step > 0:
            far_b = send_far(piece_b, blocks, step, batch)
            (far_b,), (first_a,) = together([far_b], [first_a])
        piece_b, blocks = sum_far(piece_b, blocks, far_b)
    got_a = [piece_a, first_a, both_a]
    got_b = gather_near(piece_b, batch)

    if pieces == 2:

        def unpacked(kernel, name, got, rows, shapes):
            outs = [shape(v, f32) for v in shapes]
            return pl.pallas_call(
                kernel,
                out_shape=outs,
                in_specs=[VMEM] * len(got),
                out_specs=[ANY] * len(outs),
                scratch_shapes=[pltpu.VMEM((rows, LANES), bf16)]
                + [pltpu.VMEM(v.shape, v.dtype) for v in outs]
                + [pltpu.SemaphoreType.DMA((len(outs) + 2,))],
                compiler_params=params(12),
                name=name,
            )(*got)

        second_conv_grad, project_out_grad, project_in_grad = unpacked(
            unpack_second_kernel,
            "unpack_second",
            got_a,
            half_a,
            [(9, local, chans), (local, chans), (3, chans, local)],
        )
        got_b, (second_conv_grad,) = together(got_b, [second_conv_grad])
        (first_conv_grad,) = unpacked(
            unpack_first_kernel, "unpack_first", got_b, half_b, [(9, chans, local)]
        )
    else:
        second_conv_grad, project_out_grad, project_in_grad = unpack(
            in_order(by_difference(*got_a)), [(9, local, chans), (local, chans), (3, chans, local)]
        )
        (first_conv_grad,) = unpack(in_order(got_b), [(9, chans, local)])

    if pieces == 2:
        blocks = jnp.concatenate([blocks, swap(blocks, "tensor", 2, 1)], axis=0)
        two = blocks.reshape(2, batch, BLOCK, LANES)
        blocks = jnp.where(me == 0, two, jnp.flip(two, axis=0))
    else:
        blocks = lax.all_gather(blocks, "tensor", axis=0, tiled=True)
    blocks = blocks.reshape(batch * tensor, BLOCK, LANES)
    wide = chans // LANES
    n_sum = 11 * wide
    sums = jnp.sum(blocks[:, :n_sum].astype(f32), axis=0).reshape(11, chans)
    sums = jnp.concatenate([sums, sums[8:9]], axis=0)
    mine = lax.dynamic_slice_in_dim(sums, me * local, local, axis=1)
    all_times = blocks[:, n_sum : n_sum + wide * count].reshape(-1, chans)
    stamps = blocks[:, n_sum + wide * count].astype(jnp.int32)
    all_steps = stamps[:, :count] * 32 + stamps[:, LANES // 2 : LANES // 2 + count]
    all_steps = all_steps.reshape(-1)
    one_hot = (all_steps[:, None] == jnp.arange(table_rows, dtype=jnp.int32)[None, :]).astype(bf16)
    emb = nn(one_hot, embed_table)
    sig = sigmoid(emb)
    act = (emb * sig).astype(bf16)
    my_times = lax.dynamic_slice_in_dim(all_times, me * local, local, axis=1)
    time_weight_grad = lax.dot_general(
        act, my_times, (((0,), (0,)), ((), ())), preferred_element_type=f32
    )
    if pieces == 2:
        theirs = small_in[0][:embed]
        tw = jnp.where(
            me == 0,
            jnp.concatenate([time_weight, theirs], axis=1),
            jnp.concatenate([theirs, time_weight], axis=1),
        )
    else:
        tw = tw_in[0]
    grad_emb = (nt(all_times, tw) * silu_slope(emb, sig)).astype(bf16)
    table_grad = lax.dot_general(
        one_hot, grad_emb, (((0,), (0,)), ((), ())), preferred_element_type=f32
    )
    return (
        block_out,
        images_grad,
        table_grad,
        mine[9],
        mine[10],
        first_conv_grad,
        mine[8],
        time_weight_grad,
        mine[11],
        mine[6],
        mine[7],
        second_conv_grad,
        mine[0],
        mine[1],
        mine[2],
        project_in_grad,
        mine[3],
        mine[4],
        project_out_grad,
        mine[5],
    )


def solution(mesh):
    in_specs = (
        P("batch", "tensor", None),
        P("batch"),
        P(),
        P("tensor"),
        P("tensor"),
        P(None, None, "tensor"),
        P("tensor"),
        P(None, "tensor"),
        P("tensor"),
        P("tensor"),
        P("tensor"),
        P(None, "tensor", None),
        P("tensor"),
        P("tensor"),
        P("tensor"),
        P(None, None, "tensor"),
        P("tensor"),
        P("tensor"),
        P("tensor", None),
        P("tensor"),
        P("batch", "tensor", None),
    )
    out_specs = (
        P("batch", "tensor", None),
        P("batch", "tensor", None),
        P(),
        P("tensor"),
        P("tensor"),
        P(None, None, "tensor"),
        P("tensor"),
        P(None, "tensor"),
        P("tensor"),
        P("tensor"),
        P("tensor"),
        P(None, "tensor", None),
        P("tensor"),
        P("tensor"),
        P("tensor"),
        P(None, None, "tensor"),
        P("tensor"),
        P("tensor"),
        P("tensor", None),
        P("tensor"),
    )
    sizes = dict(mesh.shape)
    return jax.shard_map(
        functools.partial(per_device, sizes["batch"], sizes["tensor"]),
        mesh=mesh,
        in_specs=in_specs,
        out_specs=out_specs,
        check_vma=False,
    )
```

```python
import functools
import math

import jax
import jax.numpy as jnp
from jax import lax
from jax.experimental import pallas as pl
from jax.experimental.pallas import tpu as pltpu
from jax.sharding import PartitionSpec as P

GROUPS = 32
LANES = 128
BLOCK = 32
EPS = 1e-06
MIB = 1024 * 1024
ANY = pl.BlockSpec(memory_space=pl.ANY)
VMEM = pl.BlockSpec(memory_space=pltpu.VMEM)
f32 = jnp.float32
bf16 = jnp.bfloat16

(
    FIRST_GAIN,
    FIRST_SHIFT,
    FIRST_BIAS,
    TIME_BIAS,
    SECOND_GAIN,
    SECOND_SHIFT,
    SECOND_BIAS,
    THIRD_GAIN,
    THIRD_SHIFT,
    QUERY_BIAS,
    VALUE_BIAS,
    OUTPUT_BIAS,
) = range(12)


def nn(a, b):
    return lax.dot_general(a, b, (((1,), (0,)), ((), ())), preferred_element_type=f32)


def nt(a, b):
    return lax.dot_general(a, b, (((1,), (1,)), ((), ())), preferred_element_type=f32)


def sigmoid(v):
    return 0.5 * jnp.tanh(0.5 * v) + 0.5


def silu_slope(v, sig):
    return sig * (1.0 + v * (1.0 - sig))


def col_sum(v):
    return jnp.sum(v, axis=0, keepdims=True)


def lane_groups(v, width):
    lanes = v.shape[1]
    lane = lax.broadcasted_iota(jnp.int32, v.shape, 1)
    step = 1
    while step < width:
        up = pltpu.roll(v, step, 1)
        down = pltpu.roll(v, lanes - step, 1)
        v = v + jnp.where((lane & step) != 0, up, down)
        step *= 2
    return v


def zero_pads(pad_ref, side, points):
    images, chans = pad_ref.shape[1], pad_ref.shape[3]
    for d in range(3):
        for b in range(images):
            pad_ref[d, b, 0:side, :] = jnp.zeros((side, chans), bf16)
            pad_ref[d, b, side + points : 2 * side + points, :] = jnp.zeros((side, chans), bf16)


def put_moved(pad_ref, b, value, side, points):
    chans = value.shape[1]
    column = lax.broadcasted_iota(jnp.int32, (side, chans), 0)
    for d, edge in ((0, 0), (1, None), (2, side - 1)):
        moved = value
        if edge is not None:
            moved = pltpu.roll(value, (1 - d) % points, 0).reshape(side, side, chans)
            moved = jnp.where((column == edge)[None], 0.0, moved).reshape(points, chans)
        pad_ref[d, b, side : side + points, :] = moved.astype(bf16)


def taps(pad_ref, b, sign, side, points):
    out = []
    for dr in (-1, 0, 1):
        for dc in (-1, 0, 1):
            top = side + sign * dr * side
            out.append(pad_ref[1 + sign * dc, b, top : top + points, :])
    return out


class Copies:
    def __init__(self, sems):
        self.sems = sems
        self.used = 0

    def start(self, src, dst):
        copy = pltpu.make_async_copy(src, dst, self.sems.at[self.used])
        self.used += 1
        copy.start()
        return copy


def wait_all(copies):
    for c in copies:
        c.wait()


def side_of(points):
    return math.isqrt(points)


def load_split(cps, refs, dst, axis, places):
    out = []
    for ref, place in zip(refs, places, strict=True):
        size = ref.shape[axis]
        idx = [slice(None)] * len(ref.shape)
        idx[axis] = pl.ds(pl.multiple_of(place * size, size), size)
        out.append(cps.start(ref, dst.at[tuple(idx)]))
    return out


def load_images(cps, refs, dst, places, count):
    out = []
    for j, (ref, place) in enumerate(zip(refs, places, strict=True)):
        size = ref.shape[1]
        first = pl.multiple_of(places[0] * count, count) if j == 0 else 0
        out.append(
            cps.start(
                ref.at[pl.ds(first, count)],
                dst.at[:, pl.ds(pl.multiple_of(place * size, size), size), :],
            )
        )
    return out


def places_of(pieces):
    if pieces == 1:
        return [0]
    me = lax.axis_index("tensor")
    return [me, 1 - me]


def split_store(own_ref, send_ref, at, value, axis, places):
    if send_ref is None:
        own_ref[at] = value.astype(own_ref.dtype)
        return
    half = value.shape[axis] // 2
    low = lax.slice_in_dim(value, 0, half, axis=axis)
    high = lax.slice_in_dim(value, half, 2 * half, axis=axis)
    first = places[0] == 0
    own_ref[at] = jnp.where(first, low, high).astype(own_ref.dtype)
    send_ref[at] = jnp.where(first, high, low).astype(send_ref.dtype)


def pack_store(own_ref, send_ref, at, value, axis, places):
    half = value.shape[axis] // 2
    low = lax.slice_in_dim(value, 0, half, axis=axis)
    high = lax.slice_in_dim(value, half, 2 * half, axis=axis)
    first = places[0] == 0
    own = jnp.where(first, low, high).astype(own_ref.dtype)
    send = jnp.where(first, high, low).astype(send_ref.dtype)
    rows = own.shape[0]
    for i in range(own.shape[1] // LANES):
        lanes = slice(i * LANES, (i + 1) * LANES)
        own_ref[at : at + rows, :] = own[:, lanes]
        send_ref[at : at + rows, :] = send[:, lanes]
        at += rows
    return at


def pack_kernel(n_vec, *refs):
    vectors, arrays = refs[:n_vec], refs[n_vec : n_vec + 2]
    tw, pi, po, vec, halves, small, sems = refs[n_vec + 2 :]
    cps = Copies(sems)
    count = halves.shape[1]
    first = pl.multiple_of((1 - lax.axis_index("tensor")) * count, count)
    copies = [
        cps.start(src.at[pl.ds(first, count)], halves.at[j])
        for j, src in enumerate(arrays)
    ]
    copies += [cps.start(v, vec.at[j]) for j, v in enumerate(vectors)]
    at = tw.shape[0]
    copies.append(cps.start(tw, small.at[0:at]))
    for j in range(3):
        copies.append(cps.start(pi.at[j], small.at[at : at + pi.shape[1]]))
        at += pi.shape[1]
    half = po.shape[0]
    for j in range(2):
        copies.append(cps.start(po.at[:, j * half : (j + 1) * half], small.at[at : at + half]))
        at += half
    vec[n_vec:, :] = jnp.zeros((16 - n_vec, vec.shape[1]), f32)
    wait_all(copies)


def part(value, b, points):
    return value[b * points : (b + 1) * points]


def lane_part(value, b, points):
    return value[:, b * points : (b + 1) * points]


def norm_first(x, size, width):
    x3 = x.astype(f32).reshape(GROUPS, width, x.shape[1])
    mean = jnp.sum(jnp.sum(x3, axis=2, keepdims=True), axis=1, keepdims=True) / size
    off = x3 - mean
    var = jnp.sum(jnp.sum(off * off, axis=2, keepdims=True), axis=1, keepdims=True) / size
    rstd = lax.rsqrt(var + EPS)
    return (off * rstd).reshape(x.shape), rstd


def moments(value, width, size):
    mean = lane_groups(col_sum(value), width) / size
    off = value - mean
    return mean, lax.rsqrt(lane_groups(col_sum(off * off), width) / size + EPS)


def pipelined(stages, count):
    for s in stages:
        for b in range(count):
            s(b)


def front_kernel(pieces, count, *refs):
    it = iter(refs)

    def take(n):
        return [next(it) for _ in range(n)]

    x_in, w1_in, w2_in, vec_in = (take(pieces) for _ in range(4))
    g_in, pi_in, po_in, tw_in = (take(1) for _ in range(4))
    small_in = take(pieces - 1)
    if pieces == 2:
        x_in, g_in = [x_in[0], x_in[1].at[0]], [g_in[0], x_in[1].at[1]]
    steps_in, table_ref = take(2)
    if pieces == 2:
        own, send = take(2)
    else:
        dw2_own, dpo_own, dpi_own = take(3)
    w1_out, w2_out, po_out, all_vec_out, x_out = take(5)
    gpad_out, sum_out, a1t_out, resid_out, gres_out, mix_out = take(6)
    stat_out, sums_out = take(2)
    w1, w2, po, vec, xin = take(5)
    gpad, sum_one, a1t, resid, gres, mix = take(6)
    stat, sums = take(2)
    gin, pi, tw, rows, apad, bpad, steps_ref = take(7)
    sems = next(it)

    cps = Copies(sems)
    places = places_of(pieces)
    chans, points = xin.shape[1], xin.shape[2]
    side = side_of(points)
    width = chans // GROUPS
    size = float(width * points)
    scale = chans ** (-0.5)
    images = range(count)

    steps_cp = cps.start(steps_in, steps_ref)
    vec_cp = load_split(cps, vec_in, vec, 1, places)
    x_cp = load_images(cps, x_in, xin, places, count)
    w1_cp = load_split(cps, w1_in, w1, 2, places)
    w2_cp = load_split(cps, w2_in, w2, 1, places)
    steps_cp.wait()
    row_cp = []
    for b in images:
        step = steps_ref[places[0] * count + b]
        row_cp.append(
            cps.start(table_ref.at[pl.ds(pl.multiple_of(step // 16 * 16, 16), 16), :], rows.at[b])
        )
    tw_cp = load_split(cps, tw_in, tw, 1, places[:1])
    pi_cp = load_split(cps, pi_in, pi, 2, places[:1])
    po_cp = load_split(cps, po_in, po, 0, places[:1])
    if pieces == 2:
        half = chans // 2
        theirs = pl.ds(pl.multiple_of(places[1] * half, half), half)
        embed = tw.shape[0]
        tw_cp.append(cps.start(small_in[0].at[0:embed], tw.at[:, theirs]))
        for j in range(3):
            rows_of = pl.ds(embed + j * chans, chans)
            pi_cp.append(cps.start(small_in[0].at[rows_of], pi.at[j, :, theirs]))
        for j in range(2):
            rows_of = pl.ds(embed + 3 * chans + j * half, half)
            lanes = pl.ds(j * half, half)
            po_cp.append(cps.start(small_in[0].at[rows_of], po.at[theirs, lanes]))
    g_cp = load_images(cps, g_in, gin, places, count)

    zero_pads(apad, side, points)
    zero_pads(bpad, side, points)
    zero_pads(gpad, side, points)

    wait_all(vec_cp)
    vcols = jnp.transpose(vec[...])

    def col(j):
        return vcols[:, j : j + 1]

    def row(j):
        return vec[j : j + 1, :]

    wait_all(x_cp)
    for b in images:
        hat, _ = norm_first(xin[b], size, width)
        pre = hat * col(FIRST_GAIN) + col(FIRST_SHIFT)
        act = (pre * sigmoid(pre)).astype(bf16)
        a1t[b] = act
        put_moved(apad, b, jnp.transpose(act).astype(f32), side, points)

    wait_all(row_cp)
    wait_all(tw_cp)
    wait_all(w1_cp)
    wait_all(w2_cp)
    wait_all(pi_cp)
    wait_all(po_cp)
    wait_all(g_cp)
    outs = [cps.start(vec, all_vec_out), cps.start(xin, x_out), cps.start(w1, w1_out)]
    outs += [cps.start(a1t, a1t_out), cps.start(w2, w2_out), cps.start(po, po_out)]
    picked = []
    for b in images:
        step = steps_ref[places[0] * count + b]
        r = lax.broadcasted_iota(jnp.int32, (16, rows.shape[2]), 0)
        picked.append(col_sum(jnp.where(r == lax.rem(step, 16), rows[b].astype(f32), 0.0)))
    emb = jnp.concatenate(picked + picked[:1] * (8 - count), axis=0)
    time_add = nn((emb * sigmoid(emb)).astype(bf16), tw[...]) + row(TIME_BIAS) + row(FIRST_BIAS)

    stats2, stats3 = [], []
    act_t = [None] * count

    def conv_one(b):
        lhs = jnp.concatenate(taps(apad, b, 1, side, points), axis=1)
        sum_one[b] = nn(lhs, w1[...].reshape(9 * chans, chans)) + time_add[b : b + 1]

    def norm_two(b):
        mean, rstd = moments(sum_one[b], width, size)
        stats2.append((mean, rstd))
        hat = (sum_one[b] - mean) * rstd
        pre = hat * row(SECOND_GAIN) + row(SECOND_SHIFT)
        act = pre * sigmoid(pre)
        act_t[b] = jnp.transpose(act.astype(bf16))
        put_moved(bpad, b, act, side, points)

    def conv_two(b):
        lhs = jnp.concatenate(taps(bpad, b, 1, side, points), axis=1)
        val = nn(lhs, w2[...].reshape(9 * chans, chans)) + row(SECOND_BIAS)
        resid[b] = val + jnp.transpose(xin[b]).astype(f32)

    normed = []

    def norm_three(b):
        mean, rstd = moments(resid[b], width, size)
        stats3.append((mean, rstd))
        hat = (resid[b] - mean) * rstd
        normed.append((hat * row(THIRD_GAIN) + row(THIRD_SHIFT)).astype(bf16))

    pipelined([conv_one, norm_two, conv_two, norm_three], count)
    outs += [cps.start(sum_one, sum_out), cps.start(resid, resid_out)]
    stat[0:count, :] = jnp.concatenate([m for m, _ in stats2], axis=0)
    stat[count : 2 * count, :] = jnp.concatenate([r for _, r in stats2], axis=0)
    outs.append(cps.start(stat, stat_out))

    pi_row = jnp.concatenate([pi[0], pi[1], pi[2]], axis=1)
    pi_t = jnp.concatenate([jnp.transpose(pi[1]), jnp.transpose(pi[2])], axis=0)
    zero = jnp.zeros((1, chans), f32)
    normed_t = jnp.concatenate([jnp.transpose(v) for v in normed], axis=1)
    normed = jnp.concatenate(normed, axis=0)
    lin = nn(normed, pi_row)
    q = (lin[:, :chans] + row(QUERY_BIAS)).astype(bf16)
    k = lin[:, chans : 2 * chans].astype(bf16)
    v = (lin[:, 2 * chans :] + row(VALUE_BIAS)).astype(bf16)
    lin_t = nn(pi_t, normed_t)
    kt = lin_t[:chans].astype(bf16)
    vt = (lin_t[chans:] + col(VALUE_BIAS)).astype(bf16)
    grad_all = jnp.concatenate([gin[b] for b in images], axis=1)
    grad_mixed = nn(po[...], grad_all).astype(bf16)
    scores = [nt(part(k, b, points), part(q, b, points)) for b in images]
    grad_w = [nn(part(v, b, points), lane_part(grad_mixed, b, points)) for b in images]
    weights, grad_s = [], []
    for b in images:
        top = scores[b] * scale
        expo = jnp.exp(top - jnp.max(top, axis=0, keepdims=True))
        probs = expo * (1.0 / jnp.sum(expo, axis=0, keepdims=True))
        weights.append(probs.astype(bf16))
        inner = probs * grad_w[b]
        grad_s.append((inner - probs * jnp.sum(inner, axis=0, keepdims=True)).astype(bf16))
    mixed = []
    for b in images:
        mixed.append(nn(lane_part(vt, b, points), weights[b]).astype(bf16))
        mix[b] = mixed[b]
    outs.append(cps.start(mix, mix_out))
    grad_qt = [nn(lane_part(kt, b, points), grad_s[b]) * scale for b in images]
    grad_q = [jnp.transpose(t.astype(bf16)) for t in grad_qt]
    grad_k = [(nn(grad_s[b], part(q, b, points)) * scale).astype(bf16) for b in images]
    grad_v = [nt(weights[b], lane_part(grad_mixed, b, points)).astype(bf16) for b in images]
    lin_grad = jnp.concatenate(
        [jnp.concatenate([grad_q[b], grad_k[b], grad_v[b]], axis=1) for b in images], axis=0
    )
    qb_grad = col_sum(sum(t.astype(f32) for t in grad_q))
    vb_grad = col_sum(sum(t.astype(f32) for t in grad_v))
    dpo = nt(jnp.concatenate(mixed, axis=1), grad_all)
    grad_normed = nt(lin_grad, pi_row)

    gain3, shift3, means = [], [], []
    for b in images:
        hat = (resid[b] - stats3[b][0]) * stats3[b][1]
        val = part(grad_normed, b, points)
        gain3.append(col_sum(val * hat))
        shift3.append(col_sum(val))
        both = jnp.concatenate([shift3[b], gain3[b]], axis=0) * row(THIRD_GAIN)
        means.append(lane_groups(both, width) / size)
    sb_grad, ob_grad = zero, zero
    for b in images:
        hat = (resid[b] - stats3[b][0]) * stats3[b][1]
        h = part(grad_normed, b, points) * row(THIRD_GAIN)
        grad_out = jnp.transpose(gin[b]).astype(f32)
        ob_grad = ob_grad + col_sum(grad_out)
        val = grad_out + stats3[b][1] * (h - means[b][0:1] - hat * means[b][1:2])
        gres[b] = val
        sb_grad = sb_grad + col_sum(val)
        put_moved(gpad, b, val, side, points)
        outs.append(cps.start(gres.at[b], gres_out.at[b]))
        outs.append(cps.start(gpad.at[:, b], gpad_out.at[:, b]))
    lane = lax.broadcasted_iota(jnp.int32, (1, chans), 1)
    stamp = jnp.zeros((1, chans), f32)
    for b in images:
        step = jnp.full((1, chans), steps_ref[places[0] * count + b], jnp.int32)
        stamp = jnp.where(lane == b, (step >> 5).astype(f32), stamp)
        stamp = jnp.where(lane == LANES // 2 + b, (step & 31).astype(f32), stamp)
    sums[...] = jnp.concatenate(
        [sb_grad, sum(gain3), sum(shift3), qb_grad, vb_grad, ob_grad, stamp, zero], axis=0
    )
    outs.append(cps.start(sums, sums_out))

    dpi = nn(normed_t, lin_grad)
    at = 0
    if pieces == 2:
        at = pack_store(own, send, at, dpo, 0, places)
        for j in range(3):
            at = pack_store(own, send, at, dpi[:, j * chans : (j + 1) * chans], 1, places)
    else:
        dpo_own[...] = dpo
        for j in range(3):
            dpi_own[j] = dpi[:, j * chans : (j + 1) * chans]

    a_all = jnp.concatenate(act_t, axis=1)
    moved = [taps(gpad, b, -1, side, points) for b in images]
    for tap in range(9):
        val = nn(a_all, jnp.concatenate([moved[b][tap] for b in images], axis=0))
        if pieces == 2:
            at = pack_store(own, send, at, val, 0, places)
        else:
            dw2_own[tap] = val

    wait_all(outs)


def copy_rows(cps, pairs, start, end):
    rows = slice(start, end)
    return [cps.start(src.at[rows], dst.at[rows]) for src, dst in pairs]


def back_kernel(pieces, count, *refs):
    it = iter(refs)

    def take(n):
        return [next(it) for _ in range(n)]

    kept = take(13)
    if pieces == 2:
        own, send_out, block_own_out, block_send_out, image_own_out, image_send_out = take(6)
    else:
        own, block_own_out, image_own_out = take(3)
        block_send_out = image_send_out = None
    small = next(it)
    w1, w2, po, vec, xin, gpad, sum_one, a1t, resid, gres, mix, stat, front_sums = take(13)
    if pieces == 2:
        send, block_own, block_send, image_own, image_send = take(5)
    else:
        block_own, image_own = take(2)
        block_send = image_send = None
    hpad, back, first_hat, first_slope, sems = take(5)
    cps = Copies(sems)
    places = places_of(pieces)
    points, chans = sum_one.shape[1], sum_one.shape[2]
    side = side_of(points)
    width = chans // GROUPS
    size = float(width * points)
    images = range(count)

    w1_in, w2_in, po_in, vec_in, x_in, gpad_in, sum_in, a1t_in, resid_in, gres_in, mix_in = kept[:11]
    early = [(vec_in, vec), (x_in, xin)]
    early = [cps.start(src, dst) for src, dst in early]
    w2_cp = cps.start(w2_in, w2)
    gpad_cp = [cps.start(gpad_in.at[:, b], gpad.at[:, b]) for b in images]
    small_cp = [(kept[11], stat), (kept[12], front_sums)]
    small_cp = [cps.start(src, dst) for src, dst in small_cp]
    sum_cp = cps.start(sum_in, sum_one)
    a1t_cp = cps.start(a1t_in, a1t)
    later = [(w1_in, w1), (po_in, po), (resid_in, resid), (gres_in, gres), (mix_in, mix)]
    later = [cps.start(src, dst) for src, dst in later]

    def row(j):
        return vec[j : j + 1, :]

    zero_pads(hpad, side, points)
    wait_all(early)
    vcols = jnp.transpose(vec[...])

    def col(j):
        return vcols[:, j : j + 1]

    first_rstd = []
    for b in images:
        hat, rstd = norm_first(xin[b], size, width)
        first_rstd.append(jnp.broadcast_to(rstd, (GROUPS, width, 1)).reshape(chans, 1))
        pre = hat * col(FIRST_GAIN) + col(FIRST_SHIFT)
        first_hat[b] = hat
        first_slope[b] = silu_slope(pre, sigmoid(pre))

    w2_cp.wait()
    wait_all(gpad_cp)
    sum_cp.wait()
    wait_all(small_cp)
    w2_cols = jnp.concatenate([w2[k] for k in range(9)], axis=1)
    gain, shift_g, times = [], [], []

    def conv_back(b):
        back[b] = nt(jnp.concatenate(taps(gpad, b, -1, side, points), axis=1), w2_cols)

    def norm_back(b):
        mean, rstd = stat[b : b + 1, :], stat[count + b : count + b + 1, :]
        hat = (sum_one[b] - mean) * rstd
        pre = hat * row(SECOND_GAIN) + row(SECOND_SHIFT)
        val = back[b] * silu_slope(pre, sigmoid(pre))
        gain.append(col_sum(val * hat))
        shift_g.append(col_sum(val))
        both = jnp.concatenate([shift_g[b], gain[b]], axis=0) * row(SECOND_GAIN)
        both = lane_groups(both, width) / size
        val = rstd * (val * row(SECOND_GAIN) - both[0:1] - hat * both[1:2])
        times.append(col_sum(val))
        put_moved(hpad, b, val, side, points)

    pipelined([conv_back, norm_back], count)
    a1t_cp.wait()
    wait_all(later)
    outs = []


    def put_out(own_ref, send_ref, own_dst, send_dst, b, val):
        split_store(own_ref, send_ref, b, val, 0, places)
        outs.append(cps.start(own_ref.at[b], own_dst.at[b]))
        if send_ref is not None:
            outs.append(cps.start(send_ref.at[b], send_dst.at[b]))

    proj = nn(jnp.transpose(po[...]), jnp.concatenate([mix[b] for b in images], axis=1))
    a_all = jnp.concatenate([a1t[b] for b in images], axis=1)
    moved = [taps(hpad, b, -1, side, points) for b in images]
    at = 0
    for tap in range(9):
        val = nn(a_all, jnp.concatenate([moved[b][tap] for b in images], axis=0))
        if pieces == 2:
            at = pack_store(own, send, at, val, 1, places)
        else:
            own[tap] = val
        if tap % 2 == 1 and tap // 2 < count:
            b = tap // 2
            val = jnp.transpose(resid[b]) + lane_part(proj, b, points) + col(OUTPUT_BIAS)
            split_store(block_own, block_send, b, val, 0, places)
    if pieces == 2:
        outs += copy_rows(cps, [(send, send_out)], 0, at)
        outs.append(cps.start(block_send, block_send_out))
    outs.append(cps.start(block_own, block_own_out))

    w1_cols = jnp.concatenate([w1[k] for k in range(9)], axis=1)
    zero = jnp.zeros((chans, 1), f32)
    gain_sum, shift_sum = [zero], [zero]
    first_back = [None] * count

    def groups(v):
        total = jnp.sum(v.reshape(GROUPS, width, 1), axis=1, keepdims=True) / size
        return jnp.broadcast_to(total, (GROUPS, width, 1)).reshape(chans, 1)

    def conv_first(b):
        first_back[b] = nt(w1_cols, jnp.concatenate(taps(hpad, b, -1, side, points), axis=1))

    def norm_first_back(b):
        hat, rstd = first_hat[b], first_rstd[b]
        val = first_back[b] * first_slope[b]
        gain = jnp.sum(val * hat, axis=1, keepdims=True)
        shift = jnp.sum(val, axis=1, keepdims=True)
        gain_sum[0] = gain_sum[0] + gain
        shift_sum[0] = shift_sum[0] + shift
        first_mean = groups(shift * col(FIRST_GAIN))
        second_mean = groups(gain * col(FIRST_GAIN))
        val = rstd * (val * col(FIRST_GAIN) - first_mean - hat * second_mean)
        val = val + jnp.transpose(gres[b])
        put_out(image_own, image_send, image_own_out, image_send_out, b, val)

    pipelined([conv_first, norm_first_back], count)

    lane = lax.broadcasted_iota(jnp.int32, (chans, LANES), 1)
    both = jnp.where(lane == 0, gain_sum[0], 0.0) + jnp.where(lane == 1, shift_sum[0], 0.0)
    both = jnp.transpose(both)
    rows = [front_sums[j : j + 1, :] for j in range(6)]
    rows += [sum(gain), sum(shift_g), sum(times), both[0:1], both[1:2]]
    flat = []
    for r in rows + times:
        flat += [r[:, i * LANES : (i + 1) * LANES] for i in range(chans // LANES)]
    flat.append(front_sums[6:7, :LANES])
    flat += [jnp.zeros((1, LANES), f32)] * (BLOCK - len(flat))
    small[...] = jnp.concatenate(flat, axis=0).astype(bf16)
    wait_all(outs)


def put_quarters(quarters, flat):
    me = lax.axis_index("batch") & 3
    rows = quarters[0].shape[0]
    if len(quarters) == 4:
        parts = [(j, ref, 0) for j, ref in enumerate(quarters)]
    else:
        odd = lax.axis_index("tensor") & 1
        mine, first, both = quarters
        parts = [(0, mine, 0), (1 + odd, first, 0), (2 - odd, both, 0), (3, both, rows)]
    for j, ref, at in parts:
        flat[pl.ds(pl.multiple_of((me ^ j) * rows, 16), rows), :] = ref[at : at + rows, :]


def unpack_first_kernel(*refs):
    quarters = refs[:-4]
    dw1_out, flat, dw1, sems = refs[-4:]
    cps = Copies(sems)
    put_quarters(quarters, flat)
    outs = []
    chans = dw1.shape[1]
    for tap in range(dw1.shape[0]):
        dw1[tap] = flat[tap * chans : (tap + 1) * chans, :].astype(f32)
        if tap in (3, 8):
            part = slice(0, 4) if tap == 3 else slice(4, 9)
            outs.append(cps.start(dw1.at[part], dw1_out.at[part]))
    wait_all(outs)


def unpack_second_kernel(*refs):
    quarters = refs[:-8]
    dw2_out, dpo_out, dpi_out, flat, dw2, dpo, dpi, sems = refs[-8:]
    cps = Copies(sems)
    put_quarters(quarters, flat)
    outs = []
    chans = dpi.shape[1]
    half = chans // 2
    for i in range(2):
        dpo[:, i * LANES : (i + 1) * LANES] = flat[i * half : (i + 1) * half, :].astype(f32)
    outs.append(cps.start(dpo, dpo_out))
    at = chans
    for j in range(3):
        dpi[j] = flat[at : at + chans, :].astype(f32)
        at += chans
    outs.append(cps.start(dpi, dpi_out))
    for tap in range(dw2.shape[0]):
        for i in range(2):
            dw2[tap, :, i * LANES : (i + 1) * LANES] = flat[at : at + half, :].astype(f32)
            at += half
        if tap % 3 == 2:
            part = slice(tap - 2, tap + 1)
            outs.append(cps.start(dw2.at[part], dw2_out.at[part]))
    wait_all(outs)


def swap(value, axis, size, bit):
    return lax.ppermute(value, axis, [(i, i ^ bit) for i in range(size)])


def near_parts(part):
    me = lax.axis_index("batch") & 3
    return [part(me ^ j).astype(bf16) for j in range(1, 4)]


def together(*groups):
    return [list(g) for g in lax.optimization_barrier(tuple(tuple(g) for g in groups))]


def send_near(sent, batch):
    return [swap(v, "batch", batch, j + 1) for j, v in enumerate(sent)]


def sum_near(got, part):
    total = part(lax.axis_index("batch") & 3).astype(f32)
    for g in got:
        total = total + g.astype(f32)
    return total.astype(bf16)


def far_steps(batch):
    return batch.bit_length() - 3


def send_far(piece, extra, step, batch):
    steps = far_steps(batch)
    mine = piece if extra is None else jnp.concatenate([piece, extra], axis=0)
    tensor = lax.axis_size("tensor")
    pairs = []
    for i in range(batch):
        for core in range(tensor):
            bit = 4 << (step if core % 2 == 0 else steps - 1 - step)
            pairs.append((i * tensor + core, (i ^ bit) * tensor + core))
    return lax.ppermute(mine, ("batch", "tensor"), pairs)


def sum_far(piece, extra, got):
    rows = piece.shape[0]
    piece = (piece.astype(f32) + got[:rows].astype(f32)).astype(bf16)
    if extra is not None:
        extra = jnp.concatenate([extra, got[rows:]], axis=0)
    return piece, extra


def gather_near(piece, batch):
    return [piece] + [swap(piece, "batch", batch, j) for j in range(1, 4)]


def plane_bit(step, core):
    return 1 if step == core % 2 else 2


def cross(value, step, batch):
    tensor = lax.axis_size("tensor")
    pairs = []
    for i in range(batch):
        for core in range(tensor):
            pairs.append((i * tensor + core, (i ^ plane_bit(step, core)) * tensor + core))
    return lax.ppermute(value, ("batch", "tensor"), pairs)


def by_difference(mine, first, both):
    rows = mine.shape[0]
    odd = (lax.axis_index("tensor") & 1) == 1
    near, far = both[:rows], both[rows:]
    return [mine, jnp.where(odd, near, first), jnp.where(odd, first, near), far]


def in_order(pieces):
    me = lax.axis_index("batch")
    parts = jnp.stack(pieces, axis=0)
    parts = parts.reshape((2, 2) + parts.shape[1:])
    parts = jnp.where((me & 1) == 1, jnp.flip(parts, axis=1), parts)
    parts = jnp.where((me & 2) == 2, jnp.flip(parts, axis=0), parts)
    return parts.reshape((-1, LANES))


def unpack(flat, shapes):
    out = []
    at = 0
    for shape in shapes:
        n = math.prod(shape) // 128
        out.append(flat[at : at + n].reshape(shape).astype(f32))
        at += n
    return out


def per_device(
    batch,
    tensor,
    images,
    timesteps,
    embed_table,
    first_gain,
    first_shift,
    first_conv,
    first_bias,
    time_weight,
    time_bias,
    second_gain,
    second_shift,
    second_conv,
    second_bias,
    third_gain,
    third_shift,
    project_in,
    query_bias,
    value_bias,
    project_out,
    output_bias,
    cotangent,
):
    per_batch, local, points = images.shape
    chans = local * tensor
    count = per_batch // tensor
    table_rows, embed = embed_table.shape
    pieces = 2 if tensor == 2 else 1
    me = lax.axis_index("tensor")
    vectors = [
        first_gain,
        first_shift,
        first_bias,
        time_bias,
        second_gain,
        second_shift,
        second_bias,
        third_gain,
        third_shift,
        query_bias,
        value_bias,
        output_bias,
    ]
    def in_hbm(array):
        return pltpu.with_memory_space_constraint(array, pltpu.HBM)

    n_vec = len(vectors)
    if pieces == 2:
        vec, halves, small = pl.pallas_call(
            functools.partial(pack_kernel, n_vec),
            out_shape=[
                jax.ShapeDtypeStruct((16, local), f32),
                jax.ShapeDtypeStruct((2, count, local, points), bf16),
                jax.ShapeDtypeStruct((embed + 4 * chans, local), bf16),
            ],
            in_specs=[ANY] * (n_vec + 5),
            out_specs=[VMEM] * 3,
            scratch_shapes=[pltpu.SemaphoreType.DMA((n_vec + 8,))],
            compiler_params=pltpu.CompilerParams(vmem_limit_bytes=4 * MIB),
            name="pack",
        )(*(in_hbm(v) for v in vectors + [images, cotangent, time_weight, project_in, project_out]))
    else:
        vec = jnp.stack(vectors + [output_bias] * 4, axis=0)

    def whole(array, axis):
        if pieces == 2:
            return [array, swap(array, "tensor", 2, 1)]
        return [lax.all_gather(array, "tensor", axis=axis, tiled=True)]

    if pieces == 2:
        x_in, g_in = [images, swap(halves, "tensor", 2, 1)], [cotangent]
        tw_in, pi_in, po_in = [time_weight], [project_in], [project_out]
        small_in = [swap(small, "tensor", 2, 1)]
    else:
        x_in, g_in = (
            [lax.all_to_all(v, "tensor", 0, 1, tiled=True)] for v in (images, cotangent)
        )
        tw_in, pi_in, po_in = whole(time_weight, 1), whole(project_in, 2), whole(project_out, 0)
        small_in = []
    vec_in = whole(vec, 1)
    w1_in = whole(first_conv, 2)
    w2_in = whole(second_conv, 1)
    my_steps = timesteps if pieces == 2 else lax.dynamic_slice_in_dim(timesteps, me * count, count)

    side = side_of(points)
    image_b = (count, chans, points)
    image_p = (count, points, chans)
    pads = (3, count, points + 2 * side, chans)

    def shape(s, d):
        return jax.ShapeDtypeStruct(s, d)

    def params(mib):
        return pltpu.CompilerParams(vmem_limit_bytes=mib * MIB)

    def cost(units, moved):
        flops = 2 * units * count * points * chans * chans
        return pl.CostEstimate(flops=flops, bytes_accessed=moved, transcendentals=0)

    half_b = 9 * chans * chans // 2 // LANES
    half_a = half_b + 4 * chans * chans // 2 // LANES
    if pieces == 2:
        grads_a = [pltpu.VMEM((half_a, LANES), bf16)] * 2
        grads_b = [pltpu.VMEM((half_b, LANES), bf16), pltpu.HBM((half_b, LANES), bf16)]
    else:
        grads_a = [shape((9, chans, chans), f32), shape((chans, chans), f32)]
        grads_a.append(shape((3, chans, chans), f32))
        grads_b = [shape((9, chans, chans), f32)]
    n_grad = len(grads_a)
    steps_in = in_hbm(my_steps)
    kept = [
        ((9, chans, chans), bf16),
        ((9, chans, chans), bf16),
        ((chans, chans), bf16),
        ((16, chans), f32),
        (image_b, bf16),
        (pads, bf16),
        (image_p, f32),
        (image_b, bf16),
        (image_p, f32),
        (image_p, f32),
        (image_b, bf16),
        ((2 * count, chans), f32),
        ((8, chans), f32),
    ]
    out_a = ANY if pieces == 2 else VMEM
    scratch_a = []

    front = pl.pallas_call(
        functools.partial(front_kernel, pieces, count),
        out_shape=grads_a
        + [pltpu.HBM(*v) for v in kept],
        in_specs=[ANY, VMEM][:pieces] * 4 + [ANY] * 4 + [VMEM] * (pieces - 1) + [ANY] * 2,
        out_specs=[VMEM] * n_grad + [ANY] * len(kept),
        scratch_shapes=scratch_a
        + [pltpu.VMEM(*v) for v in kept]
        + [
            pltpu.VMEM(image_b, bf16),
            pltpu.VMEM((3, chans, chans), bf16),
            pltpu.VMEM((embed, chans), bf16),
            pltpu.VMEM((count, 16, embed), bf16),
            pltpu.VMEM(pads, bf16),
            pltpu.VMEM(pads, bf16),
            pltpu.SMEM(my_steps.shape, jnp.int32),
            pltpu.SemaphoreType.DMA((8 * pieces + 3 * count + 23,)),
        ],
        compiler_params=params(28),
        cost_estimate=cost(54, 12 << 20),
        name="front",
    )(
        *(
            place(v)
            for pair in (x_in, w1_in, w2_in, vec_in)
            for v, place in zip(pair, (in_hbm, lambda v: v))
        ),
        *(in_hbm(v) for v in g_in + pi_in + po_in + tw_in),
        *small_in,
        steps_in,
        in_hbm(embed_table),
    )
    sums_a = front[:n_grad]
    kept_now = list(front[n_grad:])

    def quarters(sums, axes, beside=None):
        if pieces == 2:
            got = swap(sums[1], "tensor", 2, 1)
            if beside is not None:
                (got,), (beside,) = together([got], [beside])
            rows = got.shape[0] // 4
            own4, got4 = (v.reshape(4, rows, LANES) for v in (sums[0], got))

            def part(q):
                pair = [lax.dynamic_index_in_dim(v, q, 0, False).astype(f32) for v in (own4, got4)]
                return pair[0] + pair[1]

            return part, beside
        done = [
            lax.psum_scatter(v, "tensor", scatter_dimension=axis, tiled=True)
            for v, axis in zip(sums, axes, strict=True)
        ]
        flat = jnp.concatenate([v.reshape(-1, LANES) for v in done], axis=0)
        flat = jnp.pad(flat, ((0, -flat.shape[0] % 64), (0, 0)))
        rows = flat.shape[0] // 4
        flat = flat.reshape(4, rows, LANES)
        return (lambda q: lax.dynamic_index_in_dim(flat, q, 0, False)), beside

    part_a, _ = quarters(sums_a, (1, 0, 2))
    sent_a = near_parts(part_a)

    kept_now[-2:], sent_a = together(kept_now[-2:], sent_a)
    got_a = send_near(sent_a, batch)

    half = (count, chans // 2, points)
    if pieces == 2:
        outs_b = grads_b + [pltpu.HBM(half, f32), pltpu.HBM(half, bf16)] * 2
        scratch_b = [pltpu.VMEM(v.shape, v.dtype) for v in outs_b[1:]]
    else:
        outs_b = grads_b + [pltpu.HBM(image_b, f32)] * 2
        scratch_b = [pltpu.VMEM(image_b, f32)] * 2
    *outs_b, block = pl.pallas_call(
        functools.partial(back_kernel, pieces, count),
        out_shape=outs_b + [pltpu.VMEM((BLOCK, LANES), bf16)],
        in_specs=[ANY] * len(kept),
        out_specs=[VMEM, out_a][:pieces] + [ANY] * (2 * pieces) + [VMEM],
        scratch_shapes=[pltpu.VMEM(*v) for v in kept]
        + scratch_b
        + [
            pltpu.VMEM(pads, bf16),
            pltpu.VMEM(image_p, f32),
            pltpu.VMEM(image_b, f32),
            pltpu.VMEM(image_b, f32),
            pltpu.SemaphoreType.DMA((16 + 3 * count,)),
        ],
        compiler_params=params(28),
        cost_estimate=cost(33, 12 << 20),
        name="back",
    )(*(in_hbm(v) for v in kept_now))
    sums_b, block_part, image_grad = outs_b[:pieces], outs_b[pieces : 2 * pieces], outs_b[2 * pieces :]
    got_a, sums_b, (block,) = together(got_a, sums_b, [block])
    piece_a = sum_near(got_a, part_a)
    steps = far_steps(batch)
    far_a = send_far(piece_a, None, 0, batch) if steps > 0 else None
    part_b, piece_a = quarters(sums_b, (2,), piece_a)
    sent_b = near_parts(part_b)
    got_b = send_near([jnp.concatenate([v, block], axis=0) for v in sent_b], batch)
    if steps > 0:
        piece_a, _ = sum_far(piece_a, None, far_a)
    if steps > 1:
        far_a = send_far(piece_a, None, 1, batch)
    got_b, (piece_a,) = together(got_b, [piece_a])
    rows_b = sent_b[0].shape[0]
    blocks = jnp.concatenate([block] + [g[rows_b:] for g in got_b], axis=0)
    piece_b = sum_near([g[:rows_b] for g in got_b], part_b)
    for step in range(1, steps):
        if step > 1:
            far_a = send_far(piece_a, None, step, batch)
        piece_a, _ = sum_far(piece_a, None, far_a)
    if steps > 0:
        far_b = send_far(piece_b, blocks, 0, batch)
    block_part, image_grad, (piece_b,) = together(block_part, image_grad, [piece_b])

    def placed(own, send):
        if pieces == 2:
            got = swap(send, "tensor", 2, 1).astype(f32)
            low = jnp.where(me == 0, own, got)
            high = jnp.where(me == 0, got, own)
            return jnp.concatenate([low, high], axis=0)
        return lax.all_to_all(own, "tensor", 1, 0, tiled=True)

    block_out = placed(block_part[0], block_part[-1])
    images_grad = placed(image_grad[0], image_grad[-1])

    first_a = cross(piece_a, 0, batch)
    both_a = cross(jnp.concatenate([piece_a, first_a], axis=0), 1, batch)
    for step in range(steps):
        if step > 0:
            far_b = send_far(piece_b, blocks, step, batch)
            (far_b,), (first_a,) = together([far_b], [first_a])
        piece_b, blocks = sum_far(piece_b, blocks, far_b)
    got_a = [piece_a, first_a, both_a]
    got_b = gather_near(piece_b, batch)

    if pieces == 2:

        def unpacked(kernel, name, got, rows, shapes):
            outs = [shape(v, f32) for v in shapes]
            return pl.pallas_call(
                kernel,
                out_shape=outs,
                in_specs=[VMEM] * len(got),
                out_specs=[ANY] * len(outs),
                scratch_shapes=[pltpu.VMEM((rows, LANES), bf16)]
                + [pltpu.VMEM(v.shape, v.dtype) for v in outs]
                + [pltpu.SemaphoreType.DMA((len(outs) + 2,))],
                compiler_params=params(12),
                name=name,
            )(*got)

        second_conv_grad, project_out_grad, project_in_grad = unpacked(
            unpack_second_kernel,
            "unpack_second",
            got_a,
            half_a,
            [(9, local, chans), (local, chans), (3, chans, local)],
        )
        got_b, (second_conv_grad,) = together(got_b, [second_conv_grad])
        (first_conv_grad,) = unpacked(
            unpack_first_kernel, "unpack_first", got_b, half_b, [(9, chans, local)]
        )
    else:
        second_conv_grad, project_out_grad, project_in_grad = unpack(
            in_order(by_difference(*got_a)), [(9, local, chans), (local, chans), (3, chans, local)]
        )
        (first_conv_grad,) = unpack(in_order(got_b), [(9, chans, local)])

    if pieces == 2:
        blocks = jnp.concatenate([blocks, swap(blocks, "tensor", 2, 1)], axis=0)
        two = blocks.reshape(2, batch, BLOCK, LANES)
        blocks = jnp.where(me == 0, two, jnp.flip(two, axis=0))
    else:
        blocks = lax.all_gather(blocks, "tensor", axis=0, tiled=True)
    blocks = blocks.reshape(batch * tensor, BLOCK, LANES)
    wide = chans // LANES
    n_sum = 11 * wide
    sums = jnp.sum(blocks[:, :n_sum].astype(f32), axis=0).reshape(11, chans)
    sums = jnp.concatenate([sums, sums[8:9]], axis=0)
    mine = lax.dynamic_slice_in_dim(sums, me * local, local, axis=1)
    all_times = blocks[:, n_sum : n_sum + wide * count].reshape(-1, chans)
    stamps = blocks[:, n_sum + wide * count].astype(jnp.int32)
    all_steps = stamps[:, :count] * 32 + stamps[:, LANES // 2 : LANES // 2 + count]
    all_steps = all_steps.reshape(-1)
    one_hot = (all_steps[:, None] == jnp.arange(table_rows, dtype=jnp.int32)[None, :]).astype(bf16)
    emb = nn(one_hot, embed_table)
    sig = sigmoid(emb)
    act = (emb * sig).astype(bf16)
    my_times = lax.dynamic_slice_in_dim(all_times, me * local, local, axis=1)
    time_weight_grad = lax.dot_general(
        act, my_times, (((0,), (0,)), ((), ())), preferred_element_type=f32
    )
    if pieces == 2:
        theirs = small_in[0][:embed]
        tw = jnp.where(
            me == 0,
            jnp.concatenate([time_weight, theirs], axis=1),
            jnp.concatenate([theirs, time_weight], axis=1),
        )
    else:
        tw = tw_in[0]
    grad_emb = (nt(all_times, tw) * silu_slope(emb, sig)).astype(bf16)
    table_grad = lax.dot_general(
        one_hot, grad_emb, (((0,), (0,)), ((), ())), preferred_element_type=f32
    )
    return (
        block_out,
        images_grad,
        table_grad,
        mine[9],
        mine[10],
        first_conv_grad,
        mine[8],
        time_weight_grad,
        mine[11],
        mine[6],
        mine[7],
        second_conv_grad,
        mine[0],
        mine[1],
        mine[2],
        project_in_grad,
        mine[3],
        mine[4],
        project_out_grad,
        mine[5],
    )


def solution(mesh):
    in_specs = (
        P("batch", "tensor", None),
        P("batch"),
        P(),
        P("tensor"),
        P("tensor"),
        P(None, None, "tensor"),
        P("tensor"),
        P(None, "tensor"),
        P("tensor"),
        P("tensor"),
        P("tensor"),
        P(None, "tensor", None),
        P("tensor"),
        P("tensor"),
        P("tensor"),
        P(None, None, "tensor"),
        P("tensor"),
        P("tensor"),
        P("tensor", None),
        P("tensor"),
        P("batch", "tensor", None),
    )
    out_specs = (
        P("batch", "tensor", None),
        P("batch", "tensor", None),
        P(),
        P("tensor"),
        P("tensor"),
        P(None, None, "tensor"),
        P("tensor"),
        P(None, "tensor"),
        P("tensor"),
        P("tensor"),
        P("tensor"),
        P(None, "tensor", None),
        P("tensor"),
        P("tensor"),
        P("tensor"),
        P(None, None, "tensor"),
        P("tensor"),
        P("tensor"),
        P("tensor", None),
        P("tensor"),
    )
    sizes = dict(mesh.shape)
    return jax.shard_map(
        functools.partial(per_device, sizes["batch"], sizes["tensor"]),
        mesh=mesh,
        in_specs=in_specs,
        out_specs=out_specs,
        check_vma=False,
    )
```
